256 devices in a mesh: member: 8 (over x, core), space: 32 (over z, y).
Axes of the slice: x: 4, y: 4, z: 8, core: 2. Of those that a mesh axis runs over, the one named last changes fastest.
Arguments:
- noisy: float32 [8, 192, 32, 128], P('member', 'space'), may hold values from -12 to 12
- mean_field: float32 [192, 32, 128], P('space'), may hold values from -6 to 6
- coarse: float32 [256, 192], P('space', 'member'), may hold values from -6 to 6
- counts: int32 [32], P('space'), may hold values from 2 to 6, as said below
- src: int32 [192, 4], P('space'), may hold values from 0 to 7
- widx: int32 [192, 4], P('space'), may hold values from 0 to 15
- table: float32 [16], replicated, may hold values from 0.2 to 1
- sigma: float32 [8], P('member'), may hold values from 0.5 to 4
- sigma_next: float32 [8], P('member'), may hold values from 0.1 to 0.4
- w_stem: bfloat16 [180, 128], replicated, may hold values from -0.4375 to 0.4375
- noise_embed: float32 [128], replicated, may hold values from -9 to 9
- w_down: bfloat16 [128, 256], replicated, may hold values from -0.5 to 0.5
- w_query: bfloat16 [256, 256], replicated, may hold values from -0.25 to 0.25
- w_key: bfloat16 [256, 256], replicated, may hold values from -8.125 to 8.125
- w_value: bfloat16 [256, 256], replicated, may hold values from -0.375 to 0.375
- w_attn_out: bfloat16 [256, 256], replicated, may hold values from -0.375 to 0.375
- w_up: bfloat16 [256, 128], replicated, may hold values from -0.375 to 0.375
- w_out: bfloat16 [128, 36], replicated, may hold values from -0.1875 to 0.1875
Outputs:
- denoised: float32 [8, 192, 32, 128], P('member', 'space')
- next_state: float32 [8, 192, 32, 128], P('member', 'space')
The draws below stay inside these ranges and needn't reach their ends.
Inputs may be any that keep to these rules, and one draw needn't show every extreme that they name: `counts`: live patches of each space device; some device holds 6 and some holds 2. `src`: a patch's coarse blocks are held by the space device that holds the patch; slots that are not live have entries too.
All inputs are finite; a program needn't handle non-finite values.
Results may differ from the reference program's by a relative error of at most 0.006.
Values may be sent and summed in bfloat16 or wider, within the bound.
No kernel may reach another device: no remote copies, remote signals or barrier semaphores. Data moves between devices by JAX's collectives and lax.ppermute only.
A program may use at most 64 MiB of HBM per device.

```python
import math
import jax
import jax.numpy as jnp
from jax import lax

VARS = 4
CCH = 12
CIN = 20
CH = 128
CH2 = 256
HEAD_DIM = 64
P_SIZE = 32
M = 16
W = 32
SLOTS = 6
FACTOR = 8
POOL = 8
BLK_DEV = 8
K = 4
NW = 16
DOM = 64
TOKENS = 32
BR = 4
BW = 4
MEMBERS = 8
PATCHES = 192
BLOCKS = 256
N_SPACE = 32


def shared_pattern(key):
    return jax.random.truncated_normal(key, -4.0, 4.0, (CH2, CH2), jnp.float32) / math.sqrt(CH2)


def draw_counts(key, part):
    key = jax.random.fold_in(key, 11)
    first, second, third = jax.random.split(key, 3)
    light = jax.random.randint(first, (N_SPACE,), 2, 4)
    heavy = jax.random.randint(second, (N_SPACE,), 0, 5) == 0
    counts = jnp.where(heavy, SLOTS, light)
    order = jax.random.permutation(third, N_SPACE)
    counts = counts.at[order[0]].set(SLOTS)
    counts = counts.at[order[1]].set(2)
    return counts.astype(jnp.int32)


def draw_w_query(key, part):
    base = shared_pattern(key)
    return base.astype(jnp.bfloat16)


def draw_w_key(key, part):
    key = jax.random.fold_in(key, 4)
    first = jax.random.fold_in(key, 0)
    fresh = jax.random.truncated_normal(first, -4.0, 4.0, (CH2, CH2), jnp.float32) / math.sqrt(CH2)
    return fresh.astype(jnp.bfloat16)


def plant(result, rng, low, top_value):
    longest = result.shape.index(max(result.shape))
    spots = []
    for shift in (0, 1):
        where = [jax.random.randint(jax.random.fold_in(rng, axis), (), 0, length) for axis, length in enumerate(result.shape)]
        where[longest] = (where[longest] + shift) % result.shape[longest]
        spots.append(tuple(where))
    return result.at[spots[0]].set(low).at[spots[1]].set(top_value)


def block_levels(key, dims, shards, low, largest):
    level = 1.0
    for dim, parts in shards:
        heights = jax.random.uniform(jax.random.fold_in(jax.random.fold_in(key, 6), dim), (parts,), jnp.float32, low / len(shards), largest / len(shards))
        level = level * jnp.repeat(jnp.exp(heights), dims[dim] // parts).reshape((-1,) + (1,) * (len(dims) - 1 - dim))
    return level


def normal_values(rng, extent, scale, reach, cuts=(), kind=jnp.bfloat16):
    loudness = block_levels(rng, extent, cuts, -0.22, 0.18) if cuts else 1.0
    array = jax.random.normal(rng, extent, jnp.float32) * scale * loudness
    return jnp.minimum(jnp.maximum(array, -reach), reach).astype(kind)


def setup_inputs(seed: int = 0) -> dict:
    splits = jax.random.split(jax.random.key(seed), 19)
    noisy = normal_values(splits[0], (MEMBERS, PATCHES, P_SIZE, W * VARS), 2.0, 12.0, ((0, 8), (1, 32)), jnp.float32)
    mean_field = normal_values(splits[1], (PATCHES, P_SIZE, W * VARS), 1.0, 6.0, ((0, 32),), jnp.float32)
    coarse = normal_values(splits[2], (BLOCKS, BR * BW * CCH), 1.0, 6.0, ((0, 32), (1, 8)), jnp.float32)
    counts = draw_counts(jax.random.fold_in(splits[18], 71), 0)
    src = plant(jax.random.randint(splits[4], (PATCHES, K), 0, BLK_DEV), jax.random.fold_in(splits[4], 1), 0, BLK_DEV - 1).astype(jnp.int32)
    widx = plant(jax.random.randint(splits[5], (PATCHES, K), 0, NW), jax.random.fold_in(splits[5], 1), 0, NW - 1).astype(jnp.int32)
    table = jnp.clip(jax.random.uniform(splits[6], (NW,), jnp.float32, 0.2, 1.0), 0.2, 1.0)
    sigma = jnp.clip(jnp.exp(math.log(4.0) - 2.0794415 * jax.random.uniform(splits[7], (MEMBERS,), jnp.float32) ** block_levels(splits[7], (MEMBERS,), ((0, 8),), -0.2, 0.2)), 0.5, 4.0)
    sigma_next = jnp.clip(jnp.exp(math.log(0.4) - 1.3862944 * jax.random.uniform(splits[8], (MEMBERS,), jnp.float32) ** block_levels(splits[8], (MEMBERS,), ((0, 8),), -0.2, 0.2)), 0.1, 0.4)
    w_stem = normal_values(splits[9], (9 * CIN, CH), (9 * CIN) ** -0.5, 0.4375)
    noise_embed = normal_values(splits[10], (CH,), 3.0, 9.0, (), jnp.float32)
    w_down = normal_values(splits[11], (CH, CH2), CH ** -0.5, 0.5)
    w_query = draw_w_query(jax.random.fold_in(splits[18], 71), 0)
    w_key = draw_w_key(jax.random.fold_in(splits[18], 71), 0)
    w_value = normal_values(splits[14], (CH2, CH2), CH2 ** -0.5, 0.375)
    w_attn_out = normal_values(splits[15], (CH2, CH2), CH2 ** -0.5, 0.375)
    w_up = normal_values(splits[16], (CH2, CH), CH2 ** -0.5, 0.375)
    w_out = normal_values(splits[17], (CH, 9 * VARS), (9 * CH) ** -0.5, 0.1875)
    return dict(noisy=noisy, mean_field=mean_field, coarse=coarse, counts=counts, src=src, widx=widx, table=table, sigma=sigma, sigma_next=sigma_next, w_stem=w_stem, noise_embed=noise_embed, w_down=w_down, w_query=w_query, w_key=w_key, w_value=w_value, w_attn_out=w_attn_out, w_up=w_up, w_out=w_out)


SIGMA_DATA = 0.5
NORM_EPS = 1e-06

def interp_matrix(fine_count, coarse_count):
    position = (jnp.arange(fine_count, dtype=jnp.float32) + 0.5) / FACTOR - 0.5
    position = jnp.clip(position, 0.0, coarse_count - 1.0)
    centers = jnp.arange(coarse_count, dtype=jnp.float32)
    return jnp.maximum(0.0, 1.0 - jnp.abs(position[:, None] - centers[None, :]))

def upsample_blocks(mixed_blocks):
    batch_count = mixed_blocks.shape[0]
    cell_grid = mixed_blocks.reshape(batch_count, BR, BW, CCH)
    row_map = interp_matrix(P_SIZE, BR)
    col_map = interp_matrix(W, BW)
    tall_rows = jnp.einsum('pa,sabk->spbk', row_map, cell_grid, precision=lax.Precision.HIGHEST)
    return jnp.einsum('cb,spbk->spck', col_map, tall_rows, precision=lax.Precision.HIGHEST)

def stem_conv(extended, noise_shift, w_stem):
    row_count = extended.shape[0] - 2
    cell_grid = extended.reshape(row_count + 2, W, CIN)
    padded = jnp.pad(cell_grid, ((0, 0), (1, 1), (0, 0)))
    tap_list = [padded[row_tap:row_tap + row_count, col_tap:col_tap + W] for row_tap in range(3) for col_tap in range(3)]
    columns = jnp.concatenate(tap_list, axis=-1).reshape(row_count * W, 9 * CIN)
    summed = jnp.dot(columns, w_stem, preferred_element_type=jnp.float32)
    return jax.nn.silu(summed + noise_shift[None, :]).astype(jnp.bfloat16).reshape(row_count, W * CH)

def pool_domain(domain):
    cell_grid = domain.astype(jnp.float32).reshape(DOM // POOL, POOL, W // POOL, POOL, CH)
    return lax.optimization_barrier(jnp.mean(cell_grid, axis=(1, 3))).reshape(TOKENS, CH).astype(jnp.bfloat16)

def bottleneck(pooled, w_down, w_query, w_key, w_value, w_attn_out, w_up):
    batch_count = pooled.shape[0]
    heads_count = CH2 // HEAD_DIM
    flat_rows = pooled.reshape(batch_count * TOKENS, CH)
    zeta = jax.nn.silu(jnp.dot(flat_rows, w_down, preferred_element_type=jnp.float32))
    inv_scale = lax.rsqrt(lax.optimization_barrier(jnp.mean(zeta * zeta, axis=-1, keepdims=True)) + NORM_EPS)
    normed = (zeta * inv_scale).astype(jnp.bfloat16)
    query_rows = jnp.dot(normed, w_query, preferred_element_type=jnp.float32).astype(jnp.bfloat16)
    key_rows = jnp.dot(normed, w_key, preferred_element_type=jnp.float32).astype(jnp.bfloat16)
    value_rows = jnp.dot(normed, w_value, preferred_element_type=jnp.float32).astype(jnp.bfloat16)
    query_rows = query_rows.reshape(batch_count, TOKENS, heads_count, HEAD_DIM).astype(jnp.float32)
    key_rows = key_rows.reshape(batch_count, TOKENS, heads_count, HEAD_DIM).astype(jnp.float32)
    value_rows = value_rows.reshape(batch_count, TOKENS, heads_count, HEAD_DIM).astype(jnp.float32)
    scores = jnp.einsum('sthd,suhd->shtu', query_rows, key_rows) / math.sqrt(HEAD_DIM)
    scores = scores - lax.optimization_barrier(jnp.max(scores, axis=-1, keepdims=True))
    expsum = jnp.exp(scores)
    weights_att = (expsum / lax.optimization_barrier(jnp.sum(expsum, axis=-1, keepdims=True))).astype(jnp.bfloat16)
    attended = jnp.einsum('shtu,suhd->sthd', weights_att.astype(jnp.float32), value_rows)
    attended = attended.astype(jnp.bfloat16).reshape(batch_count * TOKENS, CH2)
    resid = (zeta + jnp.dot(attended, w_attn_out, preferred_element_type=jnp.float32)).astype(jnp.bfloat16)
    lifted = jnp.dot(resid, w_up, preferred_element_type=jnp.float32)
    return lifted.reshape(batch_count, TOKENS, CH)

def output_conv(domain, lifted, w_out):
    cell_grid = domain.reshape(DOM, W, CH).astype(jnp.float32)
    token_grid = lifted.reshape(DOM // POOL, 1, W // POOL, 1, CH)
    raised = jnp.broadcast_to(token_grid, (DOM // POOL, POOL, W // POOL, POOL, CH)).reshape(DOM, W, CH)
    active = jax.nn.silu(cell_grid + raised).astype(jnp.bfloat16)
    tap_terms = jnp.dot(active.reshape(DOM * W, CH), w_out, preferred_element_type=jnp.float32)
    padded = jnp.pad(tap_terms.reshape(DOM, W, 9, VARS), ((1, 1), (1, 1), (0, 0), (0, 0)))
    summed = jnp.zeros((DOM, W, VARS), jnp.float32)
    for row_tap in range(3):
        for col_tap in range(3):
            summed = summed + padded[row_tap:row_tap + DOM, col_tap:col_tap + W, 3 * row_tap + col_tap]
    return summed.reshape(DOM, W * VARS)

def ramp_weight(position):
    return jnp.minimum(position + 1, DOM - position).astype(jnp.float32)

def reference(noisy, mean_field, coarse, counts, src, widx, table, sigma, sigma_next, w_stem, noise_embed, w_down, w_query, w_key, w_value, w_attn_out, w_up, w_out):
    owners = counts.shape[0]
    patch_ids = jnp.arange(PATCHES, dtype=jnp.int32)
    owner_dev = patch_ids // SLOTS
    slot_of = patch_ids % SLOTS
    held_count = counts[owner_dev]
    left_count = counts[jnp.maximum(owner_dev - 1, 0)]
    is_live = slot_of < held_count
    has_prev = (slot_of > 0) | (owner_dev > 0)
    has_next = (slot_of + 1 < held_count) | (owner_dev < owners - 1)
    prev_index = jnp.clip(jnp.where(slot_of > 0, patch_ids - 1, (owner_dev - 1) * SLOTS + left_count - 1), 0, PATCHES - 1).astype(jnp.int32)
    next_index = jnp.clip(jnp.where(slot_of + 1 < held_count, patch_ids + 1, (owner_dev + 1) * SLOTS), 0, PATCHES - 1).astype(jnp.int32)
    block_ids = (owner_dev[:, None] * BLK_DEV + src).astype(jnp.int32)
    mix_weights = table[widx]
    mixed_blocks = lax.optimization_barrier(jnp.sum(mix_weights[:, :, None] * coarse[block_ids], axis=1))
    condition = upsample_blocks(mixed_blocks)
    shared = jnp.concatenate([mean_field.reshape(PATCHES, P_SIZE, W, VARS), condition], axis=-1)
    row_ids = jnp.arange(P_SIZE, dtype=jnp.int32)
    margin_ids = jnp.arange(M, dtype=jnp.int32)
    own_weight = ramp_weight(M + row_ids)
    prev_weight = jnp.where(has_prev[:, None], ramp_weight(P_SIZE + M + margin_ids)[None, :], 0.0)
    next_weight = jnp.where(has_next[:, None], ramp_weight(margin_ids)[None, :], 0.0)
    denominator = jnp.broadcast_to(own_weight[None, :], (PATCHES, P_SIZE))
    denominator = denominator.at[:, :M].add(prev_weight)
    denominator = denominator.at[:, P_SIZE - M:].add(next_weight)
    zero_rows = jnp.zeros((M, W * CH), jnp.bfloat16)

    def one_member(member):
        state_now, noise_level, level_next = member
        spread = noise_level * noise_level + SIGMA_DATA * SIGMA_DATA
        c_in = lax.rsqrt(spread)
        c_skip = SIGMA_DATA * SIGMA_DATA / spread
        c_out = noise_level * SIGMA_DATA * lax.rsqrt(spread)
        noise_shift = jnp.log(noise_level) / 4.0 * noise_embed
        inputs_bf = jnp.concatenate([(c_in * state_now).reshape(PATCHES, P_SIZE, W, VARS), shared], axis=-1)
        inputs_bf = inputs_bf.astype(jnp.bfloat16).reshape(PATCHES, P_SIZE, W * CIN)
        row_above = jnp.where(has_prev[:, None], inputs_bf[prev_index, P_SIZE - 1], jnp.zeros((), jnp.bfloat16))
        row_below = jnp.where(has_next[:, None], inputs_bf[next_index, 0], jnp.zeros((), jnp.bfloat16))
        extended = jnp.concatenate([row_above[:, None], inputs_bf, row_below[:, None]], axis=1)
        features = lax.map(lambda piece_rows: stem_conv(piece_rows, noise_shift, w_stem), extended)

        def domain_of(patch):
            before = jnp.where(has_prev[patch], features[prev_index[patch], P_SIZE - M:], zero_rows)
            after_rows = jnp.where(has_next[patch], features[next_index[patch], :M], zero_rows)
            return jnp.concatenate([before, features[patch], after_rows], axis=0)
        pooled = lax.map(lambda patch: pool_domain(domain_of(patch)), patch_ids)
        lifted = bottleneck(pooled, w_down, w_query, w_key, w_value, w_attn_out, w_up)
        field_out = lax.map(lambda item_pair: output_conv(domain_of(item_pair[0]), item_pair[1], w_out), (patch_ids, lifted))
        numerator = own_weight[None, :, None] * field_out[:, M:M + P_SIZE]
        numerator = numerator.at[:, :M].add(prev_weight[:, :, None] * field_out[prev_index, P_SIZE + M:])
        numerator = numerator.at[:, P_SIZE - M:].add(next_weight[:, :, None] * field_out[next_index, :M])
        blended = numerator / denominator[:, :, None]
        denoised = c_skip * state_now + c_out * blended
        stepped = state_now + (level_next / noise_level - 1.0) * (state_now - denoised)
        live_mask = is_live[:, None, None]
        return (jnp.where(live_mask, denoised, 0.0), jnp.where(live_mask, stepped, 0.0))
    denoised, next_state = lax.map(one_member, (noisy, sigma, sigma_next))
    return (denoised, next_state)
```

```python
import functools

import jax
import jax.numpy as jnp
import numpy as np
from jax import lax
from jax.experimental import pallas as pl
from jax.experimental.pallas import tpu as pltpu
from jax.sharding import PartitionSpec as P

VARS = 4
CCH = 12
CIN = 20
CH = 128
CH2 = 256
HEADS = 4
HEAD_DIM = 64
P_SIZE = 32
M = 16
W = 32
SLOTS = 6
FACTOR = 8
BLK_DEV = 8
MIX = 4
DOM = 64
TOKENS = 32
BR = 4
BW = 4
MEMBERS = 8

SIGMA_DATA = 0.5
NORM_EPS = 1e-06

F32 = jnp.float32
BF16 = jnp.bfloat16

IN_LANES = 2 * W * VARS
CELL = 64
STEM_LANES = (W + 2) * CELL
OWN_ROWS = SLOTS * P_SIZE
SIDE_ROWS = 64
OWN_TOKENS = OWN_ROWS // 8 * 4
SIDE_PATCHES = 4
PIECE = 160
CHUNKS = 9
HALF = W // 2
HALF_LANES = HALF * CH
TAP_LANES = (HALF + 2) * VARS
VMEM_LIMIT = 60 * 1024 * 1024


def interp_matrix(fine_count, coarse_count):
    position = (np.arange(fine_count) + 0.5) / FACTOR - 0.5
    position = np.clip(position, 0.0, coarse_count - 1.0)
    return np.maximum(0.0, 1.0 - np.abs(position[:, None] - np.arange(coarse_count)[None, :]))


def along_rows(rows, first, patches):
    row_map = interp_matrix(P_SIZE, BR)
    along = np.zeros((rows, 3, 2, patches, BR), np.float32)
    for row in range(rows):
        for tap in range(3):
            source = row + first + tap - 1
            if 0 <= source < patches * P_SIZE:
                along[row, tap, :, source // P_SIZE] = row_map[source % P_SIZE][None]
    return along.reshape(rows, 6 * patches * BR).astype(jnp.bfloat16)


@functools.cache
def tables():
    spread = np.zeros((3, 2, W, VARS, W + 2, CELL), np.float32)
    for tap in range(3):
        for array in range(2):
            for col in range(W):
                for var in range(VARS):
                    spread[tap, array, col, var, col + 1, tap * CIN + array * VARS + var] = 1.0
    spread = spread.reshape(3 * IN_LANES, STEM_LANES)
    spread = np.pad(spread, ((0, 0), (0, CHUNKS * 256 - STEM_LANES)))
    spread = spread.reshape(3 * IN_LANES, CHUNKS, 256).transpose(1, 0, 2)
    col_map = interp_matrix(W, BW)
    across = np.zeros((2, BW, CCH, W + 2, CELL), np.float32)
    taps = np.zeros((8, W + 2, CELL), np.float32)
    for tap in range(3):
        taps[tap, :, tap * CIN : (tap + 1) * CIN] = 1.0
        for channel in range(CCH):
            across[:, :, channel, 1 : W + 1, tap * CIN + 2 * VARS + channel] = col_map.T[None]
    across = np.concatenate([across.reshape(2 * BW * CCH, STEM_LANES), np.zeros((32, STEM_LANES))])
    place = np.zeros((3, 3, VARS, HALF, 256), np.float32)
    for cell in range(HALF):
        for row_tap in range(3):
            for col_tap in range(3):
                for var in range(VARS):
                    lane = row_tap * TAP_LANES + (cell + 2 - col_tap) * VARS + var
                    place[row_tap, col_tap, var, cell, lane] = 1.0
    place = place.reshape(36, HALF * 256)
    return (
        spread.astype(jnp.bfloat16),
        across.astype(jnp.bfloat16),
        taps.reshape(8, STEM_LANES).astype(np.float32),
        along_rows(OWN_ROWS, 0, SLOTS),
        along_rows(SIDE_ROWS, M, SIDE_PATCHES),
        place.astype(jnp.bfloat16),
    )


def silu(value):
    half = 0.5 * value
    return half + half * jnp.tanh(half)


def dot(left, right):
    return jnp.dot(left, right, preferred_element_type=F32)


def fetch(sems, pairs):
    copies = [pltpu.make_async_copy(a, b, sems.at[i]) for i, (a, b) in enumerate(pairs)]
    for copy in copies:
        copy.start()
    return copies


def mix_kernel(src, widx, table, coarse, copies_out, src_s, widx_s, table_s, blocks, sems):
    for copy in fetch(sems, [(src, src_s), (widx, widx_s), (table, table_s), (coarse, blocks)]):
        copy.wait()
    copies_out[...] = jnp.zeros_like(copies_out)
    for slot in range(SLOTS):
        total = jnp.zeros((1, 24), F32)
        for k in range(MIX):
            total = total + table_s[widx_s[k, slot]] * blocks[pl.ds(src_s[k, slot], 1)]
        for member in range(MEMBERS):
            copies_out[member, slot : slot + 1, 0:24] = total


def prepare_kernel(
    scalars, noisy, mean_field, w_stem, noise_embed, w_out, spread, place,
    held_out, first_out, second_out, own_out, levels_out, stem_out, right_out,
    scalars_s, noisy_v, mean_v, w_stem_v, embed_v, w_out_v, spread_v, place_v,
    state_rows, mean_rows, stem_left, stem_f32, sems,
):
    copies = fetch(
        sems,
        [
            (scalars, scalars_s),
            (noise_embed, embed_v),
            (noisy, noisy_v),
            (mean_field, mean_v),
            (w_stem, w_stem_v),
            (w_out, w_out_v),
            (place, place_v),
        ]
        + [(spread.at[chunk], spread_v.at[chunk]) for chunk in range(CHUNKS)],
    )
    for copy in copies[0:4]:
        copy.wait()
    held = scalars_s[2].astype(jnp.int32)
    held_out[0] = held
    level = jnp.full((1, 128), scalars_s[0], F32)
    variance = level * level + SIGMA_DATA * SIGMA_DATA
    c_in = lax.rsqrt(variance)
    levels_out[0:1] = jnp.log(level) * 0.25 * embed_v[...]
    levels_out[1:2] = SIGMA_DATA * SIGMA_DATA / variance
    levels_out[2:3] = level * SIGMA_DATA * lax.rsqrt(variance)
    levels_out[3:4] = jnp.full((1, 128), scalars_s[1], F32) / level - 1.0
    levels_out[4:5] = c_in
    even = lax.rem(lax.axis_index("space"), 2) == 0
    c_in = c_in.reshape(1, 1, 128)
    for out, to_right in ((first_out, even), (second_out, jnp.logical_not(even))):
        start = jnp.where(to_right, held - 2, 0)
        out[0:64] = (c_in * noisy_v[pl.ds(start, 2)]).astype(BF16).reshape(64, 128)
        out[64:128] = mean_v[pl.ds(start, 2)].astype(BF16).reshape(64, 128)
    for rows, value in (
        (state_rows, (c_in * noisy_v[...]).reshape(OWN_ROWS, 128)),
        (mean_rows, mean_v[...].reshape(OWN_ROWS, 128)),
    ):
        rows[0:8] = jnp.zeros((8, 128), F32)
        rows[8 : 8 + OWN_ROWS] = value
        rows[8 + OWN_ROWS :] = jnp.zeros((8, 128), F32)
    for tap in range(3):
        for array, rows in enumerate((state_rows, mean_rows)):
            lane = tap * IN_LANES + array * 128
            stem_left[:, lane : lane + 128] = rows[7 + tap : 7 + tap + OWN_ROWS].astype(BF16)

    for copy in copies[4:7]:
        copy.wait()
    stem_f32[...] = jnp.zeros_like(stem_f32)
    stem_taps = w_stem_v[...].astype(F32)
    for cell in range(4):
        for target in range(2):
            col_tap = cell - target
            if 0 <= col_tap < 3:
                for row_tap in range(3):
                    at = (3 * row_tap + col_tap) * CIN
                    to = cell * CELL + row_tap * CIN
                    stem_f32[to : to + CIN, target * CH : (target + 1) * CH] = stem_taps[at : at + CIN]
    stem_out[...] = stem_f32[...].astype(BF16)
    for cell in range(HALF):
        right_out[cell * CH : (cell + 1) * CH] = dot(
            w_out_v[...], place_v[:, cell * 256 : (cell + 1) * 256]
        ).astype(BF16)
    for chunk in range(CHUNKS):
        copies[7 + chunk].wait()
        lanes = min(256, STEM_LANES - chunk * 256)
        own_out[:, chunk * 256 : chunk * 256 + lanes] = dot(
            stem_left[...], spread_v[chunk, :, 0:lanes]
        ).astype(BF16)


def pack_kernel(held_in, cells, first_in, second_in, first_out, second_out, mix_out):
    held = held_in[0]
    for member in range(MEMBERS):
        mix_out[pl.ds(member, SLOTS, stride=MEMBERS)] = cells[member, 0:SLOTS]
    even = lax.rem(lax.axis_index("space"), 2) == 0
    for out, given, to_right in (
        (first_out, first_in, even),
        (second_out, second_in, jnp.logical_not(even)),
    ):
        start = pl.multiple_of(jnp.where(to_right, held - 2, 0) * MEMBERS, MEMBERS)
        out[0:128] = given[0:128]
        mixed = mix_out[pl.ds(start, 16)]
        high = mixed.astype(BF16)
        out[128:144] = high
        out[144:160] = (mixed - high.astype(F32)).astype(BF16)


def conditioning(mixes, count, across, taps):
    pair = mixes[pl.ds(0, count, stride=2)] + pltpu.roll(mixes[pl.ds(1, count, stride=2)], 24, 1)
    pair_high = pair.astype(BF16).astype(F32)
    both = pair_high + pltpu.roll(pair - pair_high, 48, 1)
    wide = dot(both.astype(BF16), across[...])
    wide_high = wide.astype(BF16).astype(F32)
    return wide_high, wide - wide_high


def by_tap(wide_high, wide_low, taps):
    parts = []
    for tap in range(3):
        parts += [wide_high * taps[tap : tap + 1], wide_low * taps[tap : tap + 1]]
    return jnp.concatenate(parts, axis=0).astype(BF16)


def stem(stem_in, stem_right, shift, features, store_pooled):
    rows = features.shape[0]
    for block_col in range(4):
        summed = jnp.zeros((rows, CH), F32)
        for cell_pair in range(4):
            number = block_col * 4 + cell_pair
            raw = dot(stem_in[:, number * 128 : number * 128 + 256], stem_right[...])
            for half in range(2):
                feature = silu(raw[:, half * CH : (half + 1) * CH] + shift).astype(BF16)
                lane = number * 256 + half * CH
                features[:, lane : lane + CH] = feature
                summed = summed + feature.astype(F32)
        store_pooled(block_col, jnp.sum(summed.reshape(rows // 8, 8, CH), axis=1) * (1.0 / 64.0))


def bottleneck(pooled, starts, weights, copies):
    w_down, w_query, w_key, w_value, w_attn_out, w_up = weights
    for copy in copies:
        copy.wait()
    zeta = silu(dot(pooled.astype(BF16), w_down[...]))
    scale = lax.rsqrt(jnp.mean(zeta * zeta, axis=-1, keepdims=True) + NORM_EPS)
    normed = (zeta * scale).astype(BF16)
    query = dot(normed, w_query[...]).astype(BF16)
    keyed = dot(normed, w_key[...]).astype(BF16)
    valued = dot(normed, w_value[...]).astype(BF16)
    head_of_row = lax.broadcasted_iota(jnp.int32, (HEADS * TOKENS, CH2), 0) // TOKENS
    head_of_channel = lax.broadcasted_iota(jnp.int32, (HEADS * TOKENS, CH2), 1) // HEAD_DIM
    own_head = (head_of_row == head_of_channel).astype(F32).astype(BF16)
    head_of_lane = lax.broadcasted_iota(jnp.int32, (TOKENS, HEADS * TOKENS), 1) // TOKENS
    mixed_heads = []
    residual = []
    for start in starts:
        rows = slice(start, start + TOKENS)
        keys = jnp.concatenate([keyed[rows]] * HEADS, axis=0) * own_head
        values = jnp.concatenate([valued[rows]] * HEADS, axis=0) * own_head
        scores = lax.dot_general(
            query[rows], keys, (((1,), (1,)), ((), ())), preferred_element_type=F32
        ) * (HEAD_DIM**-0.5)
        top = jnp.zeros_like(scores)
        for head in range(HEADS):
            inside = head_of_lane == head
            largest = jnp.max(jnp.where(inside, scores, -jnp.inf), axis=1, keepdims=True)
            top = jnp.where(inside, largest, top)
        weight = jnp.exp(scores - top).astype(BF16)
        mixed_heads.append((dot(weight, values) / dot(weight, own_head)).astype(BF16))
        residual.append(zeta[rows])
    attended = jnp.concatenate(mixed_heads, axis=0)
    resid = (jnp.concatenate(residual, axis=0) + dot(attended, w_attn_out[...])).astype(BF16)
    return dot(resid, w_up[...])


def activate(number, sources, first, lifted, active, base):
    half_rows = active.shape[0] // 2
    count = sum(rows for _, _, rows in sources) // 8
    for block_col in range(4):
        raised = lifted[pl.ds(number * TOKENS + first * 4 + block_col, count, stride=4)].reshape(
            count, 1, CH
        )
        done = 0
        for ref, start, rows in sources:
            part = raised[done // 8 : (done + rows) // 8]
            for cell in range(block_col * 8, block_col * 8 + 8):
                given = ref[pl.ds(start, rows), cell * CH : (cell + 1) * CH]
                value = silu(given.astype(F32).reshape(rows // 8, 8, CH) + part)
                to = base + done + cell // HALF * half_rows
                lane = cell % HALF * CH
                active[to : to + rows, lane : lane + CH] = value.reshape(rows, CH).astype(BF16)
            done += rows


def predict(halves, base, first, last, padded):
    rows = (last - first) * 8
    half_rows = halves.shape[0] // 2
    left = halves[base : base + rows]
    right = halves[half_rows + base : half_rows + base + rows]
    lane = lax.broadcasted_iota(jnp.int32, (rows, 128), 1)
    for tap in range(3):
        from_left = pltpu.roll(left, (-4 - TAP_LANES * tap) % 256, 1)[:, 0:128]
        from_right = pltpu.roll(right, (60 - TAP_LANES * tap) % 256, 1)[:, 0:128]
        padded[8 : 8 + rows, tap * 128 : (tap + 1) * 128] = jnp.where(
            lane < 68, from_left, 0.0
        ) + jnp.where(lane >= 60, from_right, 0.0)
    zero = jnp.zeros((8, 384), F32)
    padded[0:8] = zero
    padded[8 + rows : 16 + rows] = zero
    field = (
        padded[7 : 7 + rows, 0:128] + padded[8 : 8 + rows, 128:256] + padded[9 : 9 + rows, 256:384]
    )
    row = lax.broadcasted_iota(jnp.int32, (rows, 128), 0) + first * 8
    return field * jnp.minimum(row + 1, DOM - row).astype(F32)


def inner_kernel(
    held_in, *refs,
):
    inputs, (features_out, pooled_out, total), scratch = refs[:14], refs[14:17], refs[17:]
    locals_, (cond_right, stem_in, features, pooled, lifted, active, halves, padded, sems) = (
        scratch[:14],
        scratch[14:],
    )
    mixes, across, taps, along, own_in, stem_right, levels = locals_[:7]
    weights, out_right = locals_[7:13], locals_[13]
    copies = fetch(sems, list(zip(inputs, locals_)))
    held = held_in[0]
    for copy in copies[0:3]:
        copy.wait()
    wide_high, wide_low = conditioning(mixes, 24, across, taps)
    cond_right[...] = by_tap(wide_high, wide_low, taps)
    for copy in copies[3:7]:
        copy.wait()
    for start in range(0, STEM_LANES, 256):
        stop = min(start + 256, STEM_LANES)
        stem_in[:, start:stop] = own_in[:, start:stop] + dot(
            along[...], cond_right[:, start:stop]
        ).astype(BF16)
    pooled[0:8] = jnp.zeros((8, CH), F32)
    pooled[8 + OWN_TOKENS :] = jnp.zeros((8, CH), F32)

    def store_pooled(block_col, value):
        pooled[pl.ds(8 + block_col, OWN_ROWS // 8, stride=4)] = value

    stem(stem_in, stem_right, levels[0:1], features, store_pooled)
    out_copy = pltpu.make_async_copy(features, features_out, sems.at[14])
    out_copy.start()
    pooled_out[...] = pooled[8 : 8 + OWN_TOKENS]
    lifted[...] = bottleneck(
        pooled[...], [16 * patch for patch in range(1, SLOTS - 1)], weights, copies[7:13]
    )
    for patch in range(1, SLOTS - 1):
        activate(
            patch - 1, [(features, P_SIZE * patch - M, DOM)], 0, lifted, active, DOM * (patch - 1)
        )
    copies[13].wait()
    halves[...] = dot(active[...], out_right[...])
    total[...] = jnp.zeros_like(total)
    for patch in range(1, SLOTS - 1):
        span = slice(P_SIZE * patch - M, P_SIZE * patch - M + DOM)
        field = predict(halves, DOM * (patch - 1), 0, 8, padded.at[patch % 2])
        total[span] = total[span] + jnp.where(patch <= held - 2, field, 0.0)
    out_copy.wait()


def edge_kernel(
    held_in, *refs,
):
    inputs, (denoised_out, next_out), scratch = refs[:21], refs[21:23], refs[23:]
    locals_, rest = scratch[:21], scratch[21:]
    noisy, mean_field, first_in, second_in, mix_own, levels, across, taps, along = locals_[:9]
    spread, stem_right, pooled_own, features = locals_[9:13]
    weights, out_right, total = locals_[13:19], locals_[19], locals_[20]
    (
        state_rows, mean_rows, mixes, cond_right, stem_left, stem_in, ends, pooled, lifted, active,
        halves, padded, sems,
    ) = rest
    pairs = []
    for number, (given, held_here) in enumerate(zip(inputs, locals_)):
        if number == 9:
            pairs += [(given.at[chunk], held_here.at[chunk]) for chunk in range(CHUNKS)]
        else:
            pairs.append((given, held_here))
    copies = fetch(sems, pairs)
    chunk_copies = copies[9 : 9 + CHUNKS]
    copies = copies[:9] + [None] + copies[9 + CHUNKS :]
    held = held_in[0]
    position = lax.axis_index("space")
    even = lax.rem(position, 2) == 0
    has_left = position > 0
    has_right = position < lax.axis_size("space") - 1
    for copy in copies[0:9]:
        copy.wait()
    c_in = levels[4:5].reshape(1, 1, 128)

    state_rows[0, 64:96] = (c_in * noisy[0:1]).reshape(P_SIZE, 128)
    mean_rows[0, 64:96] = mean_field[0]
    state_rows[1, 0:32] = (c_in * noisy[pl.ds(held - 1, 1)]).reshape(P_SIZE, 128)
    mean_rows[1, 0:32] = mean_field[pl.ds(held - 1, 1)].reshape(P_SIZE, 128)
    mixes[16:24] = mix_own[0:8]
    mixes[24:32] = jnp.zeros((8, 128), F32)
    mixes[32:40] = mix_own[pl.ds(pl.multiple_of(8 * held - 8, 8), 8)]
    mixes[56:64] = jnp.zeros((8, 128), F32)

    def take(piece, side, rows_at, mixes_at):
        state_rows[side, rows_at : rows_at + 64] = piece[0:64].astype(F32)
        mean_rows[side, rows_at : rows_at + 64] = piece[64:128].astype(F32)
        mixes[mixes_at : mixes_at + 16] = piece[128:144].astype(F32) + piece[144:160].astype(F32)

    @pl.when(even)
    def _():
        take(second_in, 0, 0, 0)
        take(first_in, 1, 32, 40)

    @pl.when(jnp.logical_not(even))
    def _():
        take(first_in, 0, 0, 0)
        take(second_in, 1, 32, 40)

    wide_high, wide_low = conditioning(mixes, 32, across, taps)
    for side in range(2):
        span = slice(16 * side, 16 * side + 16)
        cond_right[side] = by_tap(wide_high[span], wide_low[span], taps)
        for tap in range(3):
            for array, rows in enumerate((state_rows, mean_rows)):
                lane = tap * IN_LANES + array * 128
                stem_left[SIDE_ROWS * side : SIDE_ROWS * (side + 1), lane : lane + 128] = rows[
                    side, 15 + tap : 15 + tap + SIDE_ROWS
                ].astype(BF16)
    for chunk in range(CHUNKS):
        start = chunk * 256
        stop = min(start + 256, STEM_LANES)
        chunk_copies[chunk].wait()
        given = dot(stem_left[...], spread[chunk, :, 0 : stop - start])
        for side in range(2):
            span = slice(SIDE_ROWS * side, SIDE_ROWS * (side + 1))
            stem_in[span, start:stop] = (
                given[span] + dot(along[...], cond_right[side, :, start:stop])
            ).astype(BF16)

    def store_pooled(block_col, value):
        pooled[pl.ds(block_col, 8, stride=4)] = value[0:8]
        pooled[pl.ds(64 + block_col, 8, stride=4)] = value[8:16]

    for copy in copies[10:13]:
        copy.wait()
    stem(stem_in, stem_right, levels[0:1], ends, store_pooled)
    pooled[32:48] = pooled_own[8:24]
    pooled[48:64] = pooled_own[pl.ds(pl.multiple_of(16 * held - 24, 8), 16)]

    @pl.when(jnp.logical_not(has_left))
    def _():
        ends[0:48] = jnp.zeros((48, W * CH), BF16)
        pooled[0:24] = jnp.zeros((24, CH), F32)

    @pl.when(jnp.logical_not(has_right))
    def _():
        ends[80:128] = jnp.zeros((48, W * CH), BF16)
        pooled[72:96] = jnp.zeros((24, CH), F32)

    lifted[...] = bottleneck(pooled[...], [0, 16, 48, 64], weights, copies[13:19])
    near = pl.multiple_of(P_SIZE * held - 48, 16)
    activate(0, [(ends, 32, 32)], 4, lifted, active, 0)
    activate(1, [(ends, 32, 32), (features, 16, 32)], 0, lifted, active, 32)
    activate(2, [(features, near, 32), (ends, 64, 32)], 0, lifted, active, 96)
    activate(3, [(ends, 64, 32)], 0, lifted, active, 160)
    copies[19].wait()
    halves[...] = dot(active[...], out_right[...])
    copies[20].wait()
    field = predict(halves, 0, 4, 8, padded.at[0])
    total[0:M] = total[0:M] + jnp.where(has_left, field[16:32], 0.0)
    field = predict(halves, 32, 0, 8, padded.at[1])
    total[0:48] = total[0:48] + field[16:64]
    field = predict(halves, 96, 0, 8, padded.at[0])
    total[pl.ds(near, 48)] = total[pl.ds(near, 48)] + field[0:48]
    field = predict(halves, 160, 0, 4, padded.at[1])
    last = pl.multiple_of(P_SIZE * held - M, 16)
    total[pl.ds(last, M)] = total[pl.ds(last, M)] + jnp.where(has_right, field[0:16], 0.0)

    slot = lax.broadcasted_iota(jnp.int32, (SLOTS, P_SIZE, 128), 0)
    row = lax.broadcasted_iota(jnp.int32, (SLOTS, P_SIZE, 128), 1)
    norm = jnp.full((SLOTS, P_SIZE, 128), 33, jnp.int32)
    no_left = jnp.logical_and(jnp.logical_not(has_left), jnp.logical_and(slot == 0, row < M))
    no_right = jnp.logical_and(
        jnp.logical_not(has_right), jnp.logical_and(slot == held - 1, row >= M)
    )
    norm = jnp.where(no_left, 17 + row, norm)
    norm = jnp.where(no_right, 48 - row, norm)
    blended = total[...].reshape(SLOTS, P_SIZE, 128) / norm.astype(F32)
    state = noisy[...]
    denoised = levels[1:2].reshape(1, 1, 128) * state + levels[2:3].reshape(1, 1, 128) * blended
    stepped = state + levels[3:4].reshape(1, 1, 128) * (state - denoised)
    live = slot < held
    denoised_out[...] = jnp.where(live, denoised, 0.0)
    next_out[...] = jnp.where(live, stepped, 0.0)


def shards(
    noisy,
    mean_field,
    coarse,
    counts,
    src,
    widx,
    table,
    sigma,
    sigma_next,
    w_stem,
    noise_embed,
    w_down,
    w_query,
    w_key,
    w_value,
    w_attn_out,
    w_up,
    w_out,
):
    owners = lax.axis_size("space")
    smem = pl.BlockSpec(memory_space=pltpu.SMEM)
    vmem = pl.BlockSpec(memory_space=pltpu.VMEM)
    hbm = pl.BlockSpec(memory_space=pltpu.HBM)
    limit = pltpu.CompilerParams(vmem_limit_bytes=24 * 1024 * 1024)
    limit = pltpu.CompilerParams(vmem_limit_bytes=VMEM_LIMIT)
    state = noisy[0]
    copies = pl.pallas_call(
        mix_kernel,
        out_shape=jax.ShapeDtypeStruct((MEMBERS, 8, 128), F32),
        in_specs=[hbm] * 4,
        out_specs=vmem,
        scratch_shapes=[
            pltpu.SMEM((MIX, SLOTS), jnp.int32),
            pltpu.SMEM((MIX, SLOTS), jnp.int32),
            pltpu.SMEM((16,), F32),
            pltpu.VMEM((BLK_DEV, 24), F32),
            pltpu.SemaphoreType.DMA((4,)),
        ],
        compiler_params=limit,
        name="mix",
    )(src.T, widx.T, table, coarse)
    cells = lax.all_to_all(copies, "member", 0, 0, tiled=True)

    spread, across, taps, along, along_side, place = (jnp.asarray(array) for array in tables())
    scalars = jnp.concatenate([sigma, sigma_next, counts.astype(F32)])
    embed = noise_embed.reshape(1, CH)
    held, first, second, own_in, levels, stem_right, out_right = pl.pallas_call(
        prepare_kernel,
        out_shape=(
            jax.ShapeDtypeStruct((8,), jnp.int32),
            jax.ShapeDtypeStruct((PIECE, 128), BF16),
            jax.ShapeDtypeStruct((PIECE, 128), BF16),
            jax.ShapeDtypeStruct((OWN_ROWS, STEM_LANES), BF16),
            jax.ShapeDtypeStruct((8, 128), F32),
            jax.ShapeDtypeStruct((CH2, CH2), BF16),
            jax.ShapeDtypeStruct((HALF_LANES, 256), BF16),
        ),
        in_specs=[hbm] * 8,
        out_specs=[smem] + [vmem] * 6,
        scratch_shapes=[
            pltpu.SMEM((3,), F32),
            pltpu.VMEM((SLOTS, P_SIZE, 128), F32),
            pltpu.VMEM((SLOTS, P_SIZE, 128), F32),
            pltpu.VMEM(w_stem.shape, BF16),
            pltpu.VMEM((1, CH), F32),
            pltpu.VMEM(w_out.shape, BF16),
            pltpu.VMEM(spread.shape, BF16),
            pltpu.VMEM(place.shape, BF16),
            pltpu.VMEM((OWN_ROWS + 16, 128), F32),
            pltpu.VMEM((OWN_ROWS + 16, 128), F32),
            pltpu.VMEM((OWN_ROWS, 3 * IN_LANES), BF16),
            pltpu.VMEM((256, 256), F32),
            pltpu.SemaphoreType.DMA((7 + CHUNKS,)),
        ],
        compiler_params=limit,
        cost_estimate=pl.CostEstimate(flops=10**9, bytes_accessed=8 * 10**6, transcendentals=0),
        name="prepare",
    )(scalars, state, mean_field, w_stem, embed, w_out, spread, place)

    first, second, mix_own = pl.pallas_call(
        pack_kernel,
        out_shape=(
            jax.ShapeDtypeStruct((PIECE, 128), BF16),
            jax.ShapeDtypeStruct((PIECE, 128), BF16),
            jax.ShapeDtypeStruct((SLOTS * MEMBERS, 128), F32),
        ),
        in_specs=[smem] + [vmem] * 3,
        out_specs=(vmem, vmem, vmem),
        compiler_params=limit,
        name="pack",
    )(held, cells, first, second)
    pairs = [(i, i ^ 1) for i in range(owners)]
    others = []
    for i in range(1, owners - 1, 2):
        others += [(i, i + 1), (i + 1, i)]
    first = lax.ppermute(first, "space", pairs)
    second = lax.ppermute(second, "space", others)

    weights = [w_down, w_query, w_key, w_value, w_attn_out, w_up]
    given = [mix_own, across, taps, along, own_in, stem_right, levels, *weights, out_right]
    features, pooled, total = pl.pallas_call(
        inner_kernel,
        out_shape=(
            jax.ShapeDtypeStruct((OWN_ROWS, W * CH), BF16),
            jax.ShapeDtypeStruct((OWN_TOKENS, CH), F32),
            jax.ShapeDtypeStruct((OWN_ROWS, 128), F32),
        ),
        in_specs=[smem] + [hbm] * len(given),
        out_specs=(hbm, vmem, vmem),
        scratch_shapes=[pltpu.VMEM(array.shape, array.dtype) for array in given]
        + [
            pltpu.VMEM((144, STEM_LANES), BF16),
            pltpu.VMEM((OWN_ROWS, STEM_LANES), BF16),
            pltpu.VMEM((OWN_ROWS, W * CH), BF16),
            pltpu.VMEM((OWN_TOKENS + 16, CH), F32),
            pltpu.VMEM((4 * TOKENS, CH), F32),
            pltpu.VMEM((2 * 4 * DOM, HALF_LANES), BF16),
            pltpu.VMEM((2 * 4 * DOM, 256), F32),
            pltpu.VMEM((2, 80, 384), F32),
            pltpu.SemaphoreType.DMA((15,)),
        ],
        compiler_params=limit,
        cost_estimate=pl.CostEstimate(flops=10**9, bytes_accessed=10**7, transcendentals=2 * 10**6),
        name="inner",
    )(held, *given)

    given = [state, mean_field, first, second, mix_own, levels, across, taps, along_side, spread]
    given += [stem_right, pooled, features, *weights, out_right, total]
    denoised, stepped = pl.pallas_call(
        edge_kernel,
        out_shape=(
            jax.ShapeDtypeStruct((SLOTS, P_SIZE, 128), F32),
            jax.ShapeDtypeStruct((SLOTS, P_SIZE, 128), F32),
        ),
        in_specs=[smem] + [hbm] * len(given),
        out_specs=(vmem, vmem),
        scratch_shapes=[pltpu.VMEM(array.shape, array.dtype) for array in given]
        + [
            pltpu.VMEM((2, 96, 128), F32),
            pltpu.VMEM((2, 96, 128), F32),
            pltpu.VMEM((64, 128), F32),
            pltpu.VMEM((2, 96, STEM_LANES), BF16),
            pltpu.VMEM((2 * SIDE_ROWS, 3 * IN_LANES), BF16),
            pltpu.VMEM((2 * SIDE_ROWS, STEM_LANES), BF16),
            pltpu.VMEM((2 * SIDE_ROWS, W * CH), BF16),
            pltpu.VMEM((96, CH), F32),
            pltpu.VMEM((4 * TOKENS, CH), F32),
            pltpu.VMEM((2 * 192, HALF_LANES), BF16),
            pltpu.VMEM((2 * 192, 256), F32),
            pltpu.VMEM((2, 80, 384), F32),
            pltpu.SemaphoreType.DMA((len(given) + CHUNKS,)),
        ],
        compiler_params=limit,
        cost_estimate=pl.CostEstimate(flops=10**9, bytes_accessed=10**7, transcendentals=2 * 10**6),
        name="edge",
    )(held, *given)
    return denoised[None], stepped[None]


def solution(mesh):
    placed = (
        P("member", "space", None, None),
        P("space", None, None),
        P("space", "member"),
        P("space"),
        P("space", None),
        P("space", None),
        P(),
        P("member"),
        P("member"),
        P(),
        P(),
        P(),
        P(),
        P(),
        P(),
        P(),
        P(),
        P(),
    )
    return jax.shard_map(
        shards,
        mesh=mesh,
        in_specs=placed,
        out_specs=(P("member", "space", None, None), P("member", "space", None, None)),
        check_vma=False,
    )
```

```python
import functools

import jax
import jax.numpy as jnp
import numpy as np
from jax import lax
from jax.experimental import pallas as pl
from jax.experimental.pallas import tpu as pltpu
from jax.sharding import PartitionSpec as P

VARS = 4
CCH = 12
CIN = 20
CH = 128
CH2 = 256
HEADS = 4
HEAD_DIM = 64
P_SIZE = 32
M = 16
W = 32
SLOTS = 6
FACTOR = 8
BLK_DEV = 8
MIX = 4
DOM = 64
TOKENS = 32
BR = 4
BW = 4
MEMBERS = 8

SIGMA_DATA = 0.5
NORM_EPS = 1e-06

F32 = jnp.float32
BF16 = jnp.bfloat16

IN_LANES = 2 * W * VARS
CELL = 64
STEM_LANES = (W + 2) * CELL
OWN_ROWS = SLOTS * P_SIZE
DOMAINS = SLOTS + 2
SIDE_ROWS = 64
OWN_TOKENS = OWN_ROWS // 8 * 4
SIDE_PATCHES = 4
PIECE = 160
BASIS = IN_LANES + 2 * BW * CCH
SIDE_SPAN = 80
CHUNKS = 9
HALF = W // 2
HALF_LANES = HALF * CH
TAP_LANES = (HALF + 2) * VARS
GROUP_ROWS = 224
VMEM_LIMIT = 24 * 1024 * 1024


def interp_matrix(fine_count, coarse_count):
    position = (np.arange(fine_count) + 0.5) / FACTOR - 0.5
    position = np.clip(position, 0.0, coarse_count - 1.0)
    return np.maximum(0.0, 1.0 - np.abs(position[:, None] - np.arange(coarse_count)[None, :]))


def along_rows(sources, patches):
    row_map = interp_matrix(P_SIZE, BR)
    along = np.zeros((len(sources), 2, patches, BR), np.float32)
    for row, source in enumerate(sources):
        along[row, :, source // P_SIZE] = row_map[source % P_SIZE][None]
    return along


@functools.cache
def tables():
    col_map = interp_matrix(W, BW)
    noisy, mean = (np.zeros((W, VARS, W + 2, CELL), np.float32) for _ in range(2))
    across = np.zeros((2, BW, CCH, W + 2, CELL), np.float32)
    for tap in range(3):
        at = tap * CIN
        for col in range(W):
            for var in range(VARS):
                noisy[col, var, col + 1, at + var] = 1.0
                mean[col, var, col + 1, at + VARS + var] = 1.0
        for channel in range(CCH):
            across[:, :, channel, 1 : W + 1, at + 2 * VARS + channel] = col_map.T[None]
    basis = np.concatenate([part.reshape(-1, STEM_LANES) for part in (noisy, mean, across)])
    basis = np.pad(basis, ((0, 0), (0, CHUNKS * 256 - STEM_LANES)))
    basis = basis.reshape(BASIS, CHUNKS, 256).transpose(1, 0, 2)
    along = along_rows(range(OWN_ROWS), SLOTS).reshape(OWN_ROWS, 2 * SLOTS * BR)
    side = along_rows(range(8, 8 + SIDE_SPAN), SIDE_PATCHES)
    along_side = np.zeros((2, SIDE_SPAN, 2, 2, SIDE_PATCHES, BR), np.float32)
    for number in range(2):
        along_side[number, :, :, number] = side
    along_side = along_side.reshape(2 * SIDE_SPAN, 4 * SIDE_PATCHES * BR)
    place = np.zeros((3, 3, VARS, HALF, 256), np.float32)
    for cell in range(HALF):
        for row_tap in range(3):
            for col_tap in range(3):
                for var in range(VARS):
                    lane = row_tap * TAP_LANES + (cell + 2 - col_tap) * VARS + var
                    place[row_tap, col_tap, var, cell, lane] = 1.0
    place = place.reshape(36, HALF * 256)
    return tuple(array.astype(jnp.bfloat16) for array in (basis, along, along_side, place))


def silu(value):
    half = 0.5 * value
    return half + half * jnp.tanh(half)


def dot(left, right):
    return jnp.dot(left, right, preferred_element_type=F32)


def fetch(sems, pairs):
    copies = [pltpu.make_async_copy(a, b, sems.at[i]) for i, (a, b) in enumerate(pairs)]
    for copy in copies:
        copy.start()
    return copies


def mix_kernel(src, widx, table, coarse, copies_out, src_s, widx_s, table_s, blocks, sems):
    for copy in fetch(sems, [(src, src_s), (widx, widx_s), (table, table_s), (coarse, blocks)]):
        copy.wait()
    copies_out[...] = jnp.zeros_like(copies_out)
    for slot in range(SLOTS):
        total = jnp.zeros((1, 24), F32)
        for k in range(MIX):
            total = total + table_s[widx_s[k, slot]] * blocks[pl.ds(src_s[k, slot], 1)]
        for member in range(MEMBERS):
            copies_out[member, slot : slot + 1, 0:24] = total


def prepare_kernel(
    counts, sigma, sigma_next, noise_embed, w_stem, noisy, mean_field, basis, along,
    noisy_v, mean_v, basis_v, along_v, held_out, first_out, second_out, levels_out, stem_out,
    embed_v, w_stem_v, stem_f32, sems,
):
    copies = fetch(
        sems,
        [
            (noise_embed, embed_v),
            (noisy, noisy_v),
            (mean_field, mean_v),
            (w_stem, w_stem_v),
            (basis, basis_v),
            (along, along_v),
        ],
    )
    stem_f32[...] = jnp.zeros_like(stem_f32)
    for copy in copies[0:3]:
        copy.wait()
    held = counts[0]
    held_out[0] = held
    level = jnp.full((1, 128), sigma[0], F32)
    variance = level * level + SIGMA_DATA * SIGMA_DATA
    c_in = lax.rsqrt(variance)
    levels_out[0:1] = jnp.log(level) * 0.125 * embed_v[...].reshape(1, CH)
    levels_out[1:2] = SIGMA_DATA * SIGMA_DATA / variance
    levels_out[2:3] = level * SIGMA_DATA * lax.rsqrt(variance)
    levels_out[3:4] = jnp.full((1, 128), sigma_next[0], F32) / level - 1.0
    levels_out[4:5] = c_in
    even = lax.rem(lax.axis_index("space"), 2) == 0
    c_in = c_in.reshape(1, 1, 128)
    for out, to_right in ((first_out, even), (second_out, jnp.logical_not(even))):
        start = jnp.where(to_right, held - 2, 0)
        out[0:64] = (c_in * noisy_v[pl.ds(start, 2)]).astype(BF16).reshape(64, 128)
        out[64:128] = mean_v[pl.ds(start, 2)].astype(BF16).reshape(64, 128)

    copies[3].wait()
    stem_taps = w_stem_v[...].astype(F32) * 0.5
    for cell in range(4):
        for target in range(2):
            col_tap = cell - target
            if 0 <= col_tap < 3:
                for row_tap in range(3):
                    at = (3 * row_tap + col_tap) * CIN
                    to = cell * CELL + row_tap * CIN
                    stem_f32[to : to + CIN, target * CH : (target + 1) * CH] = stem_taps[at : at + CIN]
    stem_out[...] = stem_f32[...].astype(BF16)
    for copy in copies[4:]:
        copy.wait()


def pack_kernel(held_in, cells, first_in, second_in, first_out, second_out, mix_out):
    held = held_in[0]
    for member in range(MEMBERS):
        mix_out[pl.ds(member, SLOTS, stride=MEMBERS)] = cells[member, 0:SLOTS]
    even = lax.rem(lax.axis_index("space"), 2) == 0
    for out, given, to_right in (
        (first_out, first_in, even),
        (second_out, second_in, jnp.logical_not(even)),
    ):
        start = pl.multiple_of(jnp.where(to_right, held - 2, 0) * MEMBERS, MEMBERS)
        out[0:128] = given[0:128]
        mixed = mix_out[pl.ds(start, 16)]
        high = mixed.astype(BF16)
        out[128:144] = high
        out[144:160] = (mixed - high.astype(F32)).astype(BF16)


def interpolate(mixes, count, along):
    pair = mixes[pl.ds(0, count, stride=2)] + pltpu.roll(mixes[pl.ds(1, count, stride=2)], 24, 1)
    high = pair.astype(BF16).astype(F32)
    rows = dot(along[...], jnp.concatenate([high, pair - high], axis=0).astype(BF16))
    high = rows.astype(BF16).astype(F32)
    return (high + pltpu.roll(rows - high, 48, 1)).astype(BF16)


def widen(operand, basis, blocks, wide, stem_in):
    rows = operand.shape[0]
    lane = lax.rem(lax.broadcasted_iota(jnp.int32, (1, 128), 1), CELL)
    above, here = lane < CIN, lane < 2 * CIN
    zero = jnp.zeros((8, 128), F32)
    for number in range(4):
        wide[number, 0:8] = zero
        wide[number, 8 + rows :] = zero
    given = operand[:, 0:BASIS]
    for chunk in range(CHUNKS):
        lanes = min(256, STEM_LANES - chunk * 256)
        product = dot(given, basis[chunk, :, 0:lanes])
        for half in range(lanes // 128):
            number = chunk % 2 * 2 + half
            wide[number, 8 : 8 + rows] = product[:, half * 128 : (half + 1) * 128]
            start = chunk * 256 + half * 128
            for first, to, count in blocks:
                at = 8 + first
                stem_in[to : to + count, start : start + 128] = jnp.where(
                    above,
                    wide[number, at - 1 : at - 1 + count],
                    jnp.where(
                        here, wide[number, at : at + count], wide[number, at + 1 : at + 1 + count]
                    ),
                ).astype(BF16)


def stem(stem_in, stem_right, shift, features, store_pooled):
    rows = features.shape[0]
    for block_col in range(4):
        summed = jnp.zeros((rows, CH), F32)
        for cell_pair in range(4):
            number = block_col * 4 + cell_pair
            raw = dot(stem_in[:, number * 128 : number * 128 + 256], stem_right[...])
            for part in range(2):
                half = raw[:, part * CH : (part + 1) * CH] + shift
                feature = (0.5 * half) * (1.0 + jnp.tanh(half))
                lane = number * 256 + part * CH
                features[:, lane : lane + CH] = feature.astype(BF16)
                summed = summed + feature
        store_pooled(block_col, jnp.sum(summed.reshape(rows // 8, 8, CH), axis=1) * (1.0 / 32.0))


def bottleneck(pooled, starts, weights):
    w_down, w_query, w_key, w_value, w_attn_out, w_up = weights
    zeta = silu(dot(pooled.astype(BF16), w_down[...]))
    scale = lax.rsqrt(jnp.mean(zeta * zeta, axis=-1, keepdims=True) + NORM_EPS)
    normed = (zeta * scale).astype(BF16)
    query = dot(normed, w_query[...]).astype(BF16)
    keyed = dot(normed, w_key[...]).astype(BF16)
    valued = dot(normed, w_value[...]).astype(BF16)
    head_of_row = lax.broadcasted_iota(jnp.int32, (HEADS * TOKENS, CH2), 0) // TOKENS
    head_of_channel = lax.broadcasted_iota(jnp.int32, (HEADS * TOKENS, CH2), 1) // HEAD_DIM
    own_head = (head_of_row == head_of_channel).astype(F32).astype(BF16)
    head_of_lane = lax.broadcasted_iota(jnp.int32, (TOKENS, HEADS * TOKENS), 1) // TOKENS
    mixed_heads = []
    residual = []
    for start in starts:
        rows = slice(start, start + TOKENS)
        keys = jnp.concatenate([keyed[rows]] * HEADS, axis=0) * own_head
        values = jnp.concatenate([valued[rows]] * HEADS, axis=0) * own_head
        scores = lax.dot_general(
            query[rows], keys, (((1,), (1,)), ((), ())), preferred_element_type=F32
        ) * (HEAD_DIM**-0.5)
        top = jnp.zeros_like(scores)
        for head in range(HEADS):
            inside = head_of_lane == head
            largest = jnp.max(jnp.where(inside, scores, -jnp.inf), axis=1, keepdims=True)
            top = jnp.where(inside, largest, top)
        weight = jnp.exp(scores - top).astype(BF16)
        mixed_heads.append((dot(weight, values) / dot(weight, own_head)).astype(BF16))
        residual.append(zeta[rows])
    attended = jnp.concatenate(mixed_heads, axis=0)
    resid = (jnp.concatenate(residual, axis=0) + dot(attended, w_attn_out[...])).astype(BF16)
    return 0.5 * dot(resid, w_up[...])


def activate(number, sources, first, lifted, active, base):
    half_rows = active.shape[0] // 2
    count = sum(rows for _, _, rows in sources) // 8
    for block_col in range(4):
        raised = lifted[pl.ds(number * TOKENS + first * 4 + block_col, count, stride=4)].reshape(
            count, 1, CH
        )
        done = 0
        for ref, start, rows in sources:
            part = raised[done // 8 : (done + rows) // 8]
            for cell in range(block_col * 8, block_col * 8 + 8):
                given = ref[pl.ds(start, rows), cell * CH : (cell + 1) * CH]
                half = given.astype(F32).reshape(rows // 8, 8, CH) + part
                value = half + half * jnp.tanh(half)
                to = base + done + cell // HALF * half_rows
                lane = cell % HALF * CH
                active[to : to + rows, lane : lane + CH] = value.reshape(rows, CH).astype(BF16)
            done += rows


def predict(left, right, first, last, padded):
    rows = (last - first) * 8
    lane = lax.broadcasted_iota(jnp.int32, (rows, 128), 1)
    for tap in range(3):
        from_left = pltpu.roll(left, (-4 - TAP_LANES * tap) % 256, 1)[:, 0:128]
        from_right = pltpu.roll(right, (60 - TAP_LANES * tap) % 256, 1)[:, 0:128]
        padded[8 : 8 + rows, tap * 128 : (tap + 1) * 128] = jnp.where(
            lane < 68, from_left, 0.0
        ) + jnp.where(lane >= 60, from_right, 0.0)
    zero = jnp.zeros((8, 384), F32)
    padded[0:8] = zero
    padded[8 + rows : 16 + rows] = zero
    field = (
        padded[7 : 7 + rows, 0:128] + padded[8 : 8 + rows, 128:256] + padded[9 : 9 + rows, 256:384]
    )
    row = lax.broadcasted_iota(jnp.int32, (rows, 128), 0) + first * 8
    return field * jnp.minimum(row + 1, DOM - row).astype(F32)


def own_kernel(
    noisy, mean_field, mixes, along, levels, basis, stem_right, w_out, place, *refs
):
    loaded, kept = refs[:7], refs[7:14]
    features, pooled, right_out = refs[14:17]
    w_out_v, place_v, operand, wide, stem_in, sems = refs[17:]
    copies = fetch(sems, [(w_out, w_out_v), (place, place_v)] + list(zip(loaded, kept)))
    c_in = levels[4:5].reshape(1, 1, 128)
    operand[:, 0:128] = (c_in * noisy[...]).astype(BF16).reshape(OWN_ROWS, 128)
    operand[:, 128:256] = mean_field[...].astype(BF16).reshape(OWN_ROWS, 128)
    operand[:, 256:384] = interpolate(mixes, SLOTS * BR, along)
    widen(operand, basis, [(0, 0, OWN_ROWS)], wide, stem_in)

    def store_pooled(block_col, value):
        pooled[pl.ds(block_col, OWN_ROWS // 8, stride=4)] = value

    stem(stem_in, stem_right, levels[0:1], features, store_pooled)
    for copy in copies[0:2]:
        copy.wait()
    weights = w_out_v[...]
    for cell in range(HALF):
        right_out[cell * CH : (cell + 1) * CH] = lax.dot_general(
            weights,
            place_v[:, cell * 256 : (cell + 1) * 256],
            (((0,), (0,)), ((), ())),
            preferred_element_type=F32,
        ).astype(BF16)
    for copy in copies[2:]:
        copy.wait()


def main_kernel(
    held_in, noisy, mean_field, first_in, second_in, mix_own, levels, along, basis, stem_right,
    pooled_own, features, w_down, w_query, w_key, w_value, w_attn_out, w_up, out_right,
    denoised_out, next_out,
    state_rows, mean_rows, mixes, operand, wide, stem_in, ends, pooled, lifted, active, halves,
    padded, total,
):
    held = held_in[0]
    position = lax.axis_index("space")
    even = lax.rem(position, 2) == 0
    has_left = position > 0
    has_right = position < lax.axis_size("space") - 1
    c_in = levels[4:5].reshape(1, 1, 128)

    state_rows[0, 64:96] = (c_in * noisy[0:1]).reshape(P_SIZE, 128)
    mean_rows[0, 64:96] = mean_field[0]
    state_rows[1, 0:32] = (c_in * noisy[pl.ds(held - 1, 1)]).reshape(P_SIZE, 128)
    mean_rows[1, 0:32] = mean_field[pl.ds(held - 1, 1)].reshape(P_SIZE, 128)
    mixes[16:24] = mix_own[0:8]
    mixes[24:32] = jnp.zeros((8, 128), F32)
    mixes[32:40] = mix_own[pl.ds(pl.multiple_of(8 * held - 8, 8), 8)]
    mixes[56:64] = jnp.zeros((8, 128), F32)

    def take(piece, side, rows_at, mixes_at):
        state_rows[side, rows_at : rows_at + 64] = piece[0:64].astype(F32)
        mean_rows[side, rows_at : rows_at + 64] = piece[64:128].astype(F32)
        mixes[mixes_at : mixes_at + 16] = piece[128:144].astype(F32) + piece[144:160].astype(F32)

    @pl.when(even)
    def _():
        take(second_in, 0, 0, 0)
        take(first_in, 1, 32, 40)

    @pl.when(jnp.logical_not(even))
    def _():
        take(first_in, 0, 0, 0)
        take(second_in, 1, 32, 40)

    for side in range(2):
        span = slice(SIDE_SPAN * side, SIDE_SPAN * (side + 1))
        operand[span, 0:128] = state_rows[side, 8 : 8 + SIDE_SPAN].astype(BF16)
        operand[span, 128:256] = mean_rows[side, 8 : 8 + SIDE_SPAN].astype(BF16)
    operand[:, 256:384] = interpolate(mixes, 2 * SIDE_PATCHES * BR, along)
    widen(
        operand, basis, [(8, 0, SIDE_ROWS), (SIDE_SPAN + 8, SIDE_ROWS, SIDE_ROWS)], wide, stem_in
    )

    def store_pooled(block_col, value):
        pooled[pl.ds(block_col, 8, stride=4)] = value[0:8]
        pooled[pl.ds(64 + block_col, 8, stride=4)] = value[8:16]

    stem(stem_in, stem_right, levels[0:1], ends, store_pooled)
    pooled[32:48] = pooled_own[8:24]
    pooled[48:64] = pooled_own[pl.ds(pl.multiple_of(16 * held - 24, 8), 16)]
    pooled[96:104] = jnp.zeros((8, CH), F32)
    pooled[104:200] = pooled_own[...]
    pooled[200:208] = jnp.zeros((8, CH), F32)

    @pl.when(jnp.logical_not(has_left))
    def _():
        ends[0:48] = jnp.zeros((48, W * CH), BF16)
        pooled[0:24] = jnp.zeros((24, CH), F32)

    @pl.when(jnp.logical_not(has_right))
    def _():
        ends[80:128] = jnp.zeros((48, W * CH), BF16)
        pooled[72:96] = jnp.zeros((24, CH), F32)

    lifted[...] = bottleneck(
        pooled[...],
        [0, 16, 112, 128, 144, 160, 48, 64],
        (w_down, w_query, w_key, w_value, w_attn_out, w_up),
    )
    near = pl.multiple_of(P_SIZE * held - 48, 16)
    last = pl.multiple_of(P_SIZE * held - M, 16)
    plans = [
        (4, 8, [(ends, 32, 32)], 0, 16, 32, has_left),
        (0, 8, [(ends, 32, 32), (features, 16, 32)], 0, 16, 64, True),
    ]
    for patch in range(1, SLOTS - 1):
        start = P_SIZE * patch - M
        plans.append((0, 8, [(features, start, DOM)], start, 0, 64, patch <= held - 2))
    plans += [
        (0, 8, [(features, near, 32), (ends, 64, 32)], near, 0, 48, True),
        (0, 4, [(ends, 64, 32)], last, 0, 16, has_right),
    ]
    total[...] = jnp.zeros_like(total)
    for group in range(2):
        base = 0
        for number in range(4 * group, 4 * group + 4):
            first, stop, sources = plans[number][:3]
            activate(number, sources, first, lifted, active.at[group], base)
            base += (stop - first) * 8
        halves[group] = dot(active[group], out_right[...])
    for group in range(2):
        base = 0
        for number in range(4 * group, 4 * group + 4):
            first, stop, _, to, start, end, counted = plans[number]
            rows = (stop - first) * 8
            field = predict(
                halves[group, base : base + rows],
                halves[group, GROUP_ROWS + base : GROUP_ROWS + base + rows],
                first,
                stop,
                padded.at[number % 2],
            )[start:end]
            if counted is not True:
                field = jnp.where(counted, field, 0.0)
            span = pl.ds(to, end - start)
            total[span] = total[span] + field
            base += rows

    slot = lax.broadcasted_iota(jnp.int32, (SLOTS, P_SIZE, 128), 0)
    row = lax.broadcasted_iota(jnp.int32, (SLOTS, P_SIZE, 128), 1)
    norm = jnp.full((SLOTS, P_SIZE, 128), 33, jnp.int32)
    no_left = jnp.logical_and(jnp.logical_not(has_left), jnp.logical_and(slot == 0, row < M))
    no_right = jnp.logical_and(
        jnp.logical_not(has_right), jnp.logical_and(slot == held - 1, row >= M)
    )
    norm = jnp.where(no_left, 17 + row, norm)
    norm = jnp.where(no_right, 48 - row, norm)
    blended = total[...].reshape(SLOTS, P_SIZE, 128) / norm.astype(F32)
    state = noisy[...]
    denoised = levels[1:2].reshape(1, 1, 128) * state + levels[2:3].reshape(1, 1, 128) * blended
    stepped = state + levels[3:4].reshape(1, 1, 128) * (state - denoised)
    live = slot < held
    denoised_out[...] = jnp.where(live, denoised, 0.0)
    next_out[...] = jnp.where(live, stepped, 0.0)


def shards(
    noisy,
    mean_field,
    coarse,
    counts,
    src,
    widx,
    table,
    sigma,
    sigma_next,
    w_stem,
    noise_embed,
    w_down,
    w_query,
    w_key,
    w_value,
    w_attn_out,
    w_up,
    w_out,
):
    owners = lax.axis_size("space")
    smem = pl.BlockSpec(memory_space=pltpu.SMEM)
    vmem = pl.BlockSpec(memory_space=pltpu.VMEM)
    hbm = pl.BlockSpec(memory_space=pltpu.HBM)
    limit = pltpu.CompilerParams(vmem_limit_bytes=VMEM_LIMIT)

    def in_hbm(*arrays):
        return [pltpu.with_memory_space_constraint(array, pltpu.HBM) for array in arrays]

    def in_vmem(*shapes):
        return [pltpu.VMEM(shape, dtype) for shape, dtype in shapes]

    state = noisy[0]
    copies = pl.pallas_call(
        mix_kernel,
        out_shape=pltpu.VMEM((MEMBERS, 8, 128), F32),
        in_specs=[hbm] * 4,
        out_specs=vmem,
        scratch_shapes=[
            pltpu.SMEM((MIX, SLOTS), jnp.int32),
            pltpu.SMEM((MIX, SLOTS), jnp.int32),
            pltpu.SMEM((16,), F32),
            pltpu.VMEM((BLK_DEV, 24), F32),
            pltpu.SemaphoreType.DMA((4,)),
        ],
        compiler_params=limit,
        name="mix",
    )(*in_hbm(src.T, widx.T, table, coarse))
    cells = lax.all_to_all(copies, "member", 0, 0, tiled=True)

    basis, along, along_side, place = (jnp.asarray(array) for array in tables())
    loaded = [state, mean_field, basis, along]
    prepared = pl.pallas_call(
        prepare_kernel,
        out_shape=in_vmem(*((array.shape, array.dtype) for array in loaded))
        + [jax.ShapeDtypeStruct((8,), jnp.int32)]
        + in_vmem(
            ((PIECE, 128), BF16), ((PIECE, 128), BF16), ((8, 128), F32), ((CH2, CH2), BF16)
        ),
        in_specs=[smem] * 3 + [hbm] * 6,
        out_specs=[vmem] * 4 + [smem] + [vmem] * 4,
        scratch_shapes=[
            pltpu.VMEM(noise_embed.shape, F32),
            pltpu.VMEM(w_stem.shape, BF16),
            pltpu.VMEM((256, 256), F32),
            pltpu.SemaphoreType.DMA((6,)),
        ],
        compiler_params=limit,
        cost_estimate=pl.CostEstimate(flops=10**9, bytes_accessed=8 * 10**6, transcendentals=0),
        name="prepare",
    )(counts, sigma, sigma_next, *in_hbm(noise_embed, w_stem, *loaded))
    state, mean_field, basis, along, held, first, second, levels, stem_right = prepared

    first, second, mix_own = pl.pallas_call(
        pack_kernel,
        out_shape=in_vmem(
            ((PIECE, 128), BF16), ((PIECE, 128), BF16), ((SLOTS * MEMBERS, 128), F32)
        ),
        in_specs=[smem] + [vmem] * 3,
        out_specs=[vmem] * 3,
        compiler_params=limit,
        name="pack",
    )(held, cells, first, second)
    pairs = [(i, i ^ 1) for i in range(owners)]
    others = []
    for i in range(1, owners - 1, 2):
        others += [(i, i + 1), (i + 1, i)]
    first = lax.ppermute(first, "space", pairs)
    second = lax.ppermute(second, "space", others)

    loaded = [along_side, w_down, w_query, w_key, w_value, w_attn_out, w_up]
    *loaded, features, pooled, out_right = pl.pallas_call(
        own_kernel,
        out_shape=in_vmem(*((array.shape, array.dtype) for array in loaded))
        + in_vmem(
            ((OWN_ROWS, W * CH), BF16), ((OWN_TOKENS, CH), F32), ((HALF_LANES, 256), BF16)
        ),
        in_specs=[vmem] * 7 + [hbm] * 9,
        out_specs=[vmem] * 10,
        scratch_shapes=[
            pltpu.VMEM(w_out.T.shape, BF16),
            pltpu.VMEM(place.shape, BF16),
            pltpu.VMEM((OWN_ROWS, 384), BF16),
            pltpu.VMEM((4, OWN_ROWS + 16, 128), F32),
            pltpu.VMEM((OWN_ROWS, STEM_LANES), BF16),
            pltpu.SemaphoreType.DMA((9,)),
        ],
        compiler_params=limit,
        cost_estimate=pl.CostEstimate(flops=10**9, bytes_accessed=10**7, transcendentals=2 * 10**6),
        name="own",
    )(
        state, mean_field, mix_own, along, levels, basis, stem_right,
        *in_hbm(w_out.T, place, *loaded),
    )
    along_side, *weights = loaded

    denoised, stepped = pl.pallas_call(
        main_kernel,
        out_shape=(
            jax.ShapeDtypeStruct((SLOTS, P_SIZE, 128), F32),
            jax.ShapeDtypeStruct((SLOTS, P_SIZE, 128), F32),
        ),
        in_specs=[smem] + [vmem] * 18,
        out_specs=(vmem, vmem),
        scratch_shapes=[
            pltpu.VMEM((2, 96, 128), F32),
            pltpu.VMEM((2, 96, 128), F32),
            pltpu.VMEM((64, 128), F32),
            pltpu.VMEM((2 * SIDE_SPAN, 384), BF16),
            pltpu.VMEM((4, 2 * SIDE_SPAN + 16, 128), F32),
            pltpu.VMEM((2 * SIDE_ROWS, STEM_LANES), BF16),
            pltpu.VMEM((2 * SIDE_ROWS, W * CH), BF16),
            pltpu.VMEM((208, CH), F32),
            pltpu.VMEM((DOMAINS * TOKENS, CH), F32),
            pltpu.VMEM((2, 2 * GROUP_ROWS, HALF_LANES), BF16),
            pltpu.VMEM((2, 2 * GROUP_ROWS, 256), F32),
            pltpu.VMEM((2, 80, 384), F32),
            pltpu.VMEM((OWN_ROWS, 128), F32),
        ],
        compiler_params=limit,
        cost_estimate=pl.CostEstimate(flops=10**9, bytes_accessed=10**7, transcendentals=2 * 10**6),
        name="main",
    )(
        held, state, mean_field, first, second, mix_own, levels, along_side, basis, stem_right,
        pooled, features, *weights, out_right,
    )
    return denoised[None], stepped[None]


def solution(mesh):
    placed = (
        P("member", "space", None, None),
        P("space", None, None),
        P("space", "member"),
        P("space"),
        P("space", None),
        P("space", None),
        P(),
        P("member"),
        P("member"),
        P(),
        P(),
        P(),
        P(),
        P(),
        P(),
        P(),
        P(),
        P(),
    )
    return jax.shard_map(
        shards,
        mesh=mesh,
        in_specs=placed,
        out_specs=(P("member", "space", None, None), P("member", "space", None, None)),
        check_vma=False,
    )
```

```python
import functools

import jax
import jax.numpy as jnp
import numpy as np
from jax import lax
from jax.experimental import pallas as pl
from jax.experimental.pallas import tpu as pltpu
from jax.sharding import PartitionSpec as P

VARS = 4
CCH = 12
CIN = 20
CH = 128
CH2 = 256
HEADS = 4
HEAD_DIM = 64
P_SIZE = 32
M = 16
W = 32
SLOTS = 6
FACTOR = 8
BLK_DEV = 8
MIX = 4
DOM = 64
TOKENS = 32
BR = 4
BW = 4
MEMBERS = 8
DISTANCES = (1, 3, 2)

SIGMA_DATA = 0.5
NORM_EPS = 1e-06

F32 = jnp.float32
BF16 = jnp.bfloat16

CELL = 64
STEM_LANES = (W + 2) * CELL
OWN_ROWS = SLOTS * P_SIZE
SIDE_ROWS = 64
OWN_TOKENS = OWN_ROWS // 8 * 4
SIDE_PATCHES = 4
PIECE = 160
LEFT_LANES = 1152
SIDE_SPAN = 80
HALF = W // 2
HALF_LANES = HALF * CH
TAP_LANES = (HALF + 2) * VARS
VMEM_LIMIT = 24 * 1024 * 1024


def interp_matrix(fine_count, coarse_count):
    position = (np.arange(fine_count) + 0.5) / FACTOR - 0.5
    position = np.clip(position, 0.0, coarse_count - 1.0)
    return np.maximum(0.0, 1.0 - np.abs(position[:, None] - np.arange(coarse_count)[None, :]))


def along_rows(sources, patches):
    row_map = interp_matrix(P_SIZE, BR)
    along = np.zeros((len(sources), 2, patches, BR), np.float32)
    for row, source in enumerate(sources):
        along[row, :, source // P_SIZE] = row_map[source % P_SIZE][None]
    return along


@functools.cache
def tables():
    col_map = interp_matrix(W, BW)
    noisy, mean = (np.zeros((W, VARS, W + 2, CELL), np.float32) for _ in range(2))
    across = np.zeros((2, BW, CCH, W + 2, CELL), np.float32)
    for tap in range(3):
        at = tap * CIN
        for col in range(W):
            for var in range(VARS):
                noisy[col, var, col + 1, at + var] = 1.0
                mean[col, var, col + 1, at + VARS + var] = 1.0
        for channel in range(CCH):
            across[:, :, channel, 1 : W + 1, at + 2 * VARS + channel] = col_map.T[None]
    basis = np.zeros((2, 256, LEFT_LANES), np.float32)
    for half, lanes in enumerate((slice(0, LEFT_LANES), slice(LEFT_LANES, STEM_LANES))):
        count = lanes.stop - lanes.start
        cells = slice(HALF * half, HALF * half + HALF)
        basis[half, 0:64, :count] = noisy[cells].reshape(64, STEM_LANES)[:, lanes]
        basis[half, 64:128, :count] = mean[cells].reshape(64, STEM_LANES)[:, lanes]
        basis[half, 128:224, :count] = across.reshape(96, STEM_LANES)[:, lanes]
    basis[0, 224:228] = noisy[HALF].reshape(4, STEM_LANES)[:, :LEFT_LANES]
    basis[0, 228:232] = mean[HALF].reshape(4, STEM_LANES)[:, :LEFT_LANES]
    along = along_rows(range(OWN_ROWS), SLOTS).reshape(OWN_ROWS, 2 * SLOTS * BR)
    side = along_rows(range(8, 8 + SIDE_SPAN), SIDE_PATCHES)
    along_side = np.zeros((2, SIDE_SPAN, 2, 2, SIDE_PATCHES, BR), np.float32)
    for number in range(2):
        along_side[number, :, :, number] = side
    along_side = along_side.reshape(2 * SIDE_SPAN, 4 * SIDE_PATCHES * BR)
    place = np.zeros((3, 3, VARS, HALF, 256), np.float32)
    for cell in range(HALF):
        for row_tap in range(3):
            for col_tap in range(3):
                for var in range(VARS):
                    lane = row_tap * TAP_LANES + (cell + 2 - col_tap) * VARS + var
                    place[row_tap, col_tap, var, cell, lane] = 1.0
    place = place.reshape(36, HALF * 256)
    return tuple(array.astype(jnp.bfloat16) for array in (basis, along, along_side, place))


def silu(value):
    half = 0.5 * value
    return half + half * jnp.tanh(half)


def dot(left, right):
    return jnp.dot(left, right, preferred_element_type=F32)


def fetch(sems, pairs):
    copies = [pltpu.make_async_copy(a, b, sems.at[i]) for i, (a, b) in enumerate(pairs)]
    for copy in copies:
        copy.start()
    return copies


def mix_kernel(src, widx, table, coarse, mixed_out, src_s, widx_s, table_s, blocks, sems):
    for copy in fetch(sems, [(src, src_s), (widx, widx_s), (table, table_s), (coarse, blocks)]):
        copy.wait()
    mixed_out[...] = jnp.zeros_like(mixed_out)
    for slot in range(SLOTS):
        total = jnp.zeros((1, 24), F32)
        for k in range(MIX):
            total = total + table_s[widx_s[k, slot]] * blocks[pl.ds(src_s[k, slot], 1)]
        mixed_out[slot : slot + 1, 0:24] = total


def merge_kernel(mixed, partners, merged_out):
    core = lax.rem(lax.axis_index("member"), 2)
    merged_out[pl.ds(pl.multiple_of(8 * core, 8), 8)] = mixed[...]
    merged_out[pl.ds(pl.multiple_of(8 - 8 * core, 8), 8)] = partners[...]


def prepare_kernel(counts, sigma, noise_embed, w_stem, w_out, place, *refs):
    loaded, kept, rest = refs[:11], refs[11:22], refs[22:]
    (
        held_out, first_out, second_out, levels_out, stem_out, right_out,
        embed_v, w_stem_v, w_out_v, place_v, stem_f32, sems,
    ) = rest
    noisy_v, mean_v = kept[:2]
    copies = fetch(
        sems,
        [
            (noise_embed, embed_v),
            (loaded[0], noisy_v),
            (loaded[1], mean_v),
            (w_stem, w_stem_v),
            (w_out, w_out_v),
            (place, place_v),
        ]
        + list(zip(loaded[2:], kept[2:])),
    )
    stem_f32[...] = jnp.zeros_like(stem_f32)
    for copy in copies[0:3]:
        copy.wait()
    held = counts[0]
    held_out[0] = held
    level = jnp.full((1, 128), sigma[0], F32)
    variance = level * level + SIGMA_DATA * SIGMA_DATA
    c_in = lax.rsqrt(variance)
    levels_out[0:1] = jnp.log(level) * 0.125 * embed_v[...].reshape(1, CH)
    levels_out[1:2] = SIGMA_DATA * SIGMA_DATA / variance
    levels_out[2:3] = level * SIGMA_DATA * lax.rsqrt(variance)
    levels_out[3:4] = 1.0 / level
    levels_out[4:5] = c_in
    even = lax.rem(lax.axis_index("space"), 2) == 0
    c_in = c_in.reshape(1, 1, 128)
    for out, to_right in ((first_out, even), (second_out, jnp.logical_not(even))):
        start = jnp.where(to_right, held - 2, 0)
        out[0:64] = (c_in * noisy_v[pl.ds(start, 2)]).astype(BF16).reshape(64, 128)
        out[64:128] = mean_v[pl.ds(start, 2)].astype(BF16).reshape(64, 128)

    copies[3].wait()
    stem_taps = w_stem_v[...].astype(F32) * 0.5
    for cell in range(4):
        for target in range(2):
            col_tap = cell - target
            if 0 <= col_tap < 3:
                for row_tap in range(3):
                    at = (3 * row_tap + col_tap) * CIN
                    to = cell * CELL + row_tap * CIN
                    stem_f32[to : to + CIN, target * CH : (target + 1) * CH] = stem_taps[at : at + CIN]
    stem_out[...] = stem_f32[...].astype(BF16)
    for copy in copies[4:6]:
        copy.wait()
    weights = jnp.transpose(w_out_v[...].astype(F32)).astype(BF16)
    for cell in range(HALF):
        right_out[cell * CH : (cell + 1) * CH] = dot(
            weights, place_v[:, cell * 256 : (cell + 1) * 256]
        ).astype(BF16)
    for copy in copies[6:]:
        copy.wait()


def pack_kernel(held_in, chip0, chip1, chip2, chip3, first_in, second_in, second_out, first_out, mix_out, cells):
    held = held_in[0]
    chip = lax.axis_index("member") // 2
    for distance, given in zip((0, *DISTANCES), (chip0, chip1, chip2, chip3)):
        member = 2 * jnp.bitwise_xor(chip, distance)
        cells[member] = given[0:8]
        cells[member + 1] = given[8:16]
    for member in range(MEMBERS):
        mix_out[pl.ds(member, SLOTS, stride=MEMBERS)] = cells[member, 0:SLOTS]
    even = lax.rem(lax.axis_index("space"), 2) == 0
    for out, given, to_right in (
        (first_out, first_in, even),
        (second_out, second_in, jnp.logical_not(even)),
    ):
        start = pl.multiple_of(jnp.where(to_right, held - 2, 0) * MEMBERS, MEMBERS)
        out[0:128] = given[0:128]
        mixed = mix_out[pl.ds(start, 16)]
        high = mixed.astype(BF16)
        out[128:144] = high
        out[144:160] = (mixed - high.astype(F32)).astype(BF16)


def interpolate(mixes, count, along):
    pair = mixes[pl.ds(0, count, stride=2)] + pltpu.roll(mixes[pl.ds(1, count, stride=2)], 24, 1)
    high = pair.astype(BF16).astype(F32)
    rows = dot(along[...], jnp.concatenate([high, pair - high], axis=0).astype(BF16))
    high = rows.astype(BF16).astype(F32)
    return high + pltpu.roll(rows - high, 48, 1)


def assemble(operand, state, mean, cond):
    lane = lax.broadcasted_iota(jnp.int32, state.shape, 1)
    left = lane < 64
    operand[0, :, 0:128] = jnp.where(left, state, pltpu.roll(mean, 64, 1)).astype(BF16)
    operand[1, :, 0:128] = jnp.where(left, pltpu.roll(state, 64, 1), mean).astype(BF16)
    operand[1, :, 128:256] = cond.astype(BF16)
    more = jnp.where(lane < 100, pltpu.roll(state, 32, 1), pltpu.roll(mean, 36, 1))
    operand[0, :, 128:256] = jnp.where(lane < 96, cond, jnp.where(lane < 104, more, 0.0)).astype(BF16)


def widen(operand, basis, blocks, wide, stem_in):
    rows = operand.shape[1]
    lane = lax.rem(lax.broadcasted_iota(jnp.int32, (1, 128), 1), CELL)
    above, here = lane < CIN, lane < 2 * CIN
    zero = jnp.zeros((8, 128), F32)
    for number in range(4):
        wide[number, 0:8] = zero
        wide[number, 8 + rows :] = zero
    turn = 0
    for half, (start, stop) in enumerate(((0, LEFT_LANES), (LEFT_LANES, STEM_LANES))):
        given = operand[half]
        for chunk in range(start, stop, 256):
            lanes = min(256, stop - chunk)
            at = chunk - start
            product = dot(given, basis[half, :, at : at + lanes])
            for part in range(0, lanes, 128):
                number = turn % 4
                turn += 1
                wide[number, 8 : 8 + rows] = product[:, part : part + 128]
                to_lane = chunk + part
                for first, to, count in blocks:
                    at_row = 8 + first
                    stem_in[to : to + count, to_lane : to_lane + 128] = jnp.where(
                        above,
                        wide[number, at_row - 1 : at_row - 1 + count],
                        jnp.where(
                            here,
                            wide[number, at_row : at_row + count],
                            wide[number, at_row + 1 : at_row + 1 + count],
                        ),
                    ).astype(BF16)


def stem(stem_in, stem_right, shift, features, store_pooled):
    rows = features.shape[0]
    for block_col in range(4):
        summed = jnp.zeros((rows, CH), F32)
        for cell_pair in range(4):
            number = block_col * 4 + cell_pair
            raw = dot(stem_in[:, number * 128 : number * 128 + 256], stem_right[...])
            for part in range(2):
                half = raw[:, part * CH : (part + 1) * CH] + shift
                feature = (0.5 * half) * (1.0 + jnp.tanh(half))
                lane = number * 256 + part * CH
                features[:, lane : lane + CH] = feature.astype(BF16)
                summed = summed + feature
        store_pooled(block_col, jnp.sum(summed.reshape(rows // 8, 8, CH), axis=1) * (1.0 / 32.0))


def bottleneck(pooled, starts, weights):
    w_down, w_query, w_key, w_value, w_attn_out, w_up = weights
    zeta = silu(dot(pooled.astype(BF16), w_down[...]))
    scale = lax.rsqrt(jnp.mean(zeta * zeta, axis=-1, keepdims=True) + NORM_EPS)
    given = zeta.astype(BF16)
    query = (scale * HEAD_DIM**-0.5 * dot(given, w_query[...])).astype(BF16)
    keyed = (scale * dot(given, w_key[...])).astype(BF16)
    valued = (scale * dot(given, w_value[...])).astype(BF16)
    head_of_row = lax.broadcasted_iota(jnp.int32, (HEADS * TOKENS, CH2), 0) // TOKENS
    head_of_channel = lax.broadcasted_iota(jnp.int32, (HEADS * TOKENS, CH2), 1) // HEAD_DIM
    own_head = (head_of_row == head_of_channel).astype(F32).astype(BF16)
    head_of_lane = lax.broadcasted_iota(jnp.int32, (TOKENS, HEADS * TOKENS), 1) // TOKENS
    mixed_heads = []
    residual = []
    for start in starts:
        rows = slice(start, start + TOKENS)
        keys = jnp.concatenate([keyed[rows]] * HEADS, axis=0) * own_head
        values = jnp.concatenate([valued[rows]] * HEADS, axis=0) * own_head
        scores = lax.dot_general(
            query[rows], keys, (((1,), (1,)), ((), ())), preferred_element_type=F32
        )
        top = jnp.zeros_like(scores)
        for head in range(HEADS):
            inside = head_of_lane == head
            largest = jnp.max(jnp.where(inside, scores, -jnp.inf), axis=1, keepdims=True)
            top = jnp.where(inside, largest, top)
        weight = jnp.exp(scores - top).astype(BF16)
        mixed_heads.append((dot(weight, values) / dot(weight, own_head)).astype(BF16))
        residual.append(zeta[rows])
    attended = jnp.concatenate(mixed_heads, axis=0)
    resid = (jnp.concatenate(residual, axis=0) + dot(attended, w_attn_out[...])).astype(BF16)
    return 0.5 * dot(resid, w_up[...])


def activate(number, sources, first, lifted, active, base):
    half_rows = active.shape[0] // 2
    count = sum(rows for _, _, rows in sources) // 8
    for block_col in range(4):
        raised = lifted[pl.ds(number * TOKENS + first * 4 + block_col, count, stride=4)].reshape(
            count, 1, CH
        )
        done = 0
        for ref, start, rows in sources:
            part = raised[done // 8 : (done + rows) // 8]
            for cell in range(block_col * 8, block_col * 8 + 8):
                given = ref[pl.ds(start, rows), cell * CH : (cell + 1) * CH]
                half = given.astype(F32).reshape(rows // 8, 8, CH) + part
                value = half + half * jnp.tanh(half)
                to = base + done + cell // HALF * half_rows
                lane = cell % HALF * CH
                active[to : to + rows, lane : lane + CH] = value.reshape(rows, CH).astype(BF16)
            done += rows


def predict(left, right, first, last, padded):
    rows = (last - first) * 8
    lane = lax.broadcasted_iota(jnp.int32, (rows, 128), 1)
    for tap in range(3):
        from_left = pltpu.roll(left, (-4 - TAP_LANES * tap) % 256, 1)[:, 0:128]
        from_right = pltpu.roll(right, (60 - TAP_LANES * tap) % 256, 1)[:, 0:128]
        padded[8 : 8 + rows, tap * 128 : (tap + 1) * 128] = jnp.where(
            lane < 68, from_left, 0.0
        ) + jnp.where(lane >= 60, from_right, 0.0)
    zero = jnp.zeros((8, 384), F32)
    padded[0:8] = zero
    padded[8 + rows : 16 + rows] = zero
    field = (
        padded[7 : 7 + rows, 0:128] + padded[8 : 8 + rows, 128:256] + padded[9 : 9 + rows, 256:384]
    )
    row = lax.broadcasted_iota(jnp.int32, (rows, 128), 0) + first * 8
    return field * jnp.minimum(row + 1, DOM - row).astype(F32)


def convolve(plans, group_rows, lifted, active, halves, padded, out_right, total):
    groups = active.shape[0]
    each = len(plans) // groups
    for group in range(groups):
        base = 0
        for number in range(each * group, each * group + each):
            first, stop, sources = plans[number][:3]
            activate(number, sources, first, lifted, active.at[group], base)
            base += (stop - first) * 8
        halves[group] = dot(active[group], out_right[...])
    for group in range(groups):
        base = 0
        for number in range(each * group, each * group + each):
            first, stop, _, to, start, end, counted = plans[number]
            rows = (stop - first) * 8
            field = predict(
                halves[group, base : base + rows],
                halves[group, group_rows + base : group_rows + base + rows],
                first,
                stop,
                padded.at[number % 2],
            )[start:end]
            if counted is not True:
                field = jnp.where(counted, field, 0.0)
            span = pl.ds(to, end - start)
            total[span] = total[span] + field
            base += rows


def own_kernel(
    held_in, noisy, mean_field, mixes, along, levels, basis, stem_right, out_right, *refs
):
    weights = refs[:6]
    features, pooled_out, total = refs[6:9]
    operand, wide, stem_in, pooled, lifted, active, halves, padded = refs[9:]
    held = held_in[0]
    assemble(
        operand,
        levels[4:5] * noisy[...].reshape(OWN_ROWS, 128),
        mean_field[...].reshape(OWN_ROWS, 128),
        interpolate(mixes, SLOTS * BR, along),
    )
    widen(operand, basis, [(0, 0, OWN_ROWS)], wide, stem_in)
    pooled[0:8] = jnp.zeros((8, CH), F32)
    pooled[8 + OWN_TOKENS :] = jnp.zeros((8, CH), F32)
    total[...] = jnp.zeros_like(total)

    def store_pooled(block_col, value):
        pooled[pl.ds(8 + block_col, OWN_ROWS // 8, stride=4)] = value

    stem(stem_in, stem_right, levels[0:1], features, store_pooled)
    pooled_out[...] = pooled[8 : 8 + OWN_TOKENS]
    inner = range(1, SLOTS - 1)
    lifted[...] = bottleneck(pooled[...], [16 * patch for patch in inner], weights)
    plans = []
    for patch in inner:
        start = P_SIZE * patch - M
        plans.append((0, 8, [(features, start, DOM)], start, 0, 64, patch <= held - 2))
    convolve(plans, 2 * DOM, lifted, active, halves, padded, out_right, total)


def main_kernel(
    held_in, sigma_next, noisy, mean_field, second_in, first_in, mix_own, levels, along, basis, stem_right,
    pooled_own, features, total_own, w_down, w_query, w_key, w_value, w_attn_out, w_up, out_right,
    denoised_out, next_out,
    state_rows, mean_rows, mixes, operand, wide, stem_in, ends, pooled, lifted, active, halves,
    padded, total,
):
    held = held_in[0]
    position = lax.axis_index("space")
    even = lax.rem(position, 2) == 0
    has_left = position > 0
    has_right = position < lax.axis_size("space") - 1
    c_in = levels[4:5].reshape(1, 1, 128)

    state_rows[0, 64:96] = (c_in * noisy[0:1]).reshape(P_SIZE, 128)
    mean_rows[0, 64:96] = mean_field[0]
    state_rows[1, 0:32] = (c_in * noisy[pl.ds(held - 1, 1)]).reshape(P_SIZE, 128)
    mean_rows[1, 0:32] = mean_field[pl.ds(held - 1, 1)].reshape(P_SIZE, 128)
    mixes[16:24] = mix_own[0:8]
    mixes[24:32] = jnp.zeros((8, 128), F32)
    mixes[32:40] = mix_own[pl.ds(pl.multiple_of(8 * held - 8, 8), 8)]
    mixes[56:64] = jnp.zeros((8, 128), F32)

    def take(piece, side, rows_at, mixes_at):
        state_rows[side, rows_at : rows_at + 64] = piece[0:64].astype(F32)
        mean_rows[side, rows_at : rows_at + 64] = piece[64:128].astype(F32)
        mixes[mixes_at : mixes_at + 16] = piece[128:144].astype(F32) + piece[144:160].astype(F32)

    @pl.when(even)
    def _():
        take(second_in, 0, 0, 0)
        take(first_in, 1, 32, 40)

    @pl.when(jnp.logical_not(even))
    def _():
        take(first_in, 0, 0, 0)
        take(second_in, 1, 32, 40)

    assemble(
        operand,
        state_rows[:, 8 : 8 + SIDE_SPAN].reshape(2 * SIDE_SPAN, 128),
        mean_rows[:, 8 : 8 + SIDE_SPAN].reshape(2 * SIDE_SPAN, 128),
        interpolate(mixes, 2 * SIDE_PATCHES * BR, along),
    )
    widen(
        operand, basis, [(8, 0, SIDE_ROWS), (SIDE_SPAN + 8, SIDE_ROWS, SIDE_ROWS)], wide, stem_in
    )

    def store_pooled(block_col, value):
        pooled[pl.ds(block_col, 8, stride=4)] = value[0:8]
        pooled[pl.ds(64 + block_col, 8, stride=4)] = value[8:16]

    stem(stem_in, stem_right, levels[0:1], ends, store_pooled)
    pooled[32:48] = pooled_own[8:24]
    pooled[48:64] = pooled_own[pl.ds(pl.multiple_of(16 * held - 24, 8), 16)]

    @pl.when(jnp.logical_not(has_left))
    def _():
        ends[0:48] = jnp.zeros((48, W * CH), BF16)
        pooled[0:24] = jnp.zeros((24, CH), F32)

    @pl.when(jnp.logical_not(has_right))
    def _():
        ends[80:128] = jnp.zeros((48, W * CH), BF16)
        pooled[72:96] = jnp.zeros((24, CH), F32)

    lifted[...] = bottleneck(
        pooled[...], [0, 16, 48, 64], (w_down, w_query, w_key, w_value, w_attn_out, w_up)
    )
    near = pl.multiple_of(P_SIZE * held - 48, 16)
    last = pl.multiple_of(P_SIZE * held - M, 16)
    plans = [
        (4, 8, [(ends, 32, 32)], 0, 16, 32, has_left),
        (0, 8, [(ends, 32, 32), (features, 16, 32)], 0, 16, 64, True),
        (0, 8, [(features, near, 32), (ends, 64, 32)], near, 0, 48, True),
        (0, 4, [(ends, 64, 32)], last, 0, 16, has_right),
    ]
    total[...] = total_own[...]
    convolve(plans, 96, lifted, active, halves, padded, out_right, total)

    slot = lax.broadcasted_iota(jnp.int32, (SLOTS, P_SIZE, 128), 0)
    row = lax.broadcasted_iota(jnp.int32, (SLOTS, P_SIZE, 128), 1)
    norm = jnp.full((SLOTS, P_SIZE, 128), 33, jnp.int32)
    no_left = jnp.logical_and(jnp.logical_not(has_left), jnp.logical_and(slot == 0, row < M))
    no_right = jnp.logical_and(
        jnp.logical_not(has_right), jnp.logical_and(slot == held - 1, row >= M)
    )
    norm = jnp.where(no_left, 17 + row, norm)
    norm = jnp.where(no_right, 48 - row, norm)
    blended = total[...].reshape(SLOTS, P_SIZE, 128) / norm.astype(F32)
    state = noisy[...]
    denoised = levels[1:2].reshape(1, 1, 128) * state + levels[2:3].reshape(1, 1, 128) * blended
    step = sigma_next[0] * levels[3:4].reshape(1, 1, 128) - 1.0
    stepped = state + step * (state - denoised)
    live = slot < held
    denoised_out[...] = jnp.where(live, denoised, 0.0)
    next_out[...] = jnp.where(live, stepped, 0.0)


def shards(
    noisy,
    mean_field,
    coarse,
    counts,
    src,
    widx,
    table,
    sigma,
    sigma_next,
    w_stem,
    noise_embed,
    w_down,
    w_query,
    w_key,
    w_value,
    w_attn_out,
    w_up,
    w_out,
):
    owners = lax.axis_size("space")
    smem = pl.BlockSpec(memory_space=pltpu.SMEM)
    vmem = pl.BlockSpec(memory_space=pltpu.VMEM)
    hbm = pl.BlockSpec(memory_space=pltpu.HBM)
    limit = pltpu.CompilerParams(vmem_limit_bytes=VMEM_LIMIT)

    def in_hbm(*arrays):
        return [pltpu.with_memory_space_constraint(array, pltpu.HBM) for array in arrays]

    def in_vmem(*shapes):
        return [pltpu.VMEM(shape, dtype) for shape, dtype in shapes]

    state = noisy[0]
    mixed = pl.pallas_call(
        mix_kernel,
        out_shape=pltpu.VMEM((8, 128), F32),
        in_specs=[hbm] * 4,
        out_specs=vmem,
        scratch_shapes=[
            pltpu.SMEM((MIX, SLOTS), jnp.int32),
            pltpu.SMEM((MIX, SLOTS), jnp.int32),
            pltpu.SMEM((16,), F32),
            pltpu.VMEM((BLK_DEV, 24), F32),
            pltpu.SemaphoreType.DMA((4,)),
        ],
        compiler_params=limit,
        name="mix",
    )(*in_hbm(src.T, widx.T, table, coarse))
    partners = lax.ppermute(mixed, "member", [(i, i ^ 1) for i in range(MEMBERS)])
    merged = pl.pallas_call(
        merge_kernel,
        out_shape=pltpu.VMEM((16, 128), F32),
        in_specs=[vmem] * 2,
        out_specs=vmem,
        compiler_params=limit,
        name="merge",
    )(mixed, partners)
    chips = [merged] + [
        lax.ppermute(merged, "member", [(i, i ^ (2 * distance)) for i in range(MEMBERS)])
        for distance in DISTANCES
    ]

    basis, along, along_side, place = (jnp.asarray(array) for array in tables())
    loaded = [state, mean_field, basis, along, along_side]
    loaded += [w_down, w_query, w_key, w_value, w_attn_out, w_up]
    prepared = pl.pallas_call(
        prepare_kernel,
        out_shape=in_vmem(*((array.shape, array.dtype) for array in loaded))
        + [jax.ShapeDtypeStruct((8,), jnp.int32)]
        + in_vmem(
            ((PIECE, 128), BF16),
            ((PIECE, 128), BF16),
            ((8, 128), F32),
            ((CH2, CH2), BF16),
            ((HALF_LANES, 256), BF16),
        ),
        in_specs=[smem] * 2 + [hbm] * (4 + len(loaded)),
        out_specs=[vmem] * len(loaded) + [smem] + [vmem] * 5,
        scratch_shapes=[
            pltpu.VMEM(noise_embed.shape, F32),
            pltpu.VMEM(w_stem.shape, BF16),
            pltpu.VMEM(w_out.T.shape, BF16),
            pltpu.VMEM(place.shape, BF16),
            pltpu.VMEM((256, 256), F32),
            pltpu.SemaphoreType.DMA((4 + len(loaded),)),
        ],
        compiler_params=limit,
        cost_estimate=pl.CostEstimate(flops=10**9, bytes_accessed=8 * 10**6, transcendentals=0),
        name="prepare",
    )(counts, sigma, *in_hbm(noise_embed, w_stem, w_out.T, place, *loaded))
    state, mean_field, basis, along, along_side = prepared[:5]
    weights = prepared[5:11]
    held, first, second, levels, stem_right, out_right = prepared[11:]

    second, first, mix_own = pl.pallas_call(
        pack_kernel,
        out_shape=in_vmem(
            ((PIECE, 128), BF16), ((PIECE, 128), BF16), ((SLOTS * MEMBERS, 128), F32)
        ),
        in_specs=[smem] + [vmem] * 6,
        out_specs=[vmem] * 3,
        scratch_shapes=[pltpu.VMEM((MEMBERS, 8, 128), F32)],
        compiler_params=limit,
        name="pack",
    )(held, *chips, first, second)
    pairs = [(i, i ^ 1) for i in range(owners)]
    others = []
    for i in range(1, owners - 1, 2):
        others += [(i, i + 1), (i + 1, i)]
    second = lax.ppermute(second, "space", others)
    first = lax.ppermute(first, "space", pairs)

    features, pooled, total = pl.pallas_call(
        own_kernel,
        out_shape=in_vmem(
            ((OWN_ROWS, W * CH), BF16), ((OWN_TOKENS, CH), F32), ((OWN_ROWS, 128), F32)
        ),
        in_specs=[smem] + [vmem] * 14,
        out_specs=[vmem] * 3,
        scratch_shapes=[
            pltpu.VMEM((2, OWN_ROWS, 256), BF16),
            pltpu.VMEM((4, OWN_ROWS + 16, 128), F32),
            pltpu.VMEM((OWN_ROWS, STEM_LANES), BF16),
            pltpu.VMEM((OWN_TOKENS + 16, CH), F32),
            pltpu.VMEM((4 * TOKENS, CH), F32),
            pltpu.VMEM((2, 4 * DOM, HALF_LANES), BF16),
            pltpu.VMEM((2, 4 * DOM, 256), F32),
            pltpu.VMEM((2, 80, 384), F32),
        ],
        compiler_params=limit,
        cost_estimate=pl.CostEstimate(flops=10**9, bytes_accessed=10**7, transcendentals=2 * 10**6),
        name="own",
    )(
        held, state, mean_field, mix_own, along, levels, basis, stem_right, out_right, *weights
    )

    denoised, stepped = pl.pallas_call(
        main_kernel,
        out_shape=(
            jax.ShapeDtypeStruct((SLOTS, P_SIZE, 128), F32),
            jax.ShapeDtypeStruct((SLOTS, P_SIZE, 128), F32),
        ),
        in_specs=[smem] * 2 + [vmem] * 19,
        out_specs=(vmem, vmem),
        scratch_shapes=[
            pltpu.VMEM((2, 96, 128), F32),
            pltpu.VMEM((2, 96, 128), F32),
            pltpu.VMEM((64, 128), F32),
            pltpu.VMEM((2, 2 * SIDE_SPAN, 256), BF16),
            pltpu.VMEM((4, 2 * SIDE_SPAN + 16, 128), F32),
            pltpu.VMEM((2 * SIDE_ROWS, STEM_LANES), BF16),
            pltpu.VMEM((2 * SIDE_ROWS, W * CH), BF16),
            pltpu.VMEM((96, CH), F32),
            pltpu.VMEM((4 * TOKENS, CH), F32),
            pltpu.VMEM((2, 2 * 96, HALF_LANES), BF16),
            pltpu.VMEM((2, 2 * 96, 256), F32),
            pltpu.VMEM((2, 80, 384), F32),
            pltpu.VMEM((OWN_ROWS, 128), F32),
        ],
        compiler_params=limit,
        cost_estimate=pl.CostEstimate(flops=10**9, bytes_accessed=10**7, transcendentals=2 * 10**6),
        name="main",
    )(
        held, sigma_next, state, mean_field, second, first, mix_own, levels, along_side, basis, stem_right,
        pooled, features, total, *weights, out_right,
    )
    return denoised[None], stepped[None]


def solution(mesh):
    placed = (
        P("member", "space", None, None),
        P("space", None, None),
        P("space", "member"),
        P("space"),
        P("space", None),
        P("space", None),
        P(),
        P("member"),
        P("member"),
        P(),
        P(),
        P(),
        P(),
        P(),
        P(),
        P(),
        P(),
        P(),
    )
    return jax.shard_map(
        shards,
        mesh=mesh,
        in_specs=placed,
        out_specs=(P("member", "space", None, None), P("member", "space", None, None)),
        check_vma=False,
    )
```

```python
import functools

import jax
import jax.numpy as jnp
import numpy as np
from jax import lax
from jax.experimental import pallas as pl
from jax.experimental.pallas import tpu as pltpu
from jax.sharding import PartitionSpec as P

VARS = 4
CCH = 12
CIN = 20
CH = 128
CH2 = 256
HEADS = 4
HEAD_DIM = 64
P_SIZE = 32
M = 16
W = 32
SLOTS = 6
FACTOR = 8
BLK_DEV = 8
MIX = 4
DOM = 64
TOKENS = 32
BR = 4
BW = 4
MEMBERS = 8
DISTANCES = (1, 3, 2)

SIGMA_DATA = 0.5
NORM_EPS = 1e-06

F32 = jnp.float32
BF16 = jnp.bfloat16

CELL = 64
STEM_LANES = (W + 2) * CELL
OWN_ROWS = SLOTS * P_SIZE
SIDE_ROWS = 64
OWN_TOKENS = OWN_ROWS // 8 * 4
SIDE_PATCHES = 4
PIECE = 160
LEFT_LANES = 1152
SIDE_SPAN = 80
HALF = W // 2
HALF_LANES = HALF * CH
TAP_LANES = (HALF + 2) * VARS
EARLY = 3
LATE = SLOTS - 2 - EARLY
VMEM_LIMIT = 24 * 1024 * 1024


def interp_matrix(fine_count, coarse_count):
    position = (np.arange(fine_count) + 0.5) / FACTOR - 0.5
    position = np.clip(position, 0.0, coarse_count - 1.0)
    return np.maximum(0.0, 1.0 - np.abs(position[:, None] - np.arange(coarse_count)[None, :]))


def along_rows(sources, patches):
    row_map = interp_matrix(P_SIZE, BR)
    along = np.zeros((len(sources), 2, patches, BR), np.float32)
    for row, source in enumerate(sources):
        along[row, :, source // P_SIZE] = row_map[source % P_SIZE][None]
    return along


@functools.cache
def tables():
    col_map = interp_matrix(W, BW)
    noisy, mean = (np.zeros((W, VARS, W + 2, CELL), np.float32) for _ in range(2))
    across = np.zeros((2, BW, CCH, W + 2, CELL), np.float32)
    for tap in range(3):
        at = tap * CIN
        for col in range(W):
            for var in range(VARS):
                noisy[col, var, col + 1, at + var] = 1.0
                mean[col, var, col + 1, at + VARS + var] = 1.0
        for channel in range(CCH):
            across[:, :, channel, 1 : W + 1, at + 2 * VARS + channel] = col_map.T[None]
    basis = np.zeros((2, 256, LEFT_LANES), np.float32)
    for half, lanes in enumerate((slice(0, LEFT_LANES), slice(LEFT_LANES, STEM_LANES))):
        count = lanes.stop - lanes.start
        cells = slice(HALF * half, HALF * half + HALF)
        basis[half, 0:64, :count] = noisy[cells].reshape(64, STEM_LANES)[:, lanes]
        basis[half, 64:128, :count] = mean[cells].reshape(64, STEM_LANES)[:, lanes]
        basis[half, 128:224, :count] = across.reshape(96, STEM_LANES)[:, lanes]
        basis[half, 232, :count] = np.tile(np.arange(CELL) >= 3 * CIN, W + 2)[lanes]
    basis[0, 224:228] = noisy[HALF].reshape(4, STEM_LANES)[:, :LEFT_LANES]
    basis[0, 228:232] = mean[HALF].reshape(4, STEM_LANES)[:, :LEFT_LANES]
    along = along_rows(range(OWN_ROWS), SLOTS).reshape(OWN_ROWS, 2 * SLOTS * BR)
    side = along_rows(range(8, 8 + SIDE_SPAN), SIDE_PATCHES)
    along_side = np.zeros((2, SIDE_SPAN, 2, 2, SIDE_PATCHES, BR), np.float32)
    for number in range(2):
        along_side[number, :, :, number] = side
    along_side = along_side.reshape(2 * SIDE_SPAN, 4 * SIDE_PATCHES * BR)
    place = np.zeros((3, 3, VARS, HALF, 256), np.float32)
    for cell in range(HALF):
        for row_tap in range(3):
            for col_tap in range(3):
                for var in range(VARS):
                    lane = row_tap * TAP_LANES + (cell + 2 - col_tap) * VARS + var
                    place[row_tap, col_tap, var, cell, lane] = 1.0
    place = place.reshape(36, HALF * 256)
    return tuple(array.astype(jnp.bfloat16) for array in (basis, along, along_side, place))


def silu(value):
    half = 0.5 * value
    return half + half * jnp.tanh(half)


def dot(left, right):
    return jnp.dot(left, right, preferred_element_type=F32)


def fetch(sems, pairs):
    copies = [pltpu.make_async_copy(a, b, sems.at[i]) for i, (a, b) in enumerate(pairs)]
    for copy in copies:
        copy.start()
    return copies


def mix_kernel(src, widx, table, coarse, mixed_out, src_s, widx_s, table_s, blocks, sems):
    for copy in fetch(sems, [(src, src_s), (widx, widx_s), (table, table_s), (coarse, blocks)]):
        copy.wait()
    mixed_out[...] = jnp.zeros_like(mixed_out)
    for slot in range(SLOTS):
        total = jnp.zeros((1, 24), F32)
        for k in range(MIX):
            total = total + table_s[widx_s[k, slot]] * blocks[pl.ds(src_s[k, slot], 1)]
        mixed_out[slot : slot + 1, 0:24] = total


def merge_kernel(mixed, partners, merged_out):
    core = lax.rem(lax.axis_index("member"), 2)
    merged_out[pl.ds(pl.multiple_of(8 * core, 8), 8)] = mixed[...]
    merged_out[pl.ds(pl.multiple_of(8 - 8 * core, 8), 8)] = partners[...]


def prepare_kernel(counts, sigma, noise_embed, w_stem, w_out, place, w_value, w_attn_out, *refs):
    loaded, kept, rest = refs[:9], refs[9:18], refs[18:]
    (
        first_out, second_out, levels_out, stem_out, right_out, joint_out,
        value_v, attn_v, embed_v, w_stem_v, w_out_v, place_v, stem_f32, sems,
    ) = rest
    noisy_v, mean_v = kept[:2]
    copies = fetch(
        sems,
        [
            (noise_embed, embed_v),
            (loaded[0], noisy_v),
            (loaded[1], mean_v),
            (w_stem, w_stem_v),
            (w_out, w_out_v),
            (place, place_v),
            (w_value, value_v),
            (w_attn_out, attn_v),
        ]
        + list(zip(loaded[2:], kept[2:])),
    )
    stem_f32[...] = jnp.zeros_like(stem_f32)
    for copy in copies[0:3]:
        copy.wait()
    held = counts[0]
    level = jnp.full((1, 128), sigma[0], F32)
    variance = level * level + SIGMA_DATA * SIGMA_DATA
    c_in = lax.rsqrt(variance)
    levels_out[0:1] = jnp.log(level) * 0.125 * embed_v[...].reshape(1, CH)
    levels_out[1:2] = SIGMA_DATA * SIGMA_DATA / variance
    levels_out[2:3] = level * SIGMA_DATA * lax.rsqrt(variance)
    levels_out[3:4] = 1.0 / level
    levels_out[4:5] = c_in
    even = lax.rem(lax.axis_index("space"), 2) == 0
    c_in = c_in.reshape(1, 1, 128)
    for out, to_right in ((first_out, even), (second_out, jnp.logical_not(even))):
        start = jnp.where(to_right, held - 2, 0)
        out[0:64] = (c_in * noisy_v[pl.ds(start, 2)]).astype(BF16).reshape(64, 128)
        out[64:128] = mean_v[pl.ds(start, 2)].astype(BF16).reshape(64, 128)

    copies[3].wait()
    stem_taps = w_stem_v[...].astype(F32) * 0.5
    for cell in range(4):
        for target in range(2):
            col_tap = cell - target
            if 0 <= col_tap < 3:
                for row_tap in range(3):
                    at = (3 * row_tap + col_tap) * CIN
                    to = cell * CELL + row_tap * CIN
                    stem_f32[to : to + CIN, target * CH : (target + 1) * CH] = stem_taps[at : at + CIN]
    part = levels_out[0:1]
    for number in range(3):
        high = part.astype(BF16).astype(F32)
        for target in range(2):
            to = (target + 1) * CELL + 3 * CIN + number
            stem_f32[to : to + 1, target * CH : (target + 1) * CH] = high
        part = part - high
    stem_out[...] = stem_f32[...].astype(BF16)
    for copy in copies[4:6]:
        copy.wait()
    weights = jnp.transpose(w_out_v[...].astype(F32)).astype(BF16)
    for cell in range(HALF):
        right_out[cell * CH : (cell + 1) * CH] = dot(
            weights, place_v[:, cell * 256 : (cell + 1) * 256]
        ).astype(BF16)
    for copy in copies[6:]:
        copy.wait()
    after = dot(attn_v[...], kept[8][...]).astype(BF16)
    for head in range(HEADS):
        span = slice(head * HEAD_DIM, (head + 1) * HEAD_DIM)
        joint_out[:, head * CH : (head + 1) * CH] = dot(value_v[:, span], after[span]).astype(BF16)


def pack_kernel(counts, chip0, chip1, chip2, chip3, first_in, second_in, second_out, first_out, mix_out, cells):
    held = counts[0]
    chip = lax.axis_index("member") // 2
    for distance, given in zip((0, *DISTANCES), (chip0, chip1, chip2, chip3)):
        member = 2 * jnp.bitwise_xor(chip, distance)
        cells[member] = given[0:8]
        cells[member + 1] = given[8:16]
    for member in range(MEMBERS):
        mix_out[pl.ds(member, SLOTS, stride=MEMBERS)] = cells[member, 0:SLOTS]
    even = lax.rem(lax.axis_index("space"), 2) == 0
    for out, given, to_right in (
        (first_out, first_in, even),
        (second_out, second_in, jnp.logical_not(even)),
    ):
        start = pl.multiple_of(jnp.where(to_right, held - 2, 0) * MEMBERS, MEMBERS)
        out[0:128] = given[0:128]
        mixed = mix_out[pl.ds(start, 16)]
        high = mixed.astype(BF16)
        out[128:144] = high
        out[144:160] = (mixed - high.astype(F32)).astype(BF16)


def interpolate(mixes, count, along):
    pair = mixes[pl.ds(0, count, stride=2)] + pltpu.roll(mixes[pl.ds(1, count, stride=2)], 24, 1)
    high = pair.astype(BF16).astype(F32)
    rows = dot(along[...], jnp.concatenate([high, pair - high], axis=0).astype(BF16))
    high = rows.astype(BF16).astype(F32)
    return high + pltpu.roll(rows - high, 48, 1)


def assemble(operand, state, mean, cond):
    lane = lax.broadcasted_iota(jnp.int32, state.shape, 1)
    left = lane < 64
    operand[0, :, 0:128] = jnp.where(left, state, pltpu.roll(mean, 64, 1)).astype(BF16)
    operand[1, :, 0:128] = jnp.where(left, pltpu.roll(state, 64, 1), mean).astype(BF16)
    one = lane == 104
    operand[1, :, 128:256] = jnp.where(one, 1.0, cond).astype(BF16)
    more = jnp.where(lane < 100, pltpu.roll(state, 32, 1), pltpu.roll(mean, 36, 1))
    operand[0, :, 128:256] = jnp.where(
        lane < 96, cond, jnp.where(lane < 104, more, one.astype(F32))
    ).astype(BF16)


def widen(operand, basis, blocks, wide, stem_in):
    rows = operand.shape[1]
    lane = lax.rem(lax.broadcasted_iota(jnp.int32, (1, 128), 1), CELL)
    above, here = lane < CIN, lane < 2 * CIN
    zero = jnp.zeros((8, 128), F32)
    for number in range(4):
        wide[number, 0:8] = zero
        wide[number, 8 + rows :] = zero
    turn = 0
    for half, (start, stop) in enumerate(((0, LEFT_LANES), (LEFT_LANES, STEM_LANES))):
        given = operand[half]
        for chunk in range(start, stop, 256):
            lanes = min(256, stop - chunk)
            at = chunk - start
            product = dot(given, basis[half, :, at : at + lanes])
            for part in range(0, lanes, 128):
                number = turn % 4
                turn += 1
                wide[number, 8 : 8 + rows] = product[:, part : part + 128]
                to_lane = chunk + part
                for first, to, count in blocks:
                    at_row = 8 + first
                    stem_in[to : to + count, to_lane : to_lane + 128] = jnp.where(
                        above,
                        wide[number, at_row - 1 : at_row - 1 + count],
                        jnp.where(
                            here,
                            wide[number, at_row : at_row + count],
                            wide[number, at_row + 1 : at_row + 1 + count],
                        ),
                    ).astype(BF16)


def stem(stem_in, stem_right, features, store_pooled):
    rows = features.shape[0]
    for block_col in range(4):
        summed = jnp.zeros((rows, CH), F32)
        for cell_pair in range(4):
            number = block_col * 4 + cell_pair
            halves = dot(stem_in[:, number * 128 : number * 128 + 256], stem_right[...])
            for part in range(2):
                half = halves[:, part * CH : (part + 1) * CH]
                feature = (0.5 * half) * (1.0 + jnp.tanh(half))
                lane = number * 256 + part * CH
                features[:, lane : lane + CH] = feature.astype(BF16)
                summed = summed + feature
        store_pooled(block_col, jnp.sum(summed.reshape(rows // 8, 8, CH), axis=1) * (1.0 / 32.0))


def bottleneck(pooled, starts, weights):
    w_down, w_query, w_key, w_joint, w_up = weights
    zeta = silu(dot(pooled.astype(BF16), w_down[...]))
    scale = lax.rsqrt(jnp.mean(zeta * zeta, axis=-1, keepdims=True) + NORM_EPS)
    given = zeta.astype(BF16)
    query = (scale * HEAD_DIM**-0.5 * dot(given, w_query[...])).astype(BF16)
    keyed = (scale * dot(given, w_key[...])).astype(BF16)
    valued = (scale * dot(given, w_joint[...])).astype(BF16)
    raised = dot(given, w_up[...])
    head_of_row = lax.broadcasted_iota(jnp.int32, (HEADS * TOKENS, CH2), 0) // TOKENS
    head_of_channel = lax.broadcasted_iota(jnp.int32, (HEADS * TOKENS, CH2), 1) // HEAD_DIM
    own_head = (head_of_row == head_of_channel).astype(F32).astype(BF16)
    row = lax.broadcasted_iota(jnp.int32, (HEADS * TOKENS, HEADS * TOKENS), 0) // TOKENS
    lane = lax.broadcasted_iota(jnp.int32, (HEADS * TOKENS, HEADS * TOKENS), 1) // TOKENS
    same_head = (row == lane).astype(F32).astype(BF16)
    head_of_lane = lax.broadcasted_iota(jnp.int32, (TOKENS, HEADS * TOKENS), 1) // TOKENS
    lifted = []
    for start in starts:
        rows = slice(start, start + TOKENS)
        keys = jnp.concatenate([keyed[rows]] * HEADS, axis=0) * own_head
        values = jnp.concatenate(
            [valued[rows, head * CH : (head + 1) * CH] for head in range(HEADS)], axis=0
        )
        scores = lax.dot_general(
            query[rows], keys, (((1,), (1,)), ((), ())), preferred_element_type=F32
        )
        top = jnp.zeros_like(scores)
        for head in range(HEADS):
            inside = head_of_lane == head
            largest = jnp.max(jnp.where(inside, scores, -jnp.inf), axis=1, keepdims=True)
            top = jnp.where(inside, largest, top)
        weight = jnp.exp(scores - top)
        weight = (weight / dot(weight.astype(BF16), same_head)).astype(BF16)
        lifted.append(0.5 * (raised[rows] + dot(weight, values)))
    return jnp.concatenate(lifted, axis=0)


def activate(number, sources, first, lifted, active, base):
    half_rows = active.shape[0] // 2
    count = sum(rows for _, _, rows in sources) // 8
    for block_col in range(4):
        raised = lifted[pl.ds(number * TOKENS + first * 4 + block_col, count, stride=4)].reshape(
            count, 1, CH
        )
        done = 0
        for ref, start, rows in sources:
            part = raised[done // 8 : (done + rows) // 8]
            for cell in range(block_col * 8, block_col * 8 + 8):
                given = ref[pl.ds(start, rows), cell * CH : (cell + 1) * CH]
                half = given.astype(F32).reshape(rows // 8, 8, CH) + part
                value = half + half * jnp.tanh(half)
                to = base + done + cell // HALF * half_rows
                lane = cell % HALF * CH
                active[to : to + rows, lane : lane + CH] = value.reshape(rows, CH).astype(BF16)
            done += rows


def predict(left, right, first, last, padded):
    rows = (last - first) * 8
    lane = lax.broadcasted_iota(jnp.int32, (rows, 128), 1)
    for tap in range(3):
        from_left = pltpu.roll(left, (-4 - TAP_LANES * tap) % 256, 1)[:, 0:128]
        from_right = pltpu.roll(right, (60 - TAP_LANES * tap) % 256, 1)[:, 0:128]
        padded[8 : 8 + rows, tap * 128 : (tap + 1) * 128] = jnp.where(
            lane < 68, from_left, 0.0
        ) + jnp.where(lane >= 60, from_right, 0.0)
    zero = jnp.zeros((8, 384), F32)
    padded[0:8] = zero
    padded[8 + rows : 16 + rows] = zero
    field = (
        padded[7 : 7 + rows, 0:128] + padded[8 : 8 + rows, 128:256] + padded[9 : 9 + rows, 256:384]
    )
    row = lax.broadcasted_iota(jnp.int32, (rows, 128), 0) + first * 8
    return field * jnp.minimum(row + 1, DOM - row).astype(F32)


def convolve(plans, group_rows, lifted, active, halves, padded, out_right, total):
    groups = active.shape[0]
    each = len(plans) // groups
    for group in range(groups):
        base = 0
        for number in range(each * group, each * group + each):
            first, stop, sources = plans[number][:3]
            activate(number, sources, first, lifted, active.at[group], base)
            base += (stop - first) * 8
        halves[group] = dot(active[group], out_right[...])
    for group in range(groups):
        base = 0
        for number in range(each * group, each * group + each):
            first, stop, _, to, start, end, counted = plans[number]
            rows = (stop - first) * 8
            field = predict(
                halves[group, base : base + rows],
                halves[group, group_rows + base : group_rows + base + rows],
                first,
                stop,
                padded.at[number % 2],
            )[start:end]
            if counted is not True:
                field = jnp.where(counted, field, 0.0)
            span = pl.ds(to, end - start)
            total[span] = total[span] + field
            base += rows


def inner_plans(numbers, held):
    plans = []
    for patch in (number + 1 for number in numbers):
        start = P_SIZE * patch - M
        plans.append((0, 8, start, start, 0, 64, patch <= held - 2))
    return plans


def own_kernel(
    counts, noisy, mean_field, mixes, along, levels, basis, stem_right, out_right, *refs
):
    weights = refs[:5]
    features, pooled_out, lifted, total = refs[5:9]
    operand, wide, stem_in, pooled, active, halves, padded = refs[9:]
    held = counts[0]
    assemble(
        operand,
        levels[4:5] * noisy[...].reshape(OWN_ROWS, 128),
        mean_field[...].reshape(OWN_ROWS, 128),
        interpolate(mixes, SLOTS * BR, along),
    )
    widen(operand, basis, [(0, 0, OWN_ROWS)], wide, stem_in)

    pooled[0:8] = jnp.zeros((8, CH), F32)
    pooled[8 + OWN_TOKENS :] = jnp.zeros((8, CH), F32)

    def store_pooled(block_col, value):
        pooled[pl.ds(8 + block_col, OWN_ROWS // 8, stride=4)] = value

    stem(stem_in, stem_right, features, store_pooled)
    pooled_out[...] = pooled[8 : 8 + OWN_TOKENS]
    lifted[...] = bottleneck(pooled[...], [16 * patch for patch in range(1, SLOTS - 1)], weights)
    total[...] = jnp.zeros_like(total)
    plans = [
        (first, stop, [(features, start, DOM)], *rest)
        for first, stop, start, *rest in inner_plans(range(EARLY), held)
    ]
    convolve(plans, EARLY * DOM, lifted, active, halves, padded, out_right, total)


def main_kernel(
    counts, sigma_next, noisy, mean_field, second_in, first_in, mix_own, levels, along, basis, stem_right,
    pooled_own, features, lifted_own, total_own, w_down, w_query, w_key, w_joint, w_up, out_right,
    denoised_out, next_out,
    state_rows, mean_rows, mixes, operand, wide, stem_in, ends, pooled, lifted, active, halves,
    padded, total, active_inner, halves_inner,
):
    held = counts[0]
    weights = (w_down, w_query, w_key, w_joint, w_up)
    position = lax.axis_index("space")
    even = lax.rem(position, 2) == 0
    has_left = position > 0
    has_right = position < lax.axis_size("space") - 1
    c_in = levels[4:5].reshape(1, 1, 128)

    state_rows[0, 64:96] = (c_in * noisy[0:1]).reshape(P_SIZE, 128)
    mean_rows[0, 64:96] = mean_field[0]
    state_rows[1, 0:32] = (c_in * noisy[pl.ds(held - 1, 1)]).reshape(P_SIZE, 128)
    mean_rows[1, 0:32] = mean_field[pl.ds(held - 1, 1)].reshape(P_SIZE, 128)
    mixes[16:24] = mix_own[0:8]
    mixes[24:32] = jnp.zeros((8, 128), F32)
    mixes[32:40] = mix_own[pl.ds(pl.multiple_of(8 * held - 8, 8), 8)]
    mixes[56:64] = jnp.zeros((8, 128), F32)

    def take(piece, side, rows_at, mixes_at):
        state_rows[side, rows_at : rows_at + 64] = piece[0:64].astype(F32)
        mean_rows[side, rows_at : rows_at + 64] = piece[64:128].astype(F32)
        mixes[mixes_at : mixes_at + 16] = piece[128:144].astype(F32) + piece[144:160].astype(F32)

    @pl.when(even)
    def _():
        take(second_in, 0, 0, 0)
        take(first_in, 1, 32, 40)

    @pl.when(jnp.logical_not(even))
    def _():
        take(first_in, 0, 0, 0)
        take(second_in, 1, 32, 40)

    assemble(
        operand,
        state_rows[:, 8 : 8 + SIDE_SPAN].reshape(2 * SIDE_SPAN, 128),
        mean_rows[:, 8 : 8 + SIDE_SPAN].reshape(2 * SIDE_SPAN, 128),
        interpolate(mixes, 2 * SIDE_PATCHES * BR, along),
    )
    widen(
        operand, basis, [(8, 0, SIDE_ROWS), (SIDE_SPAN + 8, SIDE_ROWS, SIDE_ROWS)], wide, stem_in
    )

    def store_pooled(block_col, value):
        pooled[pl.ds(block_col, 8, stride=4)] = value[0:8]
        pooled[pl.ds(64 + block_col, 8, stride=4)] = value[8:16]

    stem(stem_in, stem_right, ends, store_pooled)
    pooled[32:48] = pooled_own[8:24]
    pooled[48:64] = pooled_own[pl.ds(pl.multiple_of(16 * held - 24, 8), 16)]

    @pl.when(jnp.logical_not(has_left))
    def _():
        ends[0:48] = jnp.zeros((48, W * CH), BF16)
        pooled[0:24] = jnp.zeros((24, CH), F32)

    @pl.when(jnp.logical_not(has_right))
    def _():
        ends[80:128] = jnp.zeros((48, W * CH), BF16)
        pooled[72:96] = jnp.zeros((24, CH), F32)

    lifted[...] = bottleneck(pooled[...], [0, 16, 48, 64], weights)
    total[...] = total_own[...]
    plans = [
        (first, stop, [(features, start, DOM)], *rest)
        for first, stop, start, *rest in inner_plans(range(EARLY, SLOTS - 2), held)
    ]
    late = lifted_own.at[EARLY * TOKENS :]
    convolve(
        plans, LATE * DOM, late, active_inner, halves_inner, padded.at[0:2], out_right, total
    )
    near = pl.multiple_of(P_SIZE * held - 48, 16)
    last = pl.multiple_of(P_SIZE * held - M, 16)
    plans = [
        (4, 8, [(ends, 32, 32)], 0, 16, 32, has_left),
        (0, 8, [(ends, 32, 32), (features, 16, 32)], 0, 16, 64, True),
        (0, 8, [(features, near, 32), (ends, 64, 32)], near, 0, 48, True),
        (0, 4, [(ends, 64, 32)], last, 0, 16, has_right),
    ]
    convolve(plans, 96, lifted, active, halves, padded.at[2:4], out_right, total)

    slot = lax.broadcasted_iota(jnp.int32, (SLOTS, P_SIZE, 128), 0)
    row = lax.broadcasted_iota(jnp.int32, (SLOTS, P_SIZE, 128), 1)
    norm = jnp.full((SLOTS, P_SIZE, 128), 33, jnp.int32)
    no_left = jnp.logical_and(jnp.logical_not(has_left), jnp.logical_and(slot == 0, row < M))
    no_right = jnp.logical_and(
        jnp.logical_not(has_right), jnp.logical_and(slot == held - 1, row >= M)
    )
    norm = jnp.where(no_left, 17 + row, norm)
    norm = jnp.where(no_right, 48 - row, norm)
    blended = total[...].reshape(SLOTS, P_SIZE, 128) / norm.astype(F32)
    state = noisy[...]
    denoised = levels[1:2].reshape(1, 1, 128) * state + levels[2:3].reshape(1, 1, 128) * blended
    step = sigma_next[0] * levels[3:4].reshape(1, 1, 128) - 1.0
    stepped = state + step * (state - denoised)
    live = slot < held
    denoised_out[...] = jnp.where(live, denoised, 0.0)
    next_out[...] = jnp.where(live, stepped, 0.0)


def shards(
    noisy,
    mean_field,
    coarse,
    counts,
    src,
    widx,
    table,
    sigma,
    sigma_next,
    w_stem,
    noise_embed,
    w_down,
    w_query,
    w_key,
    w_value,
    w_attn_out,
    w_up,
    w_out,
):
    owners = lax.axis_size("space")
    smem = pl.BlockSpec(memory_space=pltpu.SMEM)
    vmem = pl.BlockSpec(memory_space=pltpu.VMEM)
    hbm = pl.BlockSpec(memory_space=pltpu.HBM)
    limit = pltpu.CompilerParams(vmem_limit_bytes=VMEM_LIMIT)

    def in_hbm(*arrays):
        return [pltpu.with_memory_space_constraint(array, pltpu.HBM) for array in arrays]

    def in_vmem(*shapes):
        return [pltpu.VMEM(shape, dtype) for shape, dtype in shapes]

    state = noisy[0]
    mixed = pl.pallas_call(
        mix_kernel,
        out_shape=pltpu.VMEM((8, 128), F32),
        in_specs=[hbm] * 4,
        out_specs=vmem,
        scratch_shapes=[
            pltpu.SMEM((MIX, SLOTS), jnp.int32),
            pltpu.SMEM((MIX, SLOTS), jnp.int32),
            pltpu.SMEM((16,), F32),
            pltpu.VMEM((BLK_DEV, 24), F32),
            pltpu.SemaphoreType.DMA((4,)),
        ],
        compiler_params=limit,
        name="mix",
    )(*in_hbm(src.T, widx.T, table, coarse))
    partners = lax.ppermute(mixed, "member", [(i, i ^ 1) for i in range(MEMBERS)])
    merged = pl.pallas_call(
        merge_kernel,
        out_shape=pltpu.VMEM((16, 128), F32),
        in_specs=[vmem] * 2,
        out_specs=vmem,
        compiler_params=limit,
        name="merge",
    )(mixed, partners)
    chips = [merged] + [
        lax.ppermute(merged, "member", [(i, i ^ (2 * distance)) for i in range(MEMBERS)])
        for distance in DISTANCES
    ]

    basis, along, along_side, place = (jnp.asarray(array) for array in tables())
    loaded = [state, mean_field, basis, along, along_side]
    loaded += [w_down, w_query, w_key, w_up]
    prepared = pl.pallas_call(
        prepare_kernel,
        out_shape=in_vmem(*((array.shape, array.dtype) for array in loaded))
        + in_vmem(
            ((PIECE, 128), BF16),
            ((PIECE, 128), BF16),
            ((8, 128), F32),
            ((CH2, CH2), BF16),
            ((HALF_LANES, 256), BF16),
            ((CH2, HEADS * CH), BF16),
        ),
        in_specs=[smem] * 2 + [hbm] * (6 + len(loaded)),
        out_specs=[vmem] * (len(loaded) + 6),
        scratch_shapes=[
            pltpu.VMEM(w_value.shape, BF16),
            pltpu.VMEM(w_attn_out.shape, BF16),
            pltpu.VMEM(noise_embed.shape, F32),
            pltpu.VMEM(w_stem.shape, BF16),
            pltpu.VMEM(w_out.T.shape, BF16),
            pltpu.VMEM(place.shape, BF16),
            pltpu.VMEM((256, 256), F32),
            pltpu.SemaphoreType.DMA((6 + len(loaded),)),
        ],
        compiler_params=limit,
        cost_estimate=pl.CostEstimate(flops=10**9, bytes_accessed=8 * 10**6, transcendentals=0),
        name="prepare",
    )(counts, sigma, *in_hbm(noise_embed, w_stem, w_out.T, place, w_value, w_attn_out, *loaded))
    state, mean_field, basis, along, along_side = prepared[:5]
    first, second, levels, stem_right, out_right, w_joint = prepared[9:]
    weights = [*prepared[5:8], w_joint, prepared[8]]

    second, first, mix_own = pl.pallas_call(
        pack_kernel,
        out_shape=in_vmem(
            ((PIECE, 128), BF16), ((PIECE, 128), BF16), ((SLOTS * MEMBERS, 128), F32)
        ),
        in_specs=[smem] + [vmem] * 6,
        out_specs=[vmem] * 3,
        scratch_shapes=[pltpu.VMEM((MEMBERS, 8, 128), F32)],
        compiler_params=limit,
        name="pack",
    )(counts, *chips, first, second)
    pairs = [(i, i ^ 1) for i in range(owners)]
    others = []
    for i in range(1, owners - 1, 2):
        others += [(i, i + 1), (i + 1, i)]
    second = lax.ppermute(second, "space", others)
    first = lax.ppermute(first, "space", pairs)

    features, pooled, lifted, total = pl.pallas_call(
        own_kernel,
        out_shape=in_vmem(
            ((OWN_ROWS, W * CH), BF16),
            ((OWN_TOKENS, CH), F32),
            ((4 * TOKENS, CH), F32),
            ((OWN_ROWS, 128), F32),
        ),
        in_specs=[smem] + [vmem] * 13,
        out_specs=[vmem] * 4,
        scratch_shapes=[
            pltpu.VMEM((2, OWN_ROWS, 256), BF16),
            pltpu.VMEM((4, OWN_ROWS + 16, 128), F32),
            pltpu.VMEM((OWN_ROWS, STEM_LANES), BF16),
            pltpu.VMEM((OWN_TOKENS + 16, CH), F32),
            pltpu.VMEM((1, 2 * EARLY * DOM, HALF_LANES), BF16),
            pltpu.VMEM((1, 2 * EARLY * DOM, 256), F32),
            pltpu.VMEM((2, 80, 384), F32),
        ],
        compiler_params=limit,
        cost_estimate=pl.CostEstimate(flops=10**9, bytes_accessed=10**7, transcendentals=2 * 10**6),
        name="own",
    )(
        counts, state, mean_field, mix_own, along, levels, basis, stem_right, out_right, *weights
    )

    denoised, stepped = pl.pallas_call(
        main_kernel,
        out_shape=(
            jax.ShapeDtypeStruct((SLOTS, P_SIZE, 128), F32),
            jax.ShapeDtypeStruct((SLOTS, P_SIZE, 128), F32),
        ),
        in_specs=[smem] * 2 + [vmem] * 19,
        out_specs=(vmem, vmem),
        scratch_shapes=[
            pltpu.VMEM((2, 96, 128), F32),
            pltpu.VMEM((2, 96, 128), F32),
            pltpu.VMEM((64, 128), F32),
            pltpu.VMEM((2, 2 * SIDE_SPAN, 256), BF16),
            pltpu.VMEM((4, 2 * SIDE_SPAN + 16, 128), F32),
            pltpu.VMEM((2 * SIDE_ROWS, STEM_LANES), BF16),
            pltpu.VMEM((2 * SIDE_ROWS, W * CH), BF16),
            pltpu.VMEM((96, CH), F32),
            pltpu.VMEM((4 * TOKENS, CH), F32),
            pltpu.VMEM((2, 2 * 96, HALF_LANES), BF16),
            pltpu.VMEM((2, 2 * 96, 256), F32),
            pltpu.VMEM((4, 80, 384), F32),
            pltpu.VMEM((OWN_ROWS, 128), F32),
            pltpu.VMEM((1, 2 * LATE * DOM, HALF_LANES), BF16),
            pltpu.VMEM((1, 2 * LATE * DOM, 256), F32),
        ],
        compiler_params=limit,
        cost_estimate=pl.CostEstimate(flops=10**9, bytes_accessed=10**7, transcendentals=2 * 10**6),
        name="main",
    )(
        counts, sigma_next, state, mean_field, second, first, mix_own, levels, along_side, basis, stem_right,
        pooled, features, lifted, total, *weights, out_right,
    )
    return denoised[None], stepped[None]


def solution(mesh):
    placed = (
        P("member", "space", None, None),
        P("space", None, None),
        P("space", "member"),
        P("space"),
        P("space", None),
        P("space", None),
        P(),
        P("member"),
        P("member"),
        P(),
        P(),
        P(),
        P(),
        P(),
        P(),
        P(),
        P(),
        P(),
    )
    return jax.shard_map(
        shards,
        mesh=mesh,
        in_specs=placed,
        out_specs=(P("member", "space", None, None), P("member", "space", None, None)),
        check_vma=False,
    )
```

```python
import functools

import jax
import jax.numpy as jnp
import numpy as np
from jax import lax
from jax.experimental import pallas as pl
from jax.experimental.pallas import tpu as pltpu
from jax.sharding import PartitionSpec as P

VARS = 4
CCH = 12
CIN = 20
CH = 128
CH2 = 256
HEADS = 4
HEAD_DIM = 64
P_SIZE = 32
M = 16
W = 32
SLOTS = 6
FACTOR = 8
BLK_DEV = 8
MIX = 4
DOM = 64
TOKENS = 32
BR = 4
BW = 4
MEMBERS = 8
DISTANCES = (1, 3, 2)

SIGMA_DATA = 0.5
NORM_EPS = 1e-06

F32 = jnp.float32
BF16 = jnp.bfloat16

CELL = 64
STEM_LANES = (W + 2) * CELL
OWN_ROWS = SLOTS * P_SIZE
SIDE_ROWS = 64
OWN_TOKENS = OWN_ROWS // 8 * 4
SIDE_PATCHES = 4
PIECE = 160
LEFT_LANES = 1152
SIDE_SPAN = 80
HALF = W // 2
HALF_LANES = HALF * CH
TAP_LANES = (HALF + 2) * VARS
EARLY = 2
LATE = SLOTS - 2 - EARLY
VMEM_LIMIT = 24 * 1024 * 1024


def interp_matrix(fine_count, coarse_count):
    position = (np.arange(fine_count) + 0.5) / FACTOR - 0.5
    position = np.clip(position, 0.0, coarse_count - 1.0)
    return np.maximum(0.0, 1.0 - np.abs(position[:, None] - np.arange(coarse_count)[None, :]))


def along_rows(sources, patches):
    row_map = interp_matrix(P_SIZE, BR)
    along = np.zeros((len(sources), 2, patches, BR), np.float32)
    for row, source in enumerate(sources):
        along[row, :, source // P_SIZE] = row_map[source % P_SIZE][None]
    return along


@functools.cache
def tables():
    col_map = interp_matrix(W, BW)
    noisy, mean = (np.zeros((W, VARS, W + 2, CELL), np.float32) for _ in range(2))
    across = np.zeros((2, BW, CCH, W + 2, CELL), np.float32)
    for tap in range(3):
        at = tap * CIN
        for col in range(W):
            for var in range(VARS):
                noisy[col, var, col + 1, at + var] = 1.0
                mean[col, var, col + 1, at + VARS + var] = 1.0
        for channel in range(CCH):
            across[:, :, channel, 1 : W + 1, at + 2 * VARS + channel] = col_map.T[None]
    basis = np.zeros((2, 256, LEFT_LANES), np.float32)
    for half, lanes in enumerate((slice(0, LEFT_LANES), slice(LEFT_LANES, STEM_LANES))):
        count = lanes.stop - lanes.start
        cells = slice(HALF * half, HALF * half + HALF)
        basis[half, 0:64, :count] = noisy[cells].reshape(64, STEM_LANES)[:, lanes]
        basis[half, 64:128, :count] = mean[cells].reshape(64, STEM_LANES)[:, lanes]
        basis[half, 128:224, :count] = across.reshape(96, STEM_LANES)[:, lanes]
        basis[half, 232, :count] = np.tile(np.arange(CELL) >= 3 * CIN, W + 2)[lanes]
    basis[0, 224:228] = noisy[HALF].reshape(4, STEM_LANES)[:, :LEFT_LANES]
    basis[0, 228:232] = mean[HALF].reshape(4, STEM_LANES)[:, :LEFT_LANES]
    along = along_rows(range(OWN_ROWS), SLOTS).reshape(OWN_ROWS, 2 * SLOTS * BR)
    side = along_rows(range(8, 8 + SIDE_SPAN), SIDE_PATCHES)
    along_side = np.zeros((2, SIDE_SPAN, 2, 2, SIDE_PATCHES, BR), np.float32)
    for number in range(2):
        along_side[number, :, :, number] = side
    along_side = along_side.reshape(2 * SIDE_SPAN, 4 * SIDE_PATCHES * BR)
    place = np.zeros((3, 3, VARS, HALF, 256), np.float32)
    for cell in range(HALF):
        for row_tap in range(3):
            for col_tap in range(3):
                for var in range(VARS):
                    lane = row_tap * TAP_LANES + (cell + 2 - col_tap) * VARS + var
                    place[row_tap, col_tap, var, cell, lane] = 1.0
    place = place.reshape(36, HALF * 256)
    return tuple(array.astype(jnp.bfloat16) for array in (basis, along, along_side, place))


def silu(value):
    half = 0.5 * value
    return half + half * jnp.tanh(half)


def dot(left, right):
    return jnp.dot(left, right, preferred_element_type=F32)


def fetch(sems, pairs):
    copies = [pltpu.make_async_copy(a, b, sems.at[i]) for i, (a, b) in enumerate(pairs)]
    for copy in copies:
        copy.start()
    return copies


def mix_kernel(src, widx, table, coarse, mixed_out, src_s, widx_s, table_s, blocks, sems):
    for copy in fetch(sems, [(src, src_s), (widx, widx_s), (table, table_s), (coarse, blocks)]):
        copy.wait()
    mixed_out[...] = jnp.zeros_like(mixed_out)
    for slot in range(SLOTS):
        total = jnp.zeros((1, 24), F32)
        for k in range(MIX):
            total = total + table_s[widx_s[k, slot]] * blocks[pl.ds(src_s[k, slot], 1)]
        mixed_out[slot : slot + 1, 0:24] = total


def merge_kernel(mixed, partners, merged_out):
    core = lax.rem(lax.axis_index("member"), 2)
    merged_out[pl.ds(pl.multiple_of(8 * core, 8), 8)] = mixed[...]
    merged_out[pl.ds(pl.multiple_of(8 - 8 * core, 8), 8)] = partners[...]


def prepare_kernel(counts, sigma, noise_embed, w_stem, w_out, place, w_value, w_attn_out, *refs):
    loaded, kept, rest = refs[:9], refs[9:18], refs[18:]
    (
        first_out, second_out, levels_out, stem_out, right_out, joint_out,
        value_v, attn_v, embed_v, w_stem_v, w_out_v, place_v, stem_f32, sems,
    ) = rest
    noisy_v, mean_v = kept[:2]
    copies = fetch(
        sems,
        [
            (noise_embed, embed_v),
            (loaded[0], noisy_v),
            (loaded[1], mean_v),
            (w_stem, w_stem_v),
            (w_out, w_out_v),
            (place, place_v),
            (w_value, value_v),
            (w_attn_out, attn_v),
        ]
        + list(zip(loaded[2:], kept[2:])),
    )
    stem_f32[...] = jnp.zeros_like(stem_f32)
    for copy in copies[0:3]:
        copy.wait()
    held = counts[0]
    level = jnp.full((1, 128), sigma[0], F32)
    variance = level * level + SIGMA_DATA * SIGMA_DATA
    c_in = lax.rsqrt(variance)
    levels_out[0:1] = jnp.log(level) * 0.125 * embed_v[...].reshape(1, CH)
    levels_out[1:2] = SIGMA_DATA * SIGMA_DATA / variance
    levels_out[2:3] = level * SIGMA_DATA * lax.rsqrt(variance)
    levels_out[3:4] = 1.0 / level
    levels_out[4:5] = c_in
    even = lax.rem(lax.axis_index("space"), 2) == 0
    c_in = c_in.reshape(1, 1, 128)
    for out, to_right in ((first_out, even), (second_out, jnp.logical_not(even))):
        start = jnp.where(to_right, held - 2, 0)
        out[0:64] = (c_in * noisy_v[pl.ds(start, 2)]).astype(BF16).reshape(64, 128)
        out[64:128] = mean_v[pl.ds(start, 2)].astype(BF16).reshape(64, 128)

    copies[3].wait()
    stem_taps = w_stem_v[...].astype(F32) * 0.5
    for cell in range(4):
        for target in range(2):
            col_tap = cell - target
            if 0 <= col_tap < 3:
                for row_tap in range(3):
                    at = (3 * row_tap + col_tap) * CIN
                    to = cell * CELL + row_tap * CIN
                    stem_f32[to : to + CIN, target * CH : (target + 1) * CH] = stem_taps[at : at + CIN]
    part = levels_out[0:1]
    for number in range(3):
        high = part.astype(BF16).astype(F32)
        for target in range(2):
            to = (target + 1) * CELL + 3 * CIN + number
            stem_f32[to : to + 1, target * CH : (target + 1) * CH] = high
        part = part - high
    stem_out[...] = stem_f32[...].astype(BF16)
    for copy in copies[4:6]:
        copy.wait()
    weights = jnp.transpose(w_out_v[...].astype(F32)).astype(BF16)
    for cell in range(HALF):
        right_out[cell * CH : (cell + 1) * CH] = dot(
            weights, place_v[:, cell * 256 : (cell + 1) * 256]
        ).astype(BF16)
    for copy in copies[6:]:
        copy.wait()
    after = dot(attn_v[...], kept[8][...]).astype(BF16)
    for head in range(HEADS):
        span = slice(head * HEAD_DIM, (head + 1) * HEAD_DIM)
        joint_out[:, head * CH : (head + 1) * CH] = dot(value_v[:, span], after[span]).astype(BF16)


def pack_kernel(counts, chip0, chip1, chip2, chip3, first_in, second_in, second_out, first_out, mix_out, cells):
    held = counts[0]
    chip = lax.axis_index("member") // 2
    for distance, given in zip((0, *DISTANCES), (chip0, chip1, chip2, chip3)):
        member = 2 * jnp.bitwise_xor(chip, distance)
        cells[member] = given[0:8]
        cells[member + 1] = given[8:16]
    for member in range(MEMBERS):
        mix_out[pl.ds(member, SLOTS, stride=MEMBERS)] = cells[member, 0:SLOTS]
    even = lax.rem(lax.axis_index("space"), 2) == 0
    for out, given, to_right in (
        (first_out, first_in, even),
        (second_out, second_in, jnp.logical_not(even)),
    ):
        start = pl.multiple_of(jnp.where(to_right, held - 2, 0) * MEMBERS, MEMBERS)
        out[0:128] = given[0:128]
        mixed = mix_out[pl.ds(start, 16)]
        high = mixed.astype(BF16)
        out[128:144] = high
        out[144:160] = (mixed - high.astype(F32)).astype(BF16)


def interpolate(mixes, count, along):
    pair = mixes[pl.ds(0, count, stride=2)] + pltpu.roll(mixes[pl.ds(1, count, stride=2)], 24, 1)
    high = pair.astype(BF16).astype(F32)
    rows = dot(along[...], jnp.concatenate([high, pair - high], axis=0).astype(BF16))
    high = rows.astype(BF16).astype(F32)
    return high + pltpu.roll(rows - high, 48, 1)


def assemble(operand, state, mean, cond):
    lane = lax.broadcasted_iota(jnp.int32, state.shape, 1)
    left = lane < 64
    operand[0, :, 0:128] = jnp.where(left, state, pltpu.roll(mean, 64, 1)).astype(BF16)
    operand[1, :, 0:128] = jnp.where(left, pltpu.roll(state, 64, 1), mean).astype(BF16)
    one = lane == 104
    operand[1, :, 128:256] = jnp.where(one, 1.0, cond).astype(BF16)
    more = jnp.where(lane < 100, pltpu.roll(state, 32, 1), pltpu.roll(mean, 36, 1))
    operand[0, :, 128:256] = jnp.where(
        lane < 96, cond, jnp.where(lane < 104, more, one.astype(F32))
    ).astype(BF16)


def widen(operand, basis, blocks, wide, stem_in):
    rows = operand.shape[1]
    lane = lax.rem(lax.broadcasted_iota(jnp.int32, (1, 128), 1), CELL)
    above, here = lane < CIN, lane < 2 * CIN
    zero = jnp.zeros((8, 128), F32)
    for number in range(4):
        wide[number, 0:8] = zero
        wide[number, 8 + rows :] = zero
    turn = 0
    for half, (start, stop) in enumerate(((0, LEFT_LANES), (LEFT_LANES, STEM_LANES))):
        given = operand[half]
        for chunk in range(start, stop, 256):
            lanes = min(256, stop - chunk)
            at = chunk - start
            product = dot(given, basis[half, :, at : at + lanes])
            for part in range(0, lanes, 128):
                number = turn % 4
                turn += 1
                wide[number, 8 : 8 + rows] = product[:, part : part + 128]
                to_lane = chunk + part
                for first, to, count in blocks:
                    at_row = 8 + first
                    stem_in[to : to + count, to_lane : to_lane + 128] = jnp.where(
                        above,
                        wide[number, at_row - 1 : at_row - 1 + count],
                        jnp.where(
                            here,
                            wide[number, at_row : at_row + count],
                            wide[number, at_row + 1 : at_row + 1 + count],
                        ),
                    ).astype(BF16)


def stem(stem_in, stem_right, features, store_pooled):
    rows = features.shape[0]
    for block_col in range(4):
        summed = jnp.zeros((rows, CH), F32)
        for cell_pair in range(4):
            number = block_col * 4 + cell_pair
            halves = dot(stem_in[:, number * 128 : number * 128 + 256], stem_right[...])
            for part in range(2):
                half = halves[:, part * CH : (part + 1) * CH]
                feature = (0.5 * half) * (1.0 + jnp.tanh(half))
                lane = number * 256 + part * CH
                features[:, lane : lane + CH] = feature.astype(BF16)
                summed = summed + feature
        store_pooled(block_col, jnp.sum(summed.reshape(rows // 8, 8, CH), axis=1) * (1.0 / 32.0))


def bottleneck(pooled, starts, weights):
    *_, lifted = bottleneck_steps(pooled, starts, weights)
    return lifted


def bottleneck_steps(pooled, starts, weights):
    w_down, w_query, w_key, w_joint, w_up = weights
    zeta = silu(dot(pooled.astype(BF16), w_down[...]))
    scale = lax.rsqrt(jnp.mean(zeta * zeta, axis=-1, keepdims=True) + NORM_EPS)
    given = zeta.astype(BF16)
    yield None
    query = (scale * HEAD_DIM**-0.5 * dot(given, w_query[...])).astype(BF16)
    keyed = (scale * dot(given, w_key[...])).astype(BF16)
    valued = (scale * dot(given, w_joint[...])).astype(BF16)
    raised = dot(given, w_up[...])
    head_of_row = lax.broadcasted_iota(jnp.int32, (HEADS * TOKENS, CH2), 0) // TOKENS
    head_of_channel = lax.broadcasted_iota(jnp.int32, (HEADS * TOKENS, CH2), 1) // HEAD_DIM
    own_head = (head_of_row == head_of_channel).astype(F32).astype(BF16)
    row = lax.broadcasted_iota(jnp.int32, (HEADS * TOKENS, HEADS * TOKENS), 0) // TOKENS
    lane = lax.broadcasted_iota(jnp.int32, (HEADS * TOKENS, HEADS * TOKENS), 1) // TOKENS
    same_head = (row == lane).astype(F32).astype(BF16)
    head_of_lane = lax.broadcasted_iota(jnp.int32, (TOKENS, HEADS * TOKENS), 1) // TOKENS
    yield None
    scores = []
    for start in starts:
        rows = slice(start, start + TOKENS)
        keys = jnp.concatenate([keyed[rows]] * HEADS, axis=0) * own_head
        scores.append(
            lax.dot_general(
                query[rows], keys, (((1,), (1,)), ((), ())), preferred_element_type=F32
            )
        )
    yield None
    weighted = []
    for score in scores:
        top = jnp.zeros_like(score)
        for head in range(HEADS):
            inside = head_of_lane == head
            largest = jnp.max(jnp.where(inside, score, -jnp.inf), axis=1, keepdims=True)
            top = jnp.where(inside, largest, top)
        weighted.append(jnp.exp(score - top))
    yield None
    lifted = []
    for start, weight in zip(starts, weighted):
        rows = slice(start, start + TOKENS)
        values = jnp.concatenate(
            [valued[rows, head * CH : (head + 1) * CH] for head in range(HEADS)], axis=0
        )
        weight = (weight / dot(weight.astype(BF16), same_head)).astype(BF16)
        lifted.append(0.5 * (raised[rows] + dot(weight, values)))
    yield jnp.concatenate(lifted, axis=0)


def activate(number, sources, first, lifted, active, base, block_cols=range(4)):
    half_rows = active.shape[0] // 2
    count = sum(rows for _, _, rows in sources) // 8
    for block_col in block_cols:
        raised = lifted[pl.ds(number * TOKENS + first * 4 + block_col, count, stride=4)].reshape(
            count, 1, CH
        )
        done = 0
        for ref, start, rows in sources:
            part = raised[done // 8 : (done + rows) // 8]
            for cell in range(block_col * 8, block_col * 8 + 8):
                given = ref[pl.ds(start, rows), cell * CH : (cell + 1) * CH]
                half = given.astype(F32).reshape(rows // 8, 8, CH) + part
                value = half + half * jnp.tanh(half)
                to = base + done + cell // HALF * half_rows
                lane = cell % HALF * CH
                active[to : to + rows, lane : lane + CH] = value.reshape(rows, CH).astype(BF16)
            done += rows


def predict(left, right, first, last, padded):
    rows = (last - first) * 8
    lane = lax.broadcasted_iota(jnp.int32, (rows, 128), 1)
    for tap in range(3):
        from_left = pltpu.roll(left, (-4 - TAP_LANES * tap) % 256, 1)[:, 0:128]
        from_right = pltpu.roll(right, (60 - TAP_LANES * tap) % 256, 1)[:, 0:128]
        padded[8 : 8 + rows, tap * 128 : (tap + 1) * 128] = jnp.where(
            lane < 68, from_left, 0.0
        ) + jnp.where(lane >= 60, from_right, 0.0)
    zero = jnp.zeros((8, 384), F32)
    padded[0:8] = zero
    padded[8 + rows : 16 + rows] = zero
    field = (
        padded[7 : 7 + rows, 0:128] + padded[8 : 8 + rows, 128:256] + padded[9 : 9 + rows, 256:384]
    )
    row = lax.broadcasted_iota(jnp.int32, (rows, 128), 0) + first * 8
    return field * jnp.minimum(row + 1, DOM - row).astype(F32)


def convolve(plans, group_rows, lifted, active, halves, padded, out_right, total, ready=False):
    groups = active.shape[0]
    each = len(plans) // groups
    for group in range(groups):
        base = 0
        for number in range(each * group, each * group + each):
            first, stop, sources = plans[number][:3]
            if not ready:
                activate(number, sources, first, lifted, active.at[group], base)
            base += (stop - first) * 8
        halves[group] = dot(active[group], out_right[...])
    for group in range(groups):
        base = 0
        for number in range(each * group, each * group + each):
            first, stop, _, to, start, end, counted = plans[number]
            rows = (stop - first) * 8
            field = predict(
                halves[group, base : base + rows],
                halves[group, group_rows + base : group_rows + base + rows],
                first,
                stop,
                padded.at[number % 2],
            )[start:end]
            if counted is not True:
                field = jnp.where(counted, field, 0.0)
            span = pl.ds(to, end - start)
            total[span] = total[span] + field
            base += rows


def inner_plans(numbers, held):
    plans = []
    for patch in (number + 1 for number in numbers):
        start = P_SIZE * patch - M
        plans.append((0, 8, start, start, 0, 64, patch <= held - 2))
    return plans


def own_kernel(
    counts, noisy, mean_field, mixes, along, levels, basis, stem_right, out_right, *refs
):
    weights = refs[:5]
    features, pooled_out, lifted, total = refs[5:9]
    operand, wide, stem_in, pooled, active, halves, padded = refs[9:]
    held = counts[0]
    assemble(
        operand,
        levels[4:5] * noisy[...].reshape(OWN_ROWS, 128),
        mean_field[...].reshape(OWN_ROWS, 128),
        interpolate(mixes, SLOTS * BR, along),
    )
    widen(operand, basis, [(0, 0, OWN_ROWS)], wide, stem_in)

    pooled[0:8] = jnp.zeros((8, CH), F32)
    pooled[8 + OWN_TOKENS :] = jnp.zeros((8, CH), F32)

    def store_pooled(block_col, value):
        pooled[pl.ds(8 + block_col, OWN_ROWS // 8, stride=4)] = value

    stem(stem_in, stem_right, features, store_pooled)
    pooled_out[...] = pooled[8 : 8 + OWN_TOKENS]
    lifted[...] = bottleneck(pooled[...], [16 * patch for patch in range(1, SLOTS - 1)], weights)
    total[...] = jnp.zeros_like(total)
    plans = [
        (first, stop, [(features, start, DOM)], *rest)
        for first, stop, start, *rest in inner_plans(range(EARLY), held)
    ]
    convolve(plans, EARLY * DOM, lifted, active, halves, padded, out_right, total)


def main_kernel(
    counts, sigma_next, noisy, mean_field, second_in, first_in, mix_own, levels, along, basis, stem_right,
    pooled_own, features, lifted_own, total_own, w_down, w_query, w_key, w_joint, w_up, out_right,
    denoised_out, next_out,
    state_rows, mean_rows, mixes, operand, wide, stem_in, ends, pooled, lifted, active, halves,
    padded, total, active_inner, halves_inner,
):
    held = counts[0]
    weights = (w_down, w_query, w_key, w_joint, w_up)
    position = lax.axis_index("space")
    even = lax.rem(position, 2) == 0
    has_left = position > 0
    has_right = position < lax.axis_size("space") - 1
    c_in = levels[4:5].reshape(1, 1, 128)

    state_rows[0, 64:96] = (c_in * noisy[0:1]).reshape(P_SIZE, 128)
    mean_rows[0, 64:96] = mean_field[0]
    state_rows[1, 0:32] = (c_in * noisy[pl.ds(held - 1, 1)]).reshape(P_SIZE, 128)
    mean_rows[1, 0:32] = mean_field[pl.ds(held - 1, 1)].reshape(P_SIZE, 128)
    mixes[16:24] = mix_own[0:8]
    mixes[24:32] = jnp.zeros((8, 128), F32)
    mixes[32:40] = mix_own[pl.ds(pl.multiple_of(8 * held - 8, 8), 8)]
    mixes[56:64] = jnp.zeros((8, 128), F32)

    def take(piece, side, rows_at, mixes_at):
        state_rows[side, rows_at : rows_at + 64] = piece[0:64].astype(F32)
        mean_rows[side, rows_at : rows_at + 64] = piece[64:128].astype(F32)
        mixes[mixes_at : mixes_at + 16] = piece[128:144].astype(F32) + piece[144:160].astype(F32)

    @pl.when(even)
    def _():
        take(second_in, 0, 0, 0)
        take(first_in, 1, 32, 40)

    @pl.when(jnp.logical_not(even))
    def _():
        take(first_in, 0, 0, 0)
        take(second_in, 1, 32, 40)

    assemble(
        operand,
        state_rows[:, 8 : 8 + SIDE_SPAN].reshape(2 * SIDE_SPAN, 128),
        mean_rows[:, 8 : 8 + SIDE_SPAN].reshape(2 * SIDE_SPAN, 128),
        interpolate(mixes, 2 * SIDE_PATCHES * BR, along),
    )
    widen(
        operand, basis, [(8, 0, SIDE_ROWS), (SIDE_SPAN + 8, SIDE_ROWS, SIDE_ROWS)], wide, stem_in
    )

    def store_pooled(block_col, value):
        pooled[pl.ds(block_col, 8, stride=4)] = value[0:8]
        pooled[pl.ds(64 + block_col, 8, stride=4)] = value[8:16]

    stem(stem_in, stem_right, ends, store_pooled)
    pooled[32:48] = pooled_own[8:24]
    pooled[48:64] = pooled_own[pl.ds(pl.multiple_of(16 * held - 24, 8), 16)]

    @pl.when(jnp.logical_not(has_left))
    def _():
        ends[0:48] = jnp.zeros((48, W * CH), BF16)
        pooled[0:24] = jnp.zeros((24, CH), F32)

    @pl.when(jnp.logical_not(has_right))
    def _():
        ends[80:128] = jnp.zeros((48, W * CH), BF16)
        pooled[72:96] = jnp.zeros((24, CH), F32)

    plans = [
        (first, stop, [(features, start, DOM)], *rest)
        for first, stop, start, *rest in inner_plans(range(EARLY, SLOTS - 2), held)
    ]
    late = lifted_own.at[EARLY * TOKENS :]
    parts = [(number, block_col) for number in range(LATE) for block_col in range(4)]
    for done in bottleneck_steps(pooled[...], [0, 16, 48, 64], weights):
        for number, block_col in parts[:2]:
            activate(
                number, plans[number][2], 0, late, active_inner.at[0], number * DOM, [block_col]
            )
        parts = parts[2:]
    lifted[...] = done
    total[...] = total_own[...]
    convolve(
        plans, LATE * DOM, late, active_inner, halves_inner, padded.at[0:2], out_right, total, True
    )
    near = pl.multiple_of(P_SIZE * held - 48, 16)
    last = pl.multiple_of(P_SIZE * held - M, 16)
    plans = [
        (4, 8, [(ends, 32, 32)], 0, 16, 32, has_left),
        (0, 8, [(ends, 32, 32), (features, 16, 32)], 0, 16, 64, True),
        (0, 8, [(features, near, 32), (ends, 64, 32)], near, 0, 48, True),
        (0, 4, [(ends, 64, 32)], last, 0, 16, has_right),
    ]
    convolve(plans, 96, lifted, active, halves, padded.at[2:4], out_right, total)

    slot = lax.broadcasted_iota(jnp.int32, (SLOTS, P_SIZE, 128), 0)
    row = lax.broadcasted_iota(jnp.int32, (SLOTS, P_SIZE, 128), 1)
    norm = jnp.full((SLOTS, P_SIZE, 128), 33, jnp.int32)
    no_left = jnp.logical_and(jnp.logical_not(has_left), jnp.logical_and(slot == 0, row < M))
    no_right = jnp.logical_and(
        jnp.logical_not(has_right), jnp.logical_and(slot == held - 1, row >= M)
    )
    norm = jnp.where(no_left, 17 + row, norm)
    norm = jnp.where(no_right, 48 - row, norm)
    blended = total[...].reshape(SLOTS, P_SIZE, 128) / norm.astype(F32)
    state = noisy[...]
    denoised = levels[1:2].reshape(1, 1, 128) * state + levels[2:3].reshape(1, 1, 128) * blended
    step = sigma_next[0] * levels[3:4].reshape(1, 1, 128) - 1.0
    stepped = state + step * (state - denoised)
    live = slot < held
    denoised_out[...] = jnp.where(live, denoised, 0.0)
    next_out[...] = jnp.where(live, stepped, 0.0)


def shards(
    noisy,
    mean_field,
    coarse,
    counts,
    src,
    widx,
    table,
    sigma,
    sigma_next,
    w_stem,
    noise_embed,
    w_down,
    w_query,
    w_key,
    w_value,
    w_attn_out,
    w_up,
    w_out,
):
    owners = lax.axis_size("space")
    smem = pl.BlockSpec(memory_space=pltpu.SMEM)
    vmem = pl.BlockSpec(memory_space=pltpu.VMEM)
    hbm = pl.BlockSpec(memory_space=pltpu.HBM)
    limit = pltpu.CompilerParams(vmem_limit_bytes=VMEM_LIMIT)

    def in_hbm(*arrays):
        return [pltpu.with_memory_space_constraint(array, pltpu.HBM) for array in arrays]

    def in_vmem(*shapes):
        return [pltpu.VMEM(shape, dtype) for shape, dtype in shapes]

    state = noisy[0]
    mixed = pl.pallas_call(
        mix_kernel,
        out_shape=pltpu.VMEM((8, 128), F32),
        in_specs=[hbm] * 4,
        out_specs=vmem,
        scratch_shapes=[
            pltpu.SMEM((MIX, SLOTS), jnp.int32),
            pltpu.SMEM((MIX, SLOTS), jnp.int32),
            pltpu.SMEM((16,), F32),
            pltpu.VMEM((BLK_DEV, 24), F32),
            pltpu.SemaphoreType.DMA((4,)),
        ],
        compiler_params=limit,
        name="mix",
    )(*in_hbm(src.T, widx.T, table, coarse))
    partners = lax.ppermute(mixed, "member", [(i, i ^ 1) for i in range(MEMBERS)])
    merged = pl.pallas_call(
        merge_kernel,
        out_shape=pltpu.VMEM((16, 128), F32),
        in_specs=[vmem] * 2,
        out_specs=vmem,
        compiler_params=limit,
        name="merge",
    )(mixed, partners)
    chips = [merged] + [
        lax.ppermute(merged, "member", [(i, i ^ (2 * distance)) for i in range(MEMBERS)])
        for distance in DISTANCES
    ]

    basis, along, along_side, place = (jnp.asarray(array) for array in tables())
    loaded = [state, mean_field, basis, along, along_side]
    loaded += [w_down, w_query, w_key, w_up]
    prepared = pl.pallas_call(
        prepare_kernel,
        out_shape=in_vmem(*((array.shape, array.dtype) for array in loaded))
        + in_vmem(
            ((PIECE, 128), BF16),
            ((PIECE, 128), BF16),
            ((8, 128), F32),
            ((CH2, CH2), BF16),
            ((HALF_LANES, 256), BF16),
            ((CH2, HEADS * CH), BF16),
        ),
        in_specs=[smem] * 2 + [hbm] * (6 + len(loaded)),
        out_specs=[vmem] * (len(loaded) + 6),
        scratch_shapes=[
            pltpu.VMEM(w_value.shape, BF16),
            pltpu.VMEM(w_attn_out.shape, BF16),
            pltpu.VMEM(noise_embed.shape, F32),
            pltpu.VMEM(w_stem.shape, BF16),
            pltpu.VMEM(w_out.T.shape, BF16),
            pltpu.VMEM(place.shape, BF16),
            pltpu.VMEM((256, 256), F32),
            pltpu.SemaphoreType.DMA((6 + len(loaded),)),
        ],
        compiler_params=limit,
        cost_estimate=pl.CostEstimate(flops=10**9, bytes_accessed=8 * 10**6, transcendentals=0),
        name="prepare",
    )(counts, sigma, *in_hbm(noise_embed, w_stem, w_out.T, place, w_value, w_attn_out, *loaded))
    state, mean_field, basis, along, along_side = prepared[:5]
    first, second, levels, stem_right, out_right, w_joint = prepared[9:]
    weights = [*prepared[5:8], w_joint, prepared[8]]

    second, first, mix_own = pl.pallas_call(
        pack_kernel,
        out_shape=in_vmem(
            ((PIECE, 128), BF16), ((PIECE, 128), BF16), ((SLOTS * MEMBERS, 128), F32)
        ),
        in_specs=[smem] + [vmem] * 6,
        out_specs=[vmem] * 3,
        scratch_shapes=[pltpu.VMEM((MEMBERS, 8, 128), F32)],
        compiler_params=limit,
        name="pack",
    )(counts, *chips, first, second)
    pairs = [(i, i ^ 1) for i in range(owners)]
    others = []
    for i in range(1, owners - 1, 2):
        others += [(i, i + 1), (i + 1, i)]
    second = lax.ppermute(second, "space", others)
    first = lax.ppermute(first, "space", pairs)

    features, pooled, lifted, total = pl.pallas_call(
        own_kernel,
        out_shape=in_vmem(
            ((OWN_ROWS, W * CH), BF16),
            ((OWN_TOKENS, CH), F32),
            ((4 * TOKENS, CH), F32),
            ((OWN_ROWS, 128), F32),
        ),
        in_specs=[smem] + [vmem] * 13,
        out_specs=[vmem] * 4,
        scratch_shapes=[
            pltpu.VMEM((2, OWN_ROWS, 256), BF16),
            pltpu.VMEM((4, OWN_ROWS + 16, 128), F32),
            pltpu.VMEM((OWN_ROWS, STEM_LANES), BF16),
            pltpu.VMEM((OWN_TOKENS + 16, CH), F32),
            pltpu.VMEM((1, 2 * EARLY * DOM, HALF_LANES), BF16),
            pltpu.VMEM((1, 2 * EARLY * DOM, 256), F32),
            pltpu.VMEM((2, 80, 384), F32),
        ],
        compiler_params=limit,
        cost_estimate=pl.CostEstimate(flops=10**9, bytes_accessed=10**7, transcendentals=2 * 10**6),
        name="own",
    )(
        counts, state, mean_field, mix_own, along, levels, basis, stem_right, out_right, *weights
    )

    denoised, stepped = pl.pallas_call(
        main_kernel,
        out_shape=(
            jax.ShapeDtypeStruct((SLOTS, P_SIZE, 128), F32),
            jax.ShapeDtypeStruct((SLOTS, P_SIZE, 128), F32),
        ),
        in_specs=[smem] * 2 + [vmem] * 19,
        out_specs=(vmem, vmem),
        scratch_shapes=[
            pltpu.VMEM((2, 96, 128), F32),
            pltpu.VMEM((2, 96, 128), F32),
            pltpu.VMEM((64, 128), F32),
            pltpu.VMEM((2, 2 * SIDE_SPAN, 256), BF16),
            pltpu.VMEM((4, 2 * SIDE_SPAN + 16, 128), F32),
            pltpu.VMEM((2 * SIDE_ROWS, STEM_LANES), BF16),
            pltpu.VMEM((2 * SIDE_ROWS, W * CH), BF16),
            pltpu.VMEM((96, CH), F32),
            pltpu.VMEM((4 * TOKENS, CH), F32),
            pltpu.VMEM((2, 2 * 96, HALF_LANES), BF16),
            pltpu.VMEM((2, 2 * 96, 256), F32),
            pltpu.VMEM((4, 80, 384), F32),
            pltpu.VMEM((OWN_ROWS, 128), F32),
            pltpu.VMEM((1, 2 * LATE * DOM, HALF_LANES), BF16),
            pltpu.VMEM((1, 2 * LATE * DOM, 256), F32),
        ],
        compiler_params=limit,
        cost_estimate=pl.CostEstimate(flops=10**9, bytes_accessed=10**7, transcendentals=2 * 10**6),
        name="main",
    )(
        counts, sigma_next, state, mean_field, second, first, mix_own, levels, along_side, basis, stem_right,
        pooled, features, lifted, total, *weights, out_right,
    )
    return denoised[None], stepped[None]


def solution(mesh):
    placed = (
        P("member", "space", None, None),
        P("space", None, None),
        P("space", "member"),
        P("space"),
        P("space", None),
        P("space", None),
        P(),
        P("member"),
        P("member"),
        P(),
        P(),
        P(),
        P(),
        P(),
        P(),
        P(),
        P(),
        P(),
    )
    return jax.shard_map(
        shards,
        mesh=mesh,
        in_specs=placed,
        out_specs=(P("member", "space", None, None), P("member", "space", None, None)),
        check_vma=False,
    )
```

```python
import functools

import jax
import jax.numpy as jnp
import numpy as np
from jax import lax
from jax.experimental import pallas as pl
from jax.experimental.pallas import tpu as pltpu
from jax.sharding import PartitionSpec as P

VARS = 4
CCH = 12
CIN = 20
CH = 128
CH2 = 256
HEADS = 4
HEAD_DIM = 64
P_SIZE = 32
M = 16
W = 32
SLOTS = 6
FACTOR = 8
BLK_DEV = 8
MIX = 4
DOM = 64
TOKENS = 32
BR = 4
BW = 4
MEMBERS = 8
DISTANCES = (1, 3, 2)

SIGMA_DATA = 0.5
NORM_EPS = 1e-06

F32 = jnp.float32
BF16 = jnp.bfloat16

CELL = 64
STEM_LANES = (W + 2) * CELL
OWN_ROWS = SLOTS * P_SIZE
SIDE_ROWS = 64
OWN_TOKENS = OWN_ROWS // 8 * 4
SIDE_PATCHES = 4
PIECE = 160
LEFT_LANES = 1152
SIDE_SPAN = 80
HALF = W // 2
HALF_LANES = HALF * CH
TAP_LANES = (HALF + 2) * VARS
EARLY = 2
LATE = SLOTS - 2 - EARLY
VMEM_LIMIT = 24 * 1024 * 1024


def interp_matrix(fine_count, coarse_count):
    position = (np.arange(fine_count) + 0.5) / FACTOR - 0.5
    position = np.clip(position, 0.0, coarse_count - 1.0)
    return np.maximum(0.0, 1.0 - np.abs(position[:, None] - np.arange(coarse_count)[None, :]))


def along_rows(sources, patches):
    row_map = interp_matrix(P_SIZE, BR)
    along = np.zeros((len(sources), 2, patches, BR), np.float32)
    for row, source in enumerate(sources):
        along[row, :, source // P_SIZE] = row_map[source % P_SIZE][None]
    return along


@functools.cache
def tables():
    col_map = interp_matrix(W, BW)
    noisy, mean = (np.zeros((W, VARS, W + 2, CELL), np.float32) for _ in range(2))
    across = np.zeros((2, BW, CCH, W + 2, CELL), np.float32)
    for tap in range(3):
        at = tap * CIN
        for col in range(W):
            for var in range(VARS):
                noisy[col, var, col + 1, at + var] = 1.0
                mean[col, var, col + 1, at + VARS + var] = 1.0
        for channel in range(CCH):
            across[:, :, channel, 1 : W + 1, at + 2 * VARS + channel] = col_map.T[None]
    basis = np.zeros((2, 256, LEFT_LANES), np.float32)
    for half, lanes in enumerate((slice(0, LEFT_LANES), slice(LEFT_LANES, STEM_LANES))):
        count = lanes.stop - lanes.start
        cells = slice(HALF * half, HALF * half + HALF)
        basis[half, 0:64, :count] = noisy[cells].reshape(64, STEM_LANES)[:, lanes]
        basis[half, 64:128, :count] = mean[cells].reshape(64, STEM_LANES)[:, lanes]
        basis[half, 128:224, :count] = across.reshape(96, STEM_LANES)[:, lanes]
        basis[half, 232, :count] = np.tile(np.arange(CELL) >= 3 * CIN, W + 2)[lanes]
    basis[0, 224:228] = noisy[HALF].reshape(4, STEM_LANES)[:, :LEFT_LANES]
    basis[0, 228:232] = mean[HALF].reshape(4, STEM_LANES)[:, :LEFT_LANES]
    along = along_rows(range(OWN_ROWS), SLOTS).reshape(OWN_ROWS, 2 * SLOTS * BR)
    side = along_rows(range(8, 8 + SIDE_SPAN), SIDE_PATCHES)
    along_side = np.zeros((2, SIDE_SPAN, 2, 2, SIDE_PATCHES, BR), np.float32)
    for number in range(2):
        along_side[number, :, :, number] = side
    along_side = along_side.reshape(2 * SIDE_SPAN, 4 * SIDE_PATCHES * BR)
    place = np.zeros((3, 3, VARS, HALF, 256), np.float32)
    for cell in range(HALF):
        for row_tap in range(3):
            for col_tap in range(3):
                for var in range(VARS):
                    lane = row_tap * TAP_LANES + (cell + 2 - col_tap) * VARS + var
                    place[row_tap, col_tap, var, cell, lane] = 1.0
    place = place.reshape(36, HALF * 256)
    return tuple(array.astype(jnp.bfloat16) for array in (basis, along, along_side, place))


def silu(value):
    half = 0.5 * value
    return half + half * jnp.tanh(half)


def dot(left, right):
    return jnp.dot(left, right, preferred_element_type=F32)


def fetch(sems, pairs):
    copies = [pltpu.make_async_copy(a, b, sems.at[i]) for i, (a, b) in enumerate(pairs)]
    for copy in copies:
        copy.start()
    return copies


def mix_kernel(src, widx, table, coarse, mixed_out, src_s, widx_s, table_s, blocks, sems):
    for copy in fetch(sems, [(src, src_s), (widx, widx_s), (table, table_s), (coarse, blocks)]):
        copy.wait()
    mixed_out[...] = jnp.zeros_like(mixed_out)
    for slot in range(SLOTS):
        total = jnp.zeros((1, 24), F32)
        for k in range(MIX):
            total = total + table_s[widx_s[k, slot]] * blocks[pl.ds(src_s[k, slot], 1)]
        mixed_out[slot : slot + 1, 0:24] = total


def merge_kernel(mixed, partners, merged_out):
    core = lax.rem(lax.axis_index("member"), 2)
    merged_out[pl.ds(pl.multiple_of(8 * core, 8), 8)] = mixed[...]
    merged_out[pl.ds(pl.multiple_of(8 - 8 * core, 8), 8)] = partners[...]


def prepare_kernel(counts, sigma, noise_embed, w_stem, w_out, place, w_value, w_attn_out, *refs):
    loaded, kept, rest = refs[:9], refs[9:18], refs[18:]
    (
        first_out, second_out, levels_out, stem_out, right_out, joint_out,
        value_v, attn_v, embed_v, w_stem_v, w_out_v, place_v, stem_f32, sems,
    ) = rest
    noisy_v, mean_v = kept[:2]
    copies = fetch(
        sems,
        [
            (noise_embed, embed_v),
            (loaded[0], noisy_v),
            (loaded[1], mean_v),
            (w_stem, w_stem_v),
            (w_out, w_out_v),
            (place, place_v),
            (w_value, value_v),
            (w_attn_out, attn_v),
        ]
        + list(zip(loaded[2:], kept[2:])),
    )
    stem_f32[...] = jnp.zeros_like(stem_f32)
    for copy in copies[0:3]:
        copy.wait()
    held = counts[0]
    level = jnp.full((1, 128), sigma[0], F32)
    variance = level * level + SIGMA_DATA * SIGMA_DATA
    c_in = lax.rsqrt(variance)
    levels_out[0:1] = jnp.log(level) * 0.125 * embed_v[...].reshape(1, CH)
    levels_out[1:2] = SIGMA_DATA * SIGMA_DATA / variance
    levels_out[2:3] = level * SIGMA_DATA * lax.rsqrt(variance)
    levels_out[3:4] = 1.0 / level
    levels_out[4:5] = c_in
    even = lax.rem(lax.axis_index("space"), 2) == 0
    c_in = c_in.reshape(1, 1, 128)
    for out, to_right in ((first_out, even), (second_out, jnp.logical_not(even))):
        start = jnp.where(to_right, held - 2, 0)
        out[0:64] = (c_in * noisy_v[pl.ds(start, 2)]).astype(BF16).reshape(64, 128)
        out[64:128] = mean_v[pl.ds(start, 2)].astype(BF16).reshape(64, 128)

    copies[3].wait()
    stem_taps = w_stem_v[...].astype(F32) * 0.5
    for cell in range(4):
        for target in range(2):
            col_tap = cell - target
            if 0 <= col_tap < 3:
                for row_tap in range(3):
                    at = (3 * row_tap + col_tap) * CIN
                    to = cell * CELL + row_tap * CIN
                    stem_f32[to : to + CIN, target * CH : (target + 1) * CH] = stem_taps[at : at + CIN]
    part = levels_out[0:1]
    for number in range(3):
        high = part.astype(BF16).astype(F32)
        for target in range(2):
            to = (target + 1) * CELL + 3 * CIN + number
            stem_f32[to : to + 1, target * CH : (target + 1) * CH] = high
        part = part - high
    stem_out[...] = stem_f32[...].astype(BF16)
    for copy in copies[4:6]:
        copy.wait()
    weights = jnp.transpose(w_out_v[...].astype(F32)).astype(BF16)
    for cell in range(HALF):
        right_out[cell * CH : (cell + 1) * CH] = dot(
            weights, place_v[:, cell * 256 : (cell + 1) * 256]
        ).astype(BF16)
    for copy in copies[6:]:
        copy.wait()
    after = dot(attn_v[...], kept[8][...]).astype(BF16)
    for head in range(HEADS):
        span = slice(head * HEAD_DIM, (head + 1) * HEAD_DIM)
        joint_out[:, head * CH : (head + 1) * CH] = dot(value_v[:, span], after[span]).astype(BF16)


def pack_kernel(counts, chip0, chip1, chip2, chip3, first_in, second_in, second_out, first_out, mix_out, cells):
    held = counts[0]
    chip = lax.axis_index("member") // 2
    for distance, given in zip((0, *DISTANCES), (chip0, chip1, chip2, chip3)):
        member = 2 * jnp.bitwise_xor(chip, distance)
        cells[member] = given[0:8]
        cells[member + 1] = given[8:16]
    for member in range(MEMBERS):
        mix_out[pl.ds(member, 8, stride=MEMBERS)] = cells[member]
    even = lax.rem(lax.axis_index("space"), 2) == 0
    for out, given, to_right in (
        (first_out, first_in, even),
        (second_out, second_in, jnp.logical_not(even)),
    ):
        start = pl.multiple_of(jnp.where(to_right, held - 2, 0) * MEMBERS, MEMBERS)
        out[0:128] = given[0:128]
        mixed = mix_out[pl.ds(start, 16)]
        high = mixed.astype(BF16)
        out[128:144] = high
        out[144:160] = (mixed - high.astype(F32)).astype(BF16)


def interpolate(mixes, count, along):
    pair = mixes[pl.ds(0, count, stride=2)] + pltpu.roll(mixes[pl.ds(1, count, stride=2)], 24, 1)
    high = pair.astype(BF16).astype(F32)
    rows = dot(along[...], jnp.concatenate([high, pair - high], axis=0).astype(BF16))
    high = rows.astype(BF16).astype(F32)
    return high + pltpu.roll(rows - high, 48, 1)


def assemble(operand, state, mean, cond):
    lane = lax.broadcasted_iota(jnp.int32, state.shape, 1)
    left = lane < 64
    operand[0, :, 0:128] = jnp.where(left, state, pltpu.roll(mean, 64, 1)).astype(BF16)
    operand[1, :, 0:128] = jnp.where(left, pltpu.roll(state, 64, 1), mean).astype(BF16)
    one = lane == 104
    operand[1, :, 128:256] = jnp.where(one, 1.0, cond).astype(BF16)
    more = jnp.where(lane < 100, pltpu.roll(state, 32, 1), pltpu.roll(mean, 36, 1))
    operand[0, :, 128:256] = jnp.where(
        lane < 96, cond, jnp.where(lane < 104, more, one.astype(F32))
    ).astype(BF16)


def widen(operand, basis, blocks, wide, stem_in):
    rows = operand.shape[1]
    lane = lax.rem(lax.broadcasted_iota(jnp.int32, (1, 128), 1), CELL)
    above, here = lane < CIN, lane < 2 * CIN
    zero = jnp.zeros((8, 128), F32)
    for number in range(4):
        wide[number, 0:8] = zero
        wide[number, 8 + rows :] = zero
    turn = 0
    for half, (start, stop) in enumerate(((0, LEFT_LANES), (LEFT_LANES, STEM_LANES))):
        given = operand[half]
        for chunk in range(start, stop, 256):
            lanes = min(256, stop - chunk)
            at = chunk - start
            product = dot(given, basis[half, :, at : at + lanes])
            for part in range(0, lanes, 128):
                number = turn % 4
                turn += 1
                wide[number, 8 : 8 + rows] = product[:, part : part + 128]
                to_lane = chunk + part
                for first, to, count in blocks:
                    at_row = 8 + first
                    stem_in[to : to + count, to_lane : to_lane + 128] = jnp.where(
                        above,
                        wide[number, at_row - 1 : at_row - 1 + count],
                        jnp.where(
                            here,
                            wide[number, at_row : at_row + count],
                            wide[number, at_row + 1 : at_row + 1 + count],
                        ),
                    ).astype(BF16)


def stem(stem_in, stem_right, features, store_pooled):
    rows = features.shape[0]
    for block_col in range(4):
        summed = jnp.zeros((rows, CH), F32)
        for cell_pair in range(4):
            number = block_col * 4 + cell_pair
            halves = dot(stem_in[:, number * 128 : number * 128 + 256], stem_right[...])
            for part in range(2):
                half = halves[:, part * CH : (part + 1) * CH]
                feature = (0.5 * half) * (1.0 + jnp.tanh(half))
                lane = number * 256 + part * CH
                features[:, lane : lane + CH] = feature.astype(BF16)
                summed = summed + feature
        store_pooled(block_col, jnp.sum(summed.reshape(rows // 8, 8, CH), axis=1) * (1.0 / 32.0))


def bottleneck(pooled, starts, weights):
    *_, lifted = bottleneck_steps(pooled, starts, weights)
    return lifted


def bottleneck_steps(pooled, starts, weights):
    w_down, w_query, w_key, w_joint, w_up = weights
    zeta = silu(dot(pooled.astype(BF16), w_down[...]))
    scale = lax.rsqrt(jnp.mean(zeta * zeta, axis=-1, keepdims=True) + NORM_EPS)
    given = zeta.astype(BF16)
    yield None
    query = (scale * HEAD_DIM**-0.5 * dot(given, w_query[...])).astype(BF16)
    keyed = (scale * dot(given, w_key[...])).astype(BF16)
    valued = (scale * dot(given, w_joint[...])).astype(BF16)
    raised = dot(given, w_up[...])
    head_of_row = lax.broadcasted_iota(jnp.int32, (HEADS * TOKENS, CH2), 0) // TOKENS
    head_of_channel = lax.broadcasted_iota(jnp.int32, (HEADS * TOKENS, CH2), 1) // HEAD_DIM
    own_head = (head_of_row == head_of_channel).astype(F32).astype(BF16)
    row = lax.broadcasted_iota(jnp.int32, (HEADS * TOKENS, HEADS * TOKENS), 0) // TOKENS
    lane = lax.broadcasted_iota(jnp.int32, (HEADS * TOKENS, HEADS * TOKENS), 1) // TOKENS
    same_head = (row == lane).astype(F32).astype(BF16)
    head_of_lane = lax.broadcasted_iota(jnp.int32, (TOKENS, HEADS * TOKENS), 1) // TOKENS
    yield None
    scores = []
    for start in starts:
        rows = slice(start, start + TOKENS)
        keys = jnp.concatenate([keyed[rows]] * HEADS, axis=0) * own_head
        scores.append(
            lax.dot_general(
                query[rows], keys, (((1,), (1,)), ((), ())), preferred_element_type=F32
            )
        )
    yield None
    weighted = []
    for score in scores:
        top = jnp.zeros_like(score)
        for head in range(HEADS):
            inside = head_of_lane == head
            largest = jnp.max(jnp.where(inside, score, -jnp.inf), axis=1, keepdims=True)
            top = jnp.where(inside, largest, top)
        weighted.append(jnp.exp(score - top))
    yield None
    lifted = []
    for start, weight in zip(starts, weighted):
        rows = slice(start, start + TOKENS)
        values = jnp.concatenate(
            [valued[rows, head * CH : (head + 1) * CH] for head in range(HEADS)], axis=0
        )
        weight = (weight / dot(weight.astype(BF16), same_head)).astype(BF16)
        lifted.append(0.5 * (raised[rows] + dot(weight, values)))
    yield jnp.concatenate(lifted, axis=0)


def activate(number, sources, first, lifted, active, base, block_cols=range(4)):
    half_rows = active.shape[0] // 2
    count = sum(rows for _, _, rows in sources) // 8
    for block_col in block_cols:
        raised = lifted[pl.ds(number * TOKENS + first * 4 + block_col, count, stride=4)].reshape(
            count, 1, CH
        )
        done = 0
        for ref, start, rows in sources:
            part = raised[done // 8 : (done + rows) // 8]
            for cell in range(block_col * 8, block_col * 8 + 8):
                given = ref[pl.ds(start, rows), cell * CH : (cell + 1) * CH]
                half = given.astype(F32).reshape(rows // 8, 8, CH) + part
                value = half + half * jnp.tanh(half)
                to = base + done + cell // HALF * half_rows
                lane = cell % HALF * CH
                active[to : to + rows, lane : lane + CH] = value.reshape(rows, CH).astype(BF16)
            done += rows


def predict(left, right, first, last, padded):
    rows = (last - first) * 8
    lane = lax.broadcasted_iota(jnp.int32, (rows, 128), 1)
    for tap in range(3):
        from_left = pltpu.roll(left, (-4 - TAP_LANES * tap) % 256, 1)[:, 0:128]
        from_right = pltpu.roll(right, (60 - TAP_LANES * tap) % 256, 1)[:, 0:128]
        padded[8 : 8 + rows, tap * 128 : (tap + 1) * 128] = jnp.where(
            lane < 68, from_left, 0.0
        ) + jnp.where(lane >= 60, from_right, 0.0)
    zero = jnp.zeros((8, 384), F32)
    padded[0:8] = zero
    padded[8 + rows : 16 + rows] = zero
    field = (
        padded[7 : 7 + rows, 0:128] + padded[8 : 8 + rows, 128:256] + padded[9 : 9 + rows, 256:384]
    )
    row = lax.broadcasted_iota(jnp.int32, (rows, 128), 0) + first * 8
    return field * jnp.minimum(row + 1, DOM - row).astype(F32)


def convolve(plans, group_rows, lifted, active, halves, padded, out_right, total, ready=False):
    groups = active.shape[0]
    each = len(plans) // groups
    for group in range(groups):
        base = 0
        for number in range(each * group, each * group + each):
            first, stop, sources = plans[number][:3]
            if not ready:
                activate(number, sources, first, lifted, active.at[group], base)
            base += (stop - first) * 8
        halves[group] = dot(active[group], out_right[...])
    for group in range(groups):
        base = 0
        for number in range(each * group, each * group + each):
            first, stop, _, to, start, end, counted = plans[number]
            rows = (stop - first) * 8
            field = predict(
                halves[group, base : base + rows],
                halves[group, group_rows + base : group_rows + base + rows],
                first,
                stop,
                padded.at[number % 2],
            )[start:end]
            if counted is not True:
                field = jnp.where(counted, field, 0.0)
            span = pl.ds(to, end - start)
            total[span] = total[span] + field
            base += rows


def inner_plans(numbers, held):
    plans = []
    for patch in (number + 1 for number in numbers):
        start = P_SIZE * patch - M
        plans.append((0, 8, start, start, 0, 64, patch <= held - 2))
    return plans


def own_kernel(
    counts, noisy, mean_field, mixes, along, levels, basis, stem_right, out_right, *refs
):
    weights = refs[:5]
    features, pooled_out, lifted, total = refs[5:9]
    operand, wide, stem_in, pooled, active, halves, padded = refs[9:]
    held = counts[0]
    assemble(
        operand,
        levels[4:5] * noisy[...].reshape(OWN_ROWS, 128),
        mean_field[...].reshape(OWN_ROWS, 128),
        interpolate(mixes, SLOTS * BR, along),
    )
    widen(operand, basis, [(0, 0, OWN_ROWS)], wide, stem_in)

    pooled[0:8] = jnp.zeros((8, CH), F32)
    pooled[8 + OWN_TOKENS :] = jnp.zeros((8, CH), F32)

    def store_pooled(block_col, value):
        pooled[pl.ds(8 + block_col, OWN_ROWS // 8, stride=4)] = value

    stem(stem_in, stem_right, features, store_pooled)
    pooled_out[...] = pooled[8 : 8 + OWN_TOKENS]
    lifted[...] = bottleneck(pooled[...], [16 * patch for patch in range(1, SLOTS - 1)], weights)
    total[...] = jnp.zeros_like(total)
    plans = [
        (first, stop, [(features, start, DOM)], *rest)
        for first, stop, start, *rest in inner_plans(range(EARLY), held)
    ]
    convolve(plans, EARLY * DOM, lifted, active, halves, padded, out_right, total)


def main_kernel(
    counts, sigma_next, noisy, mean_field, second_in, first_in, mix_own, levels, along, basis, stem_right,
    pooled_own, features, lifted_own, total_own, w_down, w_query, w_key, w_joint, w_up, out_right,
    denoised_out, next_out,
    state_rows, mean_rows, mixes, operand, wide, stem_in, ends, pooled, lifted, active, halves,
    padded, total, active_inner, halves_inner,
):
    held = counts[0]
    weights = (w_down, w_query, w_key, w_joint, w_up)
    position = lax.axis_index("space")
    even = lax.rem(position, 2) == 0
    has_left = position > 0
    has_right = position < lax.axis_size("space") - 1
    c_in = levels[4:5].reshape(1, 1, 128)

    state_rows[0, 64:96] = (c_in * noisy[0:1]).reshape(P_SIZE, 128)
    mean_rows[0, 64:96] = mean_field[0]
    state_rows[1, 0:32] = (c_in * noisy[pl.ds(held - 1, 1)]).reshape(P_SIZE, 128)
    mean_rows[1, 0:32] = mean_field[pl.ds(held - 1, 1)].reshape(P_SIZE, 128)
    mixes[16:24] = mix_own[0:8]
    mixes[24:32] = jnp.zeros((8, 128), F32)
    mixes[32:40] = mix_own[pl.ds(pl.multiple_of(8 * held - 8, 8), 8)]
    mixes[56:64] = jnp.zeros((8, 128), F32)

    def take(piece, side, rows_at, mixes_at):
        state_rows[side, rows_at : rows_at + 64] = piece[0:64].astype(F32)
        mean_rows[side, rows_at : rows_at + 64] = piece[64:128].astype(F32)
        mixes[mixes_at : mixes_at + 16] = piece[128:144].astype(F32) + piece[144:160].astype(F32)

    @pl.when(even)
    def _():
        take(second_in, 0, 0, 0)
        take(first_in, 1, 32, 40)

    @pl.when(jnp.logical_not(even))
    def _():
        take(first_in, 0, 0, 0)
        take(second_in, 1, 32, 40)

    assemble(
        operand,
        state_rows[:, 8 : 8 + SIDE_SPAN].reshape(2 * SIDE_SPAN, 128),
        mean_rows[:, 8 : 8 + SIDE_SPAN].reshape(2 * SIDE_SPAN, 128),
        interpolate(mixes, 2 * SIDE_PATCHES * BR, along),
    )
    widen(
        operand, basis, [(8, 0, SIDE_ROWS), (SIDE_SPAN + 8, SIDE_ROWS, SIDE_ROWS)], wide, stem_in
    )

    def store_pooled(block_col, value):
        pooled[pl.ds(block_col, 8, stride=4)] = value[0:8]
        pooled[pl.ds(64 + block_col, 8, stride=4)] = value[8:16]

    stem(stem_in, stem_right, ends, store_pooled)
    pooled[32:48] = pooled_own[8:24]
    pooled[48:64] = pooled_own[pl.ds(pl.multiple_of(16 * held - 24, 8), 16)]

    @pl.when(jnp.logical_not(has_left))
    def _():
        ends[0:48] = jnp.zeros((48, W * CH), BF16)
        pooled[0:24] = jnp.zeros((24, CH), F32)

    @pl.when(jnp.logical_not(has_right))
    def _():
        ends[80:128] = jnp.zeros((48, W * CH), BF16)
        pooled[72:96] = jnp.zeros((24, CH), F32)

    plans = [
        (first, stop, [(features, start, DOM)], *rest)
        for first, stop, start, *rest in inner_plans(range(EARLY, SLOTS - 2), held)
    ]
    late = lifted_own.at[EARLY * TOKENS :]
    parts = [(number, block_col) for number in range(LATE) for block_col in range(4)]
    for done in bottleneck_steps(pooled[...], [0, 16, 48, 64], weights):
        for number, block_col in parts[:2]:
            activate(
                number, plans[number][2], 0, late, active_inner.at[0], number * DOM, [block_col]
            )
        parts = parts[2:]
    lifted[...] = done
    total[...] = total_own[...]
    convolve(
        plans, LATE * DOM, late, active_inner, halves_inner, padded.at[0:2], out_right, total, True
    )
    near = pl.multiple_of(P_SIZE * held - 48, 16)
    last = pl.multiple_of(P_SIZE * held - M, 16)
    plans = [
        (4, 8, [(ends, 32, 32)], 0, 16, 32, has_left),
        (0, 8, [(ends, 32, 32), (features, 16, 32)], 0, 16, 64, True),
        (0, 8, [(features, near, 32), (ends, 64, 32)], near, 0, 48, True),
        (0, 4, [(ends, 64, 32)], last, 0, 16, has_right),
    ]
    convolve(plans, 96, lifted, active, halves, padded.at[2:4], out_right, total)

    slot = lax.broadcasted_iota(jnp.int32, (SLOTS, P_SIZE, 128), 0)
    row = lax.broadcasted_iota(jnp.int32, (SLOTS, P_SIZE, 128), 1)
    norm = jnp.full((SLOTS, P_SIZE, 128), 33, jnp.int32)
    no_left = jnp.logical_and(jnp.logical_not(has_left), jnp.logical_and(slot == 0, row < M))
    no_right = jnp.logical_and(
        jnp.logical_not(has_right), jnp.logical_and(slot == held - 1, row >= M)
    )
    norm = jnp.where(no_left, 17 + row, norm)
    norm = jnp.where(no_right, 48 - row, norm)
    blended = total[...].reshape(SLOTS, P_SIZE, 128) / norm.astype(F32)
    state = noisy[...]
    denoised = levels[1:2].reshape(1, 1, 128) * state + levels[2:3].reshape(1, 1, 128) * blended
    step = sigma_next[0] * levels[3:4].reshape(1, 1, 128) - 1.0
    stepped = state + step * (state - denoised)
    live = slot < held
    denoised_out[...] = jnp.where(live, denoised, 0.0)
    next_out[...] = jnp.where(live, stepped, 0.0)


def shards(
    noisy,
    mean_field,
    coarse,
    counts,
    src,
    widx,
    table,
    sigma,
    sigma_next,
    w_stem,
    noise_embed,
    w_down,
    w_query,
    w_key,
    w_value,
    w_attn_out,
    w_up,
    w_out,
):
    owners = lax.axis_size("space")
    smem = pl.BlockSpec(memory_space=pltpu.SMEM)
    vmem = pl.BlockSpec(memory_space=pltpu.VMEM)
    hbm = pl.BlockSpec(memory_space=pltpu.HBM)
    limit = pltpu.CompilerParams(vmem_limit_bytes=VMEM_LIMIT)

    def in_hbm(*arrays):
        return [pltpu.with_memory_space_constraint(array, pltpu.HBM) for array in arrays]

    def in_vmem(*shapes):
        return [pltpu.VMEM(shape, dtype) for shape, dtype in shapes]

    state = noisy[0]
    mixed = pl.pallas_call(
        mix_kernel,
        out_shape=pltpu.VMEM((8, 128), F32),
        in_specs=[hbm] * 4,
        out_specs=vmem,
        scratch_shapes=[
            pltpu.SMEM((MIX, SLOTS), jnp.int32),
            pltpu.SMEM((MIX, SLOTS), jnp.int32),
            pltpu.SMEM((16,), F32),
            pltpu.VMEM((BLK_DEV, 24), F32),
            pltpu.SemaphoreType.DMA((4,)),
        ],
        compiler_params=limit,
        name="mix",
    )(*in_hbm(src.T, widx.T, table, coarse))
    partners = lax.ppermute(mixed, "member", [(i, i ^ 1) for i in range(MEMBERS)])
    merged = pl.pallas_call(
        merge_kernel,
        out_shape=pltpu.VMEM((16, 128), F32),
        in_specs=[vmem] * 2,
        out_specs=vmem,
        compiler_params=limit,
        name="merge",
    )(mixed, partners)
    chips = [merged] + [
        lax.ppermute(merged, "member", [(i, i ^ (2 * distance)) for i in range(MEMBERS)])
        for distance in DISTANCES
    ]

    basis, along, along_side, place = (jnp.asarray(array) for array in tables())
    loaded = [state, mean_field, basis, along, along_side]
    loaded += [w_down, w_query, w_key, w_up]
    prepared = pl.pallas_call(
        prepare_kernel,
        out_shape=in_vmem(*((array.shape, array.dtype) for array in loaded))
        + in_vmem(
            ((PIECE, 128), BF16),
            ((PIECE, 128), BF16),
            ((8, 128), F32),
            ((CH2, CH2), BF16),
            ((HALF_LANES, 256), BF16),
            ((CH2, HEADS * CH), BF16),
        ),
        in_specs=[smem] * 2 + [hbm] * (6 + len(loaded)),
        out_specs=[vmem] * (len(loaded) + 6),
        scratch_shapes=[
            pltpu.VMEM(w_value.shape, BF16),
            pltpu.VMEM(w_attn_out.shape, BF16),
            pltpu.VMEM(noise_embed.shape, F32),
            pltpu.VMEM(w_stem.shape, BF16),
            pltpu.VMEM(w_out.T.shape, BF16),
            pltpu.VMEM(place.shape, BF16),
            pltpu.VMEM((256, 256), F32),
            pltpu.SemaphoreType.DMA((6 + len(loaded),)),
        ],
        compiler_params=limit,
        cost_estimate=pl.CostEstimate(flops=10**9, bytes_accessed=8 * 10**6, transcendentals=0),
        name="prepare",
    )(counts, sigma, *in_hbm(noise_embed, w_stem, w_out.T, place, w_value, w_attn_out, *loaded))
    state, mean_field, basis, along, along_side = prepared[:5]
    first, second, levels, stem_right, out_right, w_joint = prepared[9:]
    weights = [*prepared[5:8], w_joint, prepared[8]]

    second, first, mix_own = pl.pallas_call(
        pack_kernel,
        out_shape=in_vmem(
            ((PIECE, 128), BF16), ((PIECE, 128), BF16), ((8 * MEMBERS, 128), F32)
        ),
        in_specs=[smem] + [vmem] * 6,
        out_specs=[vmem] * 3,
        scratch_shapes=[pltpu.VMEM((MEMBERS, 8, 128), F32)],
        compiler_params=limit,
        name="pack",
    )(counts, *chips, first, second)
    pairs = [(i, i ^ 1) for i in range(owners)]
    others = []
    for i in range(1, owners - 1, 2):
        others += [(i, i + 1), (i + 1, i)]
    second = lax.ppermute(second, "space", others)
    first = lax.ppermute(first, "space", pairs)

    features, pooled, lifted, total = pl.pallas_call(
        own_kernel,
        out_shape=in_vmem(
            ((OWN_ROWS, W * CH), BF16),
            ((OWN_TOKENS, CH), F32),
            ((4 * TOKENS, CH), F32),
            ((OWN_ROWS, 128), F32),
        ),
        in_specs=[smem] + [vmem] * 13,
        out_specs=[vmem] * 4,
        scratch_shapes=[
            pltpu.VMEM((2, OWN_ROWS, 256), BF16),
            pltpu.VMEM((4, OWN_ROWS + 16, 128), F32),
            pltpu.VMEM((OWN_ROWS, STEM_LANES), BF16),
            pltpu.VMEM((OWN_TOKENS + 16, CH), F32),
            pltpu.VMEM((1, 2 * EARLY * DOM, HALF_LANES), BF16),
            pltpu.VMEM((1, 2 * EARLY * DOM, 256), F32),
            pltpu.VMEM((2, 80, 384), F32),
        ],
        compiler_params=limit,
        cost_estimate=pl.CostEstimate(flops=10**9, bytes_accessed=10**7, transcendentals=2 * 10**6),
        name="own",
    )(
        counts, state, mean_field, mix_own, along, levels, basis, stem_right, out_right, *weights
    )

    denoised, stepped = pl.pallas_call(
        main_kernel,
        out_shape=(
            jax.ShapeDtypeStruct((SLOTS, P_SIZE, 128), F32),
            jax.ShapeDtypeStruct((SLOTS, P_SIZE, 128), F32),
        ),
        in_specs=[smem] * 2 + [vmem] * 19,
        out_specs=(vmem, vmem),
        scratch_shapes=[
            pltpu.VMEM((2, 96, 128), F32),
            pltpu.VMEM((2, 96, 128), F32),
            pltpu.VMEM((64, 128), F32),
            pltpu.VMEM((2, 2 * SIDE_SPAN, 256), BF16),
            pltpu.VMEM((4, 2 * SIDE_SPAN + 16, 128), F32),
            pltpu.VMEM((2 * SIDE_ROWS, STEM_LANES), BF16),
            pltpu.VMEM((2 * SIDE_ROWS, W * CH), BF16),
            pltpu.VMEM((96, CH), F32),
            pltpu.VMEM((4 * TOKENS, CH), F32),
            pltpu.VMEM((2, 2 * 96, HALF_LANES), BF16),
            pltpu.VMEM((2, 2 * 96, 256), F32),
            pltpu.VMEM((4, 80, 384), F32),
            pltpu.VMEM((OWN_ROWS, 128), F32),
            pltpu.VMEM((1, 2 * LATE * DOM, HALF_LANES), BF16),
            pltpu.VMEM((1, 2 * LATE * DOM, 256), F32),
        ],
        compiler_params=limit,
        cost_estimate=pl.CostEstimate(flops=10**9, bytes_accessed=10**7, transcendentals=2 * 10**6),
        name="main",
    )(
        counts, sigma_next, state, mean_field, second, first, mix_own, levels, along_side, basis, stem_right,
        pooled, features, lifted, total, *weights, out_right,
    )
    return denoised[None], stepped[None]


def solution(mesh):
    placed = (
        P("member", "space", None, None),
        P("space", None, None),
        P("space", "member"),
        P("space"),
        P("space", None),
        P("space", None),
        P(),
        P("member"),
        P("member"),
        P(),
        P(),
        P(),
        P(),
        P(),
        P(),
        P(),
        P(),
        P(),
    )
    return jax.shard_map(
        shards,
        mesh=mesh,
        in_specs=placed,
        out_specs=(P("member", "space", None, None), P("member", "space", None, None)),
        check_vma=False,
    )
```
